32 devices in a mesh: lon: 16 (over z, x, core), lat: 2 (over y).
Axes of the slice: x: 2, y: 2, z: 4, core: 2. Of those that a mesh axis runs over, the one named last changes fastest.
Arguments:
- heat_anomaly: float32 [16, 64, 2048], P(None, 'lat', 'lon'), may hold values from -11 to 11
- saltiness_anomaly: float32 [16, 64, 2048], P(None, 'lat', 'lon'), may hold values from -3 to 3
- zonal_stability_ratio: float32 [16, 64, 2048], P(None, 'lat', 'lon'), may hold values from -0.4 to 0.4
- meridional_stability_ratio: float32 [16, 64, 2048], P(None, 'lat', 'lon'), may hold values from -0.4 to 0.4
- ocean_layer_count: int32 [64, 2048], P('lat', 'lon'), may hold values from 0 to 16
Outputs:
- temperature_next: float32 [16, 64, 2048], P(None, 'lat', 'lon')
- salinity_next: float32 [16, 64, 2048], P(None, 'lat', 'lon')
The draws below stay inside these ranges and needn't reach their ends.
All inputs are finite; a program needn't handle non-finite values.
Results may differ from the reference program's by a relative error of at most 0.0003.
Values sent between devices are 32-bit elements; how exact they have to be, the bound alone decides.
No kernel may reach another device: no remote copies, remote signals or barrier semaphores. Data moves between devices by JAX's collectives and lax.ppermute only.
A program may use at most 64 MiB of HBM per device.

```python
import jax
import jax.numpy as jnp
from jax import lax

K = 16
NJ = 64
NI = 2048
N_LAT = 2


def draw_heat_anomaly(key, part):
    level = (jnp.arange(K, dtype=jnp.float32) + 0.5) / K
    profile = (8.0 * (1.0 - 2.0 * level))[:, None, None]
    noise = 0.7 * jnp.clip(jax.random.normal(key, (K, NJ, NI), jnp.float32), -4.0, 4.0)
    return profile + noise


def draw_saltiness_anomaly(key, part):
    level = (jnp.arange(K, dtype=jnp.float32) + 0.5) / K
    profile = (1.6 * (2.0 * level - 1.0))[:, None, None]
    noise = 0.25 * jnp.clip(jax.random.normal(key, (K, NJ, NI), jnp.float32), -4.0, 4.0)
    return profile + noise


def set_ends(entries, own_key, least, largest):
    extent = entries.shape
    spot = [jax.random.randint(jax.random.fold_in(own_key, axis), (), 0, extent[axis]) for axis in range(len(extent))]
    entries = entries.at[tuple(spot)].set(least)
    longest = extent.index(max(extent))
    spot[longest] = (spot[longest] + 1) % extent[longest]
    return entries.at[tuple(spot)].set(largest)


def steps_of(key, extent, shards, least, top_value):
    level, own = 1.0, jax.random.fold_in(key, 6)
    for position, shards_of in shards:
        heights = jnp.exp(jax.random.uniform(jax.random.fold_in(own, position), (shards_of,), jnp.float32, least / len(shards), top_value / len(shards)))
        level = level * jnp.repeat(heights, extent[position] // shards_of).reshape([-1 if axis == position else 1 for axis in range(len(extent))])
    return level


def setup_inputs(seed: int = 0) -> dict:
    arg_keys = jax.random.split(jax.random.key(seed), 6)
    return {
        "heat_anomaly": draw_heat_anomaly(jax.random.fold_in(arg_keys[5], 71), 0),
        "saltiness_anomaly": draw_saltiness_anomaly(jax.random.fold_in(arg_keys[5], 71), 0),
        "zonal_stability_ratio": jnp.clip(jax.random.uniform(arg_keys[2], (K, NJ, NI), jnp.float32, -0.4, 0.4) * steps_of(arg_keys[2], (K, NJ, NI), ((1, 2), (2, 16)), -0.4, 0.0), -0.4, 0.4),
        "meridional_stability_ratio": jnp.clip(jax.random.uniform(arg_keys[3], (K, NJ, NI), jnp.float32, -0.4, 0.4) * steps_of(arg_keys[3], (K, NJ, NI), ((1, 2), (2, 16)), -0.4, 0.0), -0.4, 0.4),
        "ocean_layer_count": set_ends(jax.random.randint(arg_keys[4], (NJ, NI), 0, K + 1), jax.random.fold_in(arg_keys[4], 1), 0, K).astype(jnp.int32),
    }


heat_swelling_alpha = 0.1655
coef_beta = 0.76554
cabbeling_parameter = 0.05952
lambda_salt = 0.00054914
thermobaric_parameter = 0.0001497
press_salt = 0.00001109
cross_coupling_contribution = 0.0024341
total_depth = 5000.0
kappa_iso = 0.1
slope_max = 1.0
strat_min = 0.1


def minmod(former, second):
    return jnp.where(former * second > 0.0, jnp.sign(former) * jnp.minimum(jnp.abs(former), jnp.abs(second)), 0.0)


def seawater_heaviness(heat_anomaly, saltiness_anomaly, seafloor_distances):
    return (-heat_swelling_alpha * (1.0 + 0.5 * cabbeling_parameter * heat_anomaly + thermobaric_parameter * seafloor_distances) * heat_anomaly
            + coef_beta * (1.0 - 0.5 * lambda_salt * saltiness_anomaly - press_salt * seafloor_distances) * saltiness_anomaly
            - cross_coupling_contribution * heat_anomaly * saltiness_anomaly)


def vertical_diff(field):
    along = field.ndim - 3
    layer_stack_sum = field.shape[along]
    top_part = lax.slice_in_dim(field, 1, 2, axis=along) - lax.slice_in_dim(field, 0, 1, axis=along)
    middle = 0.5 * (lax.slice_in_dim(field, 2, layer_stack_sum, axis=along) - lax.slice_in_dim(field, 0, layer_stack_sum - 2, axis=along))
    bottom = lax.slice_in_dim(field, layer_stack_sum - 1, layer_stack_sum, axis=along) - lax.slice_in_dim(field, layer_stack_sum - 2, layer_stack_sum - 1, axis=along)
    return jnp.concatenate([top_part, middle, bottom], axis=along)


def face_flux(tracers, tracer_vert, rho_field, rho_vert, ocean_presence_flags, face_speed, along):
    def window(array, lower, upper):
        axis_pos = array.ndim + along
        return lax.slice_in_dim(array, lower, array.shape[axis_pos] - upper, axis=axis_pos)

    wet_face = window(ocean_presence_flags, 0, 1) * window(ocean_presence_flags, 1, 0)
    masked_step = wet_face * (window(tracers, 1, 0) - window(tracers, 0, 1))
    step_back = window(masked_step, 0, 2)
    step_here = window(masked_step, 1, 1)
    step_ahead = window(masked_step, 2, 0)
    cell_left = window(tracers, 1, 2)
    cell_right = window(tracers, 2, 1)
    face_wet = window(wet_face, 1, 1)
    positive = jnp.maximum(face_speed, 0.0)
    negative = jnp.minimum(face_speed, 0.0)
    advective = face_wet * (positive * (cell_left + 0.5 * (1.0 - face_speed) * minmod(step_back, step_here))
                            + negative * (cell_right - 0.5 * (1.0 + face_speed) * minmod(step_ahead, step_here)))
    rho_step = window(rho_field, 2, 1) - window(rho_field, 1, 2)
    strat_face = jnp.maximum(0.5 * (window(rho_vert, 1, 2) + window(rho_vert, 2, 1)), strat_min)
    slope_face = jnp.clip(-rho_step / strat_face, -slope_max, slope_max)
    vert_face = 0.5 * (window(tracer_vert, 1, 2) + window(tracer_vert, 2, 1))
    isoneutral = -kappa_iso * face_wet * (cell_right - cell_left + slope_face * vert_face)
    flux_total = advective + isoneutral
    return window(flux_total, 0, 1) - window(flux_total, 1, 0)


def stencil(padded, east_cols, north_rows):
    layer_stack_sum = padded.shape[1]
    depth_levels = total_depth * (lax.broadcasted_iota(jnp.float32, (layer_stack_sum, 1, 1), 0) + 0.5) / layer_stack_sum
    tracers = padded[:2]
    ocean_presence_flags = padded[2]
    rho_field = seawater_heaviness(padded[0], padded[1], depth_levels)
    rho_vert = vertical_diff(rho_field)
    tracer_vert = vertical_diff(tracers)
    along_x = face_flux(tracers[:, :, 2:-2, :], tracer_vert[:, :, 2:-2, :], rho_field[:, 2:-2, :],
                        rho_vert[:, 2:-2, :], ocean_presence_flags[:, 2:-2, :], east_cols, -1)
    along_y = face_flux(tracers[:, :, :, 2:-2], tracer_vert[:, :, :, 2:-2], rho_field[:, :, 2:-2],
                        rho_vert[:, :, 2:-2], ocean_presence_flags[:, :, 2:-2], north_rows, -2)
    interior = tracers[:, :, 2:-2, 2:-2]
    return ocean_presence_flags[:, 2:-2, 2:-2] * (interior + along_x + along_y)


def reference(heat_anomaly, saltiness_anomaly, zonal_stability_ratio, meridional_stability_ratio, ocean_layer_count):
    layer_stack_sum, latitude_band_sum, profile_sum = heat_anomaly.shape
    ocean_presence_flags = (lax.broadcasted_iota(jnp.int32, (layer_stack_sum, 1, 1), 0) < ocean_layer_count[None]).astype(jnp.float32)
    scalar_quantities = jnp.stack([heat_anomaly, saltiness_anomaly, ocean_presence_flags])
    lon_padded = jnp.concatenate([scalar_quantities[..., -2:], scalar_quantities, scalar_quantities[..., :2]], axis=-1)
    flipped = jnp.flip(scalar_quantities[:, :, latitude_band_sum - 3:, :], -1)
    ghost_rows = jnp.flip(jnp.roll(flipped, 1, -1)[:, :, 0:2, :], 2)
    ghost_wide = jnp.concatenate([ghost_rows[..., -2:], ghost_rows, ghost_rows[..., :2]], axis=-1)
    south_rows = jnp.zeros((3, layer_stack_sum, 2, profile_sum + 4), jnp.float32)
    padded = jnp.concatenate([south_rows, lon_padded, ghost_wide], axis=2)
    east_all = jnp.concatenate([zonal_stability_ratio[..., -1:], zonal_stability_ratio], axis=-1)
    north_all = jnp.concatenate([jnp.zeros((layer_stack_sum, 1, profile_sum), jnp.float32), meridional_stability_ratio], axis=1)
    block_size = latitude_band_sum // N_LAT

    def one_block(block_index):
        offset = (block_index * block_size).astype(jnp.int32)
        row_block = lax.dynamic_slice_in_dim(padded, offset, block_size + 4, 2)
        east_piece = lax.dynamic_slice_in_dim(east_all, offset, block_size, 1)
        north_piece = lax.dynamic_slice_in_dim(north_all, offset, block_size + 1, 1)
        return stencil(row_block, east_piece, north_piece)

    result = lax.map(one_block, jnp.arange(N_LAT, dtype=jnp.int32))
    result = jnp.moveaxis(result, 0, 2).reshape(2, layer_stack_sum, latitude_band_sum, profile_sum)
    return result[0], result[1]
```

```python
import functools

import jax
import jax.numpy as jnp
from jax import lax
from jax.experimental import pallas as pl
from jax.experimental.pallas import tpu as pltpu
from jax.sharding import PartitionSpec as P

heat_swelling_alpha = 0.1655
coef_beta = 0.76554
cabbeling_parameter = 0.05952
lambda_salt = 0.00054914
thermobaric_parameter = 0.0001497
press_salt = 1.109e-05
cross_coupling_contribution = 0.0024341
total_depth = 5000.0
kappa_iso = 0.1
strat_min = 0.1

LANES = 128
F32 = jnp.float32


def iota(shape, axis):
    return lax.broadcasted_iota(jnp.int32, shape, axis)


def roll(array, shift, axis=1):
    size = array.shape[axis]
    return pltpu.roll(array, shift % size, axis)


def minmod(x, y):
    return jnp.maximum(jnp.minimum(x, jnp.maximum(y, 0.0)), jnp.minimum(y, 0.0))


def level_factors(levels):
    depth = total_depth * (iota((levels, LANES), 0).astype(F32) + 0.5) / levels
    heat = -heat_swelling_alpha * (1.0 + thermobaric_parameter * depth)
    salt = coef_beta * (1.0 - press_salt * depth)
    return heat, salt


def density(t, s, factors):
    heat, salt = factors
    return t * (
        heat
        - (0.5 * heat_swelling_alpha * cabbeling_parameter) * t
        - cross_coupling_contribution * s
    ) + s * (salt - (0.5 * coef_beta * lambda_salt) * s)


def vertical(q, level):
    levels = q.shape[0]
    step = roll(q, -1, 0) - q
    below = roll(step, 1, 0)
    return jnp.where(level == levels - 1, below, step) + jnp.where(level == 0, step, below)


def column_row(t, s, n, factors, level):
    r = density(t, s, factors)
    return {
        "t": t,
        "s": s,
        "r": r,
        "tz": vertical(t, level),
        "sz": vertical(s, level),
        "rz": vertical(r, level),
        "n": n,
    }


def shifted(row, by):
    return {name: roll(value, by) for name, value in row.items()}


def weights(c, wet):
    size = jnp.abs(c)
    return jnp.where(wet, c, 0.0), jnp.where(wet, 0.5 * (size - c * c), 0.0)


def face_step(a, b, wet, name):
    return jnp.where(wet, b[name] - a[name], 0.0)


def face_base(a, b, c, wet, steps):
    wc, wg = weights(c, wet)
    steep = (a["r"] - b["r"]) / jnp.maximum(a["rz"] + b["rz"], 4.0 * strat_min)
    tilt = jnp.where(wet, jnp.clip(steep, -0.25, 0.25), 0.0) * (-kappa_iso)
    forward = c > 0.0
    base = [
        wc * jnp.where(forward, a[q], b[q]) - kappa_iso * d + tilt * (a[q + "z"] + b[q + "z"])
        for q, d in zip("ts", steps)
    ]
    return base, wg, forward


def strided(ref, row, levels, rows):
    return ref[pl.ds(row, levels, stride=rows), :]


def pack_kernel(levels, rows, t_ref, s_ref, c_ref, m_ref, n_ref, side_ref, north_ref, south_ref, fold_ref, own_ref):
    lane = iota((levels, LANES), 1)
    group = lane // 4

    def gather(ref):
        out = jnp.zeros((levels, LANES), F32)
        for j in range(rows):
            out = jnp.where(group == j, roll(strided(ref, j, levels, rows), 4 * j + 2), out)
        return out

    side_ref[0:levels, :] = gather(t_ref)
    side_ref[levels : 2 * levels, :] = gather(s_ref)
    side_ref[2 * levels : 3 * levels, :] = gather(c_ref)
    counts = n_ref[...].astype(F32)
    row = iota((rows, LANES), 0)
    lanes = iota((rows, LANES), 1)
    moved = jnp.concatenate(
        [roll(counts[j : j + 1], 4 * j + 2) for j in range(rows)], axis=0
    )
    line = jnp.sum(jnp.where(lanes // 4 == row, moved, 0.0), axis=0, keepdims=True)
    side_ref[3 * levels :, :] = jnp.broadcast_to(line, (8, LANES))

    def lines(out_ref, picks, tracers):
        at = 0
        for ref in tracers:
            for j in picks:
                out_ref[at : at + levels, :] = strided(ref, j, levels, rows)
                at += levels
        return at

    def tally(picks):
        return jnp.concatenate(
            [counts[j : j + 1] for j in picks] + [jnp.zeros((8 - len(picks), LANES), F32)], axis=0
        )

    at = lines(north_ref, (rows - 2, rows - 1), (t_ref, s_ref))
    north_ref[at : at + levels, :] = strided(m_ref, rows - 1, levels, rows)
    north_ref[at + levels :, :] = tally((rows - 2, rows - 1))
    at = lines(south_ref, (0, 1), (t_ref, s_ref))
    south_ref[at:, :] = tally((0, 1))
    own_ref[0:levels, :] = strided(m_ref, 0, levels, rows)
    own_ref[levels:, :] = strided(m_ref, rows - 2, levels, rows)

    def mirrored(x):
        index = (LANES - iota(x.shape, 1)) % LANES
        return jnp.take_along_axis(x, index, axis=1)

    at = 0
    for ref in (t_ref, s_ref):
        for j in (rows - 2, rows - 3):
            fold_ref[at : at + levels, :] = mirrored(strided(ref, j, levels, rows))
            at += levels
    fold_ref[at:, :] = mirrored(tally((rows - 2, rows - 3)))


NAMES = ("t", "s", "r", "tz", "sz", "rz")


def interior_kernel(levels, rows, t_ref, s_ref, c_ref, m_ref, n_ref, pt_ref, ps_ref):
    shape = (levels, LANES)
    level = iota(shape, 0)
    last_lane = iota((1, LANES), 1) == LANES - 1
    factors = level_factors(levels)
    zero = jnp.zeros(shape, F32)

    def step(j, carry):
        prev, m1, d2, limited2, base2, wg2, m2, acc2, acc1 = carry
        t, s = strided(t_ref, j, levels, rows), strided(s_ref, j, levels, rows)
        c, m = strided(c_ref, j, levels, rows), strided(m_ref, j, levels, rows)
        n = n_ref[pl.ds(j, 1), :]
        here = column_row(t, s, n, factors, level)
        east = shifted(here, -1)
        wet = level < jnp.minimum(n, jnp.where(last_lane, 0, east["n"]))
        steps = [face_step(here, east, wet, q) for q in "ts"]
        base, wg, forward = face_base(here, east, c, wet, steps)
        inside = level < n
        acc = []
        for q, d, flux in zip("ts", steps, base):
            limited = minmod(roll(d, 1), d)
            flux = flux + wg * jnp.where(forward, limited, roll(limited, -1))
            acc.append(jnp.where(inside, here[q], 0.0) + roll(flux, 1) - flux)
        wet = level < jnp.minimum(prev["n"], n)
        d1 = [face_step(prev, here, wet, q) for q in "ts"]
        base1, wg1, _ = face_base(prev, here, m1, wet, d1)
        limited1 = [minmod(x, y) for x, y in zip(d2, d1)]
        forward2 = m2 > 0.0
        flux2 = [b + wg2 * jnp.where(forward2, x, y) for b, x, y in zip(base2, limited2, limited1)]
        done = [x - f for x, f in zip(acc2, flux2)]
        acc1 = [x + f for x, f in zip(acc1, flux2)]
        pt_ref[pl.ds(j, 1)] = done[0][None]
        ps_ref[pl.ds(j, 1)] = done[1][None]
        return here, m, d1, limited1, base1, wg1, m1, acc1, acc

    nothing = [zero, zero]
    start = dict({name: zero for name in NAMES}, n=jnp.zeros((1, LANES), jnp.int32))
    carry = (start, zero, nothing, nothing, nothing, zero, zero, nothing, nothing)
    unroll = 4

    def block(i, carry):
        for u in range(unroll):
            carry = step(i * unroll + u, carry)
        return carry

    carry = lax.fori_loop(0, rows // unroll, block, carry)
    _, _, _, limited2, base2, wg2, m2, acc2, acc1 = carry
    flux2 = [b + wg2 * jnp.where(m2 > 0.0, x, 0.0) for b, x in zip(base2, limited2)]
    for ref, a2, a1, f in zip((pt_ref, ps_ref), acc2, acc1, flux2):
        ref[rows] = a2 - f
        ref[rows + 1] = a1 + f


def edge_kernel(
    levels, rows, top_ref, pt_ref, ps_ref, side_ref, north_ref, south_ref, own_ref,
    west_in, east_in, fold_column_in, below_in, above_in, fold_in, t_ref, s_ref,
):
    shape = (levels, LANES)
    level = iota(shape, 0).astype(F32)
    lane = iota(shape, 1)
    place = lane % 4
    factors = level_factors(levels)
    K = levels

    def faces(cells, speeds):
        wets = [level < jnp.minimum(a["n"], b["n"]) for a, b in zip(cells, cells[1:])]
        d = [[face_step(a, b, w, q) for q in "ts"] for a, b, w in zip(cells, cells[1:], wets)]
        limited = [[minmod(x, y) for x, y in zip(d[i], d[i + 1])] for i in (0, 1)]
        base, wg, forward = face_base(cells[1], cells[2], speeds[1], wets[1], d[1])
        flux = [b + wg * jnp.where(forward, x, y) for b, x, y in zip(base, *limited)]
        first = last = None
        if speeds[0] is not None:
            _, wg0 = weights(speeds[0], wets[0])
            first = [wg0 * jnp.where(speeds[0] > 0.0, 0.0, x) for x in limited[0]]
        if speeds[2] is not None:
            _, wg2 = weights(speeds[2], wets[2])
            last = [wg2 * jnp.where(speeds[2] > 0.0, x, 0.0) for x in limited[1]]
        return first, flux, last

    own, west, east = side_ref[...], west_in[...], east_in[...]

    def side(left, right):
        both = jnp.where(iota(left.shape, 1) % 4 < 2, left, right)
        row = column_row(both[:K], both[K : 2 * K], both[3 * K : 3 * K + 1], factors, iota(shape, 0))
        cells = [row] + [shifted(row, -i) for i in (1, 2, 3)]
        speed = both[2 * K : 3 * K]
        return faces(cells, [roll(speed, -i) for i in range(3)])

    _, west_flux, west_last = side(west, own)
    east_first, east_flux, _ = side(own, east)
    lon = []
    for fw, lw, fe, le in zip(west_flux, west_last, east_first, east_flux):
        group = jnp.where(
            place == 0,
            -fe,
            jnp.where(place == 1, roll(fe - le, 1), jnp.where(place == 2, roll(fw - lw, 2), roll(lw, 3))),
        )
        lon.append(group)

    def cell(array, which, fix=None):
        t, s = array[which * K : (which + 1) * K], array[(2 + which) * K : (3 + which) * K]
        return t, s

    def rows_of(array, at_counts, which):
        t, s = array[which * K : (which + 1) * K], array[(2 + which) * K : (3 + which) * K]
        n = array[at_counts + which : at_counts + which + 1]
        return column_row(t, s, n, factors, iota(shape, 0))

    below, south, north = below_in[...], south_ref[...], north_ref[...]
    own_speeds = own_ref[...]
    cells = [rows_of(below, 5 * K, 0), rows_of(below, 5 * K, 1), rows_of(south, 4 * K, 0), rows_of(south, 4 * K, 1)]
    _, south_flux, south_last = faces(cells, [None, below[4 * K : 5 * K], own_speeds[:K]])

    is_top = top_ref[0] > 0
    fold, column = fold_in[...], fold_column_in[...]
    parts = []
    for q in range(2):
        for j in (rows - 2, rows - 3):
            parts.append(roll(column[q * K : (q + 1) * K], -(4 * j + 2)))
    line = column[3 * K : 3 * K + 1]
    parts.append(
        jnp.concatenate(
            [roll(line, -(4 * (rows - 2) + 2)), roll(line, -(4 * (rows - 3) + 2)), jnp.zeros((6, LANES), F32)], axis=0
        )
    )
    fold = jnp.where(iota(fold.shape, 1) == 0, jnp.concatenate(parts, axis=0), fold)
    above = jnp.where(is_top, fold, above_in[...])
    cells = [rows_of(north, 5 * K, 0), rows_of(north, 5 * K, 1), rows_of(above, 4 * K, 0), rows_of(above, 4 * K, 1)]
    north_first, north_flux, _ = faces(cells, [own_speeds[K:], north[4 * K : 5 * K], None])

    edge_lanes = (lane >= LANES - 2) | (lane < 2)
    for q, (p_ref, out_ref) in enumerate(((pt_ref, t_ref), (ps_ref, s_ref))):
        extra = {
            0: south_flux[q] - south_last[q],
            1: south_last[q],
            rows - 2: -north_first[q],
            rows - 1: north_first[q] - north_flux[q],
        }
        for j in range(rows):
            value = p_ref[j + 2] + jnp.where(edge_lanes, roll(lon[q], LANES - 2 - 4 * j), 0.0)
            if j in extra:
                value = value + extra[j]
            out_ref[pl.ds(j, levels, stride=rows), :] = value


def body(nlat, nlon, t, s, c, m, n):
    levels, rows, _ = t.shape
    vmem = pl.BlockSpec(memory_space=pltpu.VMEM)
    flat = [x.reshape(levels * rows, LANES) for x in (t, s, c, m)]
    f = functools.partial
    out = lambda *shape: jax.ShapeDtypeStruct(shape, F32)
    K = levels
    side, north, south, fold, own = pl.pallas_call(
        f(pack_kernel, levels, rows),
        out_shape=(out(3 * K + 8, LANES), out(5 * K + 8, LANES), out(4 * K + 8, LANES), out(4 * K + 8, LANES), out(2 * K, LANES)),
        in_specs=[vmem] * 5,
        out_specs=(vmem,) * 5,
        name="pack",
    )(*flat, n)

    def at(lat, lon):
        return (lon % nlon) * nlat + lat

    ring = range(nlon)
    both = ("lon", "lat")
    west_in = lax.ppermute(side, "lon", [(i, (i + 1) % nlon) for i in ring])
    fold_in = lax.ppermute(fold, both, [(at(nlat - 1, i), at(nlat - 1, nlon - 1 - i)) for i in ring])
    fold_column_in = lax.ppermute(side, both, [(at(nlat - 1, i), at(nlat - 1, nlon - i)) for i in ring])
    east_in = lax.ppermute(side, "lon", [(i, (i - 1) % nlon) for i in ring])
    below_in = lax.ppermute(north, "lat", [(i, i + 1) for i in range(nlat - 1)])
    above_in = lax.ppermute(south, "lat", [(i + 1, i) for i in range(nlat - 1)])

    pt, ps = pl.pallas_call(
        f(interior_kernel, levels, rows),
        out_shape=(out(rows + 2, K, LANES),) * 2,
        in_specs=[vmem] * 5,
        out_specs=(vmem,) * 2,
        cost_estimate=pl.CostEstimate(flops=40_000_000, bytes_accessed=2_000_000, transcendentals=0),
        name="interior",
    )(*flat, n)

    top = (lax.axis_index("lat") == nlat - 1).astype(jnp.int32).reshape(1)
    t_next, s_next = pl.pallas_call(
        f(edge_kernel, levels, rows),
        out_shape=(out(levels * rows, LANES),) * 2,
        in_specs=[pl.BlockSpec(memory_space=pltpu.SMEM)] + [vmem] * 12,
        out_specs=(vmem,) * 2,
        name="edge",
    )(top, pt, ps, side, north, south, own, west_in, east_in, fold_column_in, below_in, above_in, fold_in)
    return t_next.reshape(t.shape), s_next.reshape(t.shape)


def solution(mesh):
    spec = P(None, "lat", "lon")
    return jax.shard_map(
        functools.partial(body, mesh.shape["lat"], mesh.shape["lon"]),
        mesh=mesh,
        in_specs=(spec,) * 4 + (P("lat", "lon"),),
        out_specs=(spec,) * 2,
        check_vma=False,
    )
```

```python
import functools

import jax
import jax.numpy as jnp
from jax import lax
from jax.experimental import pallas as pl
from jax.experimental.pallas import tpu as pltpu
from jax.sharding import PartitionSpec as P

heat_swelling_alpha = 0.1655
coef_beta = 0.76554
cabbeling_parameter = 0.05952
lambda_salt = 0.00054914
thermobaric_parameter = 0.0001497
press_salt = 1.109e-05
cross_coupling_contribution = 0.0024341
total_depth = 5000.0
kappa_iso = 0.1
strat_min = 0.1

LANES = 128
VMEM = 8 * 1024 * 1024
UNROLL = 8
F32 = jnp.float32


def iota(shape, axis):
    return lax.broadcasted_iota(jnp.int32, shape, axis)


def roll(array, shift, axis=1):
    size = array.shape[axis]
    return pltpu.roll(array, shift % size, axis)


def minmod(x, y):
    return jnp.maximum(jnp.minimum(x, jnp.maximum(y, 0.0)), jnp.minimum(y, 0.0))


def level_factors(levels):
    depth = total_depth * (iota((levels, LANES), 0).astype(F32) + 0.5) / levels
    heat = -heat_swelling_alpha * (1.0 + thermobaric_parameter * depth)
    salt = coef_beta * (1.0 - press_salt * depth)
    return heat, salt


def density(t, s, factors):
    heat, salt = factors
    return t * (
        heat
        - (0.5 * heat_swelling_alpha * cabbeling_parameter) * t
        - cross_coupling_contribution * s
    ) + s * (salt - (0.5 * coef_beta * lambda_salt) * s)


def vertical(q, level):
    levels = q.shape[0]
    step = roll(q, -1, 0) - q
    below = roll(step, 1, 0)
    return jnp.where(level == levels - 1, below, step) + jnp.where(level == 0, step, below)


def column_row(t, s, n, factors, level):
    r = density(t, s, factors)
    return {
        "t": t,
        "s": s,
        "r": r,
        "tz": vertical(t, level),
        "sz": vertical(s, level),
        "rz": vertical(r, level),
        "n": n,
    }


def shifted(row, by):
    return {name: roll(value, by) for name, value in row.items()}


def weights(c, wet):
    size = jnp.abs(c)
    return jnp.where(wet, c, 0.0), jnp.where(wet, 0.5 * (size - c * c), 0.0)


def face_step(a, b, wet, name):
    return jnp.where(wet, b[name] - a[name], 0.0)


def face_base(a, b, c, wet, steps):
    wc, wg = weights(c, wet)
    steep = (a["r"] - b["r"]) / jnp.maximum(a["rz"] + b["rz"], 4.0 * strat_min)
    tilt = jnp.where(wet, jnp.clip(steep, -0.25, 0.25), 0.0) * (-kappa_iso)
    forward = c > 0.0
    base = [
        wc * jnp.where(forward, a[q], b[q]) - kappa_iso * d + tilt * (a[q + "z"] + b[q + "z"])
        for q, d in zip("ts", steps)
    ]
    return base, wg, forward


def strided(ref, row):
    levels, rows, _ = ref.shape
    return ref.reshape(levels * rows, LANES)[pl.ds(row, levels, stride=rows), :]


def put(ref, row, value):
    levels, rows, _ = ref.shape
    ref.reshape(levels * rows, LANES)[pl.ds(row, levels, stride=rows), :] = value


def pack_kernel(
    levels, rows, lat_size, t_hbm, s_hbm, c_hbm, m_hbm, n_hbm,
    t_ref, s_ref, c_ref, m_ref, n_ref, side_ref, lat_ref, fold_ref, column_ref, own_ref, *more,
):
    *more, t_in, s_in, c_in, sems = more
    K = levels
    pairs = ((t_hbm, t_in), (s_hbm, s_in), (c_hbm, c_in), (n_hbm, n_ref), (m_hbm, m_ref))
    copies = [pltpu.make_async_copy(src, dst, sems.at[i]) for i, (src, dst) in enumerate(pairs)]
    for copy in copies:
        copy.start()
    lane = iota((levels, LANES), 1)
    group = lane // 4

    def gather(ref, rows_ref):
        out = jnp.zeros((levels, LANES), F32)
        for j in range(rows):
            row = strided(ref, j)
            rows_ref[j] = row
            out = jnp.where(group == j, roll(row, 4 * j + 2), out)
        return out

    def mirrored(x):
        index = (LANES - iota(x.shape, 1)) % LANES
        return jnp.take_along_axis(x, index, axis=1)

    def tracer_rows(out_ref, tracer, ref, picks, change=lambda x: x):
        for i, j in enumerate(picks):
            at = (2 * tracer + i) * K
            out_ref[at : at + K, :] = change(ref[j])

    south, north, fold = (0, 1), (rows - 2, rows - 1), (rows - 2, rows - 3)
    is_top = lax.axis_index("lat") == lat_size - 1
    for tracer, (ref, source) in enumerate(((t_ref, t_in), (s_ref, s_in))):
        copies[tracer].wait()
        side_ref[tracer * K : (tracer + 1) * K, :] = gather(source, ref)
        tracer_rows(fold_ref, tracer, ref, fold, mirrored)
        if more:
            tracer_rows(lat_ref, tracer, ref, north)
            tracer_rows(more[0], tracer, ref, south)
        else:
            for i in range(2):
                at = (2 * tracer + i) * K
                lat_ref[at : at + K, :] = jnp.where(is_top, ref[south[i]], ref[north[i]])

    copies[2].wait()
    side_ref[2 * K : 3 * K, :] = gather(c_in, c_ref)
    copies[3].wait()
    counts = n_ref[...].astype(F32)
    moved = jnp.concatenate([roll(counts[j : j + 1], 4 * j + 2) for j in range(rows)], axis=0)
    line = jnp.sum(
        jnp.where(iota((rows, LANES), 1) // 4 == iota((rows, LANES), 0), moved, 0.0), axis=0, keepdims=True
    )
    side_ref[3 * K :, :] = jnp.broadcast_to(line, (8, LANES))

    def tally(picks):
        return jnp.concatenate(
            [counts[j : j + 1] for j in picks] + [jnp.zeros((8 - len(picks), LANES), F32)], axis=0
        )

    fold_ref[4 * K :, :] = mirrored(tally(fold))
    first = jnp.zeros((levels, LANES), F32)
    for i, (ref, j) in enumerate((ref, j) for ref in (t_ref, s_ref) for j in fold):
        first = jnp.where(lane == i, roll(ref[j], i), first)
    column_ref[:K, :] = first
    column_ref[K : K + 8, :] = tally(fold)
    if more:
        lat_ref[5 * K :, :] = tally(north)
        more[0][4 * K : 5 * K, :] = jnp.zeros((K, LANES), F32)
        more[0][5 * K :, :] = tally(south)
    else:
        lat_ref[5 * K :, :] = jnp.where(is_top, tally(south), tally(north))
    copies[4].wait()
    lat_ref[4 * K : 5 * K, :] = strided(m_ref, rows - 1)
    for i, j in enumerate((0, rows - 2, rows - 1)):
        own_ref[i * K : (i + 1) * K, :] = strided(m_ref, j)


NAMES = ("t", "s", "r", "tz", "sz", "rz")


def interior_kernel(levels, rows, t_ref, s_ref, c_ref, m_ref, n_ref, pt_ref, ps_ref):
    shape = (levels, LANES)
    level = iota(shape, 0)
    last_lane = iota((1, LANES), 1) == LANES - 1
    factors = level_factors(levels)
    zero = jnp.zeros(shape, F32)

    def step(j, carry):
        prev, m1, d2, limited2, base2, wg2, m2, acc2, acc1 = carry
        t, s, c, m = t_ref[j], s_ref[j], c_ref[j], strided(m_ref, j)
        n = n_ref[pl.ds(j, 1), :]
        here = column_row(t, s, n, factors, level)
        east = shifted(here, -1)
        wet = level < jnp.minimum(n, jnp.where(last_lane, 0, east["n"]))
        steps = [face_step(here, east, wet, q) for q in "ts"]
        base, wg, forward = face_base(here, east, c, wet, steps)
        inside = level < n
        acc = []
        for q, d, flux in zip("ts", steps, base):
            limited = minmod(roll(d, 1), d)
            flux = flux + wg * jnp.where(forward, limited, roll(limited, -1))
            acc.append(jnp.where(inside, here[q], 0.0) + roll(flux, 1) - flux)
        wet = level < jnp.minimum(prev["n"], n)
        d1 = [face_step(prev, here, wet, q) for q in "ts"]
        base1, wg1, _ = face_base(prev, here, m1, wet, d1)
        limited1 = [minmod(x, y) for x, y in zip(d2, d1)]
        forward2 = m2 > 0.0
        flux2 = [b + wg2 * jnp.where(forward2, x, y) for b, x, y in zip(base2, limited2, limited1)]
        done = [x - f for x, f in zip(acc2, flux2)]
        acc1 = [x + f for x, f in zip(acc1, flux2)]
        pt_ref[pl.ds(j, 1)] = done[0][None]
        ps_ref[pl.ds(j, 1)] = done[1][None]
        return here, m, d1, limited1, base1, wg1, m1, acc1, acc

    nothing = [zero, zero]
    start = dict({name: zero for name in NAMES}, n=jnp.zeros((1, LANES), jnp.int32))
    carry = (start, zero, nothing, nothing, nothing, zero, zero, nothing, nothing)

    def block(i, carry):
        for u in range(UNROLL):
            carry = step(i * UNROLL + u, carry)
        return carry

    carry = lax.fori_loop(0, rows // UNROLL, block, carry)
    _, _, _, limited2, base2, wg2, m2, acc2, acc1 = carry
    flux2 = [b + wg2 * jnp.where(m2 > 0.0, x, 0.0) for b, x in zip(base2, limited2)]
    for ref, a2, a1, f in zip((pt_ref, ps_ref), acc2, acc1, flux2):
        ref[rows] = a2 - f
        ref[rows + 1] = a1 + f


def edge_kernel(
    levels, rows, lat_size, lon_size, pt_ref, ps_ref, side_ref, t_ref, s_ref, n_ref, own_ref,
    core_in, inter_in, below_in, above_in, fold_in, column_in, own_column, t_out, s_out,
    t_new, s_new, sems,
):
    shape = (levels, LANES)
    level = iota(shape, 0).astype(F32)
    lane = iota(shape, 1)
    place = lane % 4
    factors = level_factors(levels)
    K = levels
    row_at = lax.axis_index("lat")
    is_top, is_bottom = row_at == lat_size - 1, row_at == 0
    is_odd = lax.axis_index("lon") % 2 == 1

    def faces(cells, speeds):
        wets = [level < jnp.minimum(a["n"], b["n"]) for a, b in zip(cells, cells[1:])]
        d = [[face_step(a, b, w, q) for q in "ts"] for a, b, w in zip(cells, cells[1:], wets)]
        limited = [[minmod(x, y) for x, y in zip(d[i], d[i + 1])] for i in (0, 1)]
        base, wg, forward = face_base(cells[1], cells[2], speeds[1], wets[1], d[1])
        flux = [b + wg * jnp.where(forward, x, y) for b, x, y in zip(base, *limited)]
        first = last = None
        if speeds[0] is not None:
            _, wg0 = weights(speeds[0], wets[0])
            first = [wg0 * jnp.where(speeds[0] > 0.0, 0.0, x) for x in limited[0]]
        if speeds[2] is not None:
            _, wg2 = weights(speeds[2], wets[2])
            last = [wg2 * jnp.where(speeds[2] > 0.0, x, 0.0) for x in limited[1]]
        return first, flux, last

    def cell_row(t, s, n):
        return column_row(t, s, n, factors, iota(shape, 0))

    own, core, inter = side_ref[...], core_in[...], inter_in[...]
    west, east = jnp.where(is_odd, core, inter), jnp.where(is_odd, inter, core)

    def side(left, right):
        both = jnp.where(iota(left.shape, 1) % 4 < 2, left, right)
        row = cell_row(both[:K], both[K : 2 * K], both[3 * K : 3 * K + 1])
        cells = [row] + [shifted(row, -i) for i in (1, 2, 3)]
        speed = both[2 * K : 3 * K]
        return faces(cells, [roll(speed, -i) for i in range(3)])

    _, west_flux, west_last = side(west, own)
    east_first, east_flux, _ = side(own, east)
    lon = []
    for fw, lw, fe, le in zip(west_flux, west_last, east_flux, east_first):
        group = jnp.where(
            place == 0,
            -le,
            jnp.where(place == 1, roll(le - fe, 1), jnp.where(place == 2, roll(fw - lw, 2), roll(lw, 3))),
        )
        lon.append(group)

    counts = n_ref[...].astype(F32)

    def own_row(j):
        return cell_row(t_ref[j], s_ref[j], counts[j : j + 1])

    def sent_row(array, which, at_counts):
        t, s = array[which * K : (which + 1) * K], array[(2 + which) * K : (3 + which) * K]
        return cell_row(t, s, array[at_counts + which : at_counts + which + 1])

    below = jnp.where(is_bottom, 0.0, below_in[...])
    cells = [sent_row(below, 0, 5 * K), sent_row(below, 1, 5 * K), own_row(0), own_row(1)]
    _, south_flux, south_last = faces(cells, [None, below[4 * K : 5 * K], own_ref[:K]])

    pivot = (lax.axis_index("lon") * 2) % lon_size == 0
    column = jnp.where(pivot, own_column[...], column_in[...])
    parts = [roll(column[:K], -i) for i in range(4)] + [column[K : K + 8]]
    fold = fold_in[...]
    fold = jnp.where(iota(fold.shape, 1) == 0, jnp.concatenate(parts, axis=0), fold)
    above = above_in[...]
    above = jnp.where(is_top, fold, jnp.concatenate([above[: 4 * K], above[5 * K :]], axis=0))
    cells = [own_row(rows - 2), own_row(rows - 1), sent_row(above, 0, 4 * K), sent_row(above, 1, 4 * K)]
    north_first, north_flux, _ = faces(cells, [own_ref[K : 2 * K], own_ref[2 * K :], None])

    edge_lanes = (lane >= LANES - 2) | (lane < 2)

    copies = []
    for q, (p_ref, new_ref, out_ref) in enumerate(((pt_ref, t_new, t_out), (ps_ref, s_new, s_out))):

        extra = {
            0: south_flux[q] - south_last[q],
            1: south_last[q],
            rows - 2: -north_first[q],
            rows - 1: north_first[q] - north_flux[q],
        }
        for j in range(rows):
            value = p_ref[j + 2] + jnp.where(edge_lanes, roll(lon[q], LANES - 2 - 4 * j), 0.0)
            put(new_ref, j, value + extra[j] if j in extra else value)
        copies.append(pltpu.make_async_copy(new_ref, out_ref, sems.at[q]))
        copies[q].start()
    for copy in copies:
        copy.wait()


def body(nlat, nlon, t, s, c, m, n):
    levels, rows, _ = t.shape
    vmem, hbm = pl.BlockSpec(memory_space=pltpu.VMEM), pl.BlockSpec(memory_space=pltpu.HBM)
    f = functools.partial
    out = lambda *shape: jax.ShapeDtypeStruct(shape, F32)
    K = levels
    params = pltpu.CompilerParams(vmem_limit_bytes=VMEM)
    swap = nlat == 2
    field, lat_shape = out(rows, K, LANES), out(5 * K + 8, LANES)
    shapes = [field] * 3 + [out(*m.shape), jax.ShapeDtypeStruct(n.shape, n.dtype)]
    shapes += [out(3 * K + 8, LANES), lat_shape, out(4 * K + 8, LANES), out(5 * K, LANES), out(3 * K, LANES)]
    shapes += [] if swap else [lat_shape]
    t_v, s_v, c_v, m_v, n_v, side, lat, fold, column, own, *more = pl.pallas_call(
        f(pack_kernel, levels, rows, nlat),
        out_shape=tuple(shapes),
        in_specs=[hbm] * 5,
        out_specs=(vmem,) * len(shapes),
        scratch_shapes=[pltpu.VMEM(t.shape, F32)] * 3 + [pltpu.SemaphoreType.DMA((5,))],
        compiler_params=params,
        name="pack",
    )(*[pltpu.with_memory_space_constraint(x, pltpu.HBM) for x in (t, s, c, m, n)])

    def across(array, partner):
        to = {(j, i): (j, i ^ 1 if i ^ 1 < nlon else i) for j in range(nlat - 1) for i in range(nlon)}
        top = nlat - 1
        for i in range(nlon):
            to[top, i] = (top, partner(i) % nlon)
        for i in range(nlon):
            if to[top, i] == (top, i) and to.get((0, i), (0, i)) != (0, i):
                other = to[0, i]
                to[top, i], to[0, i], to[other] = (0, i), other, (top, i)
        pairs = [(i * nlat + j, to[j, i][1] * nlat + to[j, i][0]) for i in range(nlon) for j in range(nlat)]
        return lax.ppermute(array, ("lon", "lat"), pairs)

    ring, rung = range(nlon), range(nlat)
    core_in = lax.ppermute(side, "lon", [(i, i ^ 1) for i in ring])
    inter_in = lax.ppermute(side, "lon", [(i, (i + (1 if i % 2 else -1)) % nlon) for i in ring])
    below_in = above_in = lax.ppermute(lat, "lat", [(i, (i + 1) % nlat) for i in rung])
    if not swap:
        above_in = lax.ppermute(more[0], "lat", [(i, (i - 1) % nlat) for i in rung])
    fold_in = across(fold, lambda i: nlon - 1 - i)
    column_in = across(column, lambda i: nlon - i)

    pt, ps = pl.pallas_call(
        f(interior_kernel, levels, rows),
        out_shape=(out(rows + 2, K, LANES),) * 2,
        in_specs=[vmem] * 5,
        out_specs=(vmem,) * 2,
        cost_estimate=pl.CostEstimate(flops=40_000_000, bytes_accessed=2_000_000, transcendentals=0),
        compiler_params=params,
        name="interior",
    )(t_v, s_v, c_v, m_v, n_v)

    return pl.pallas_call(
        f(edge_kernel, levels, rows, nlat, nlon),
        out_shape=(out(*t.shape),) * 2,
        in_specs=[vmem] * 14,
        out_specs=(hbm,) * 2,
        scratch_shapes=[pltpu.VMEM(t.shape, F32)] * 2 + [pltpu.SemaphoreType.DMA((2,))],
        compiler_params=params,
        name="edge",
    )(pt, ps, side, t_v, s_v, n_v, own, core_in, inter_in, below_in, above_in, fold_in, column_in, column)


def solution(mesh):
    spec = P(None, "lat", "lon")
    return jax.shard_map(
        functools.partial(body, mesh.shape["lat"], mesh.shape["lon"]),
        mesh=mesh,
        in_specs=(spec,) * 4 + (P("lat", "lon"),),
        out_specs=(spec,) * 2,
        check_vma=False,
    )
```

```python
import functools

import jax
import jax.numpy as jnp
from jax import lax
from jax.experimental import pallas as pl
from jax.experimental.pallas import tpu as pltpu
from jax.sharding import PartitionSpec as P

heat_swelling_alpha = 0.1655
coef_beta = 0.76554
cabbeling_parameter = 0.05952
lambda_salt = 0.00054914
thermobaric_parameter = 0.0001497
press_salt = 1.109e-05
cross_coupling_contribution = 0.0024341
total_depth = 5000.0
kappa_iso = 0.1
strat_min = 0.1

LANES = 128
VMEM = 8 * 1024 * 1024
UNROLL = 8
F32 = jnp.float32


def iota(shape, axis):
    return lax.broadcasted_iota(jnp.int32, shape, axis)


def roll(array, shift, axis=1):
    size = array.shape[axis]
    return pltpu.roll(array, shift % size, axis)


def minmod(x, y):
    return jnp.maximum(jnp.minimum(x, jnp.maximum(y, 0.0)), jnp.minimum(y, 0.0))


def level_factors(levels):
    depth = total_depth * (iota((levels, LANES), 0).astype(F32) + 0.5) / levels
    heat = -heat_swelling_alpha * (1.0 + thermobaric_parameter * depth)
    salt = coef_beta * (1.0 - press_salt * depth)
    return heat, salt


def density(t, s, factors):
    heat, salt = factors
    return t * (
        heat
        - (0.5 * heat_swelling_alpha * cabbeling_parameter) * t
        - cross_coupling_contribution * s
    ) + s * (salt - (0.5 * coef_beta * lambda_salt) * s)


def vertical(q, level):
    levels = q.shape[0]
    step = roll(q, -1, 0) - q
    below = roll(step, 1, 0)
    return jnp.where(level == levels - 1, below, step) + jnp.where(level == 0, step, below)


def column_row(t, s, n, factors, level):
    r = density(t, s, factors)
    return {
        "t": t,
        "s": s,
        "r": r,
        "tz": vertical(t, level),
        "sz": vertical(s, level),
        "rz": vertical(r, level),
        "n": n,
    }


def shifted(row, by):
    return {name: roll(value, by) for name, value in row.items()}


def weights(c, wet):
    size = jnp.abs(c)
    return jnp.where(wet, c, 0.0), jnp.where(wet, 0.5 * (size - c * c), 0.0)


def face_step(a, b, wet, name):
    return jnp.where(wet, b[name] - a[name], 0.0)


def face_base(a, b, c, wet, steps):
    wc, wg = weights(c, wet)
    steep = (a["r"] - b["r"]) / jnp.maximum(a["rz"] + b["rz"], 4.0 * strat_min)
    tilt = jnp.where(wet, jnp.clip(steep, -0.25, 0.25), 0.0) * (-kappa_iso)
    forward = c > 0.0
    base = [
        wc * jnp.where(forward, a[q], b[q]) - kappa_iso * d + tilt * (a[q + "z"] + b[q + "z"])
        for q, d in zip("ts", steps)
    ]
    return base, wg, forward


def strided(ref, row):
    levels, rows, _ = ref.shape
    return ref.reshape(levels * rows, LANES)[pl.ds(row, levels, stride=rows), :]


def put(ref, row, value):
    levels, rows, _ = ref.shape
    ref.reshape(levels * rows, LANES)[pl.ds(row, levels, stride=rows), :] = value


def pack_kernel(
    levels, rows, lat_size, t_hbm, s_hbm, c_hbm, m_hbm, n_hbm,
    t_ref, s_ref, c_ref, m_ref, n_ref, side_ref, lat_ref, fold_ref, column_ref, own_ref, *more,
):
    *more, sems = more
    K = levels
    pairs = ((t_hbm, t_ref), (s_hbm, s_ref), (c_hbm, c_ref), (n_hbm, n_ref), (m_hbm, m_ref))
    copies = [pltpu.make_async_copy(src, dst, sems.at[i]) for i, (src, dst) in enumerate(pairs)]
    for copy in copies:
        copy.start()
    lane = iota((levels, LANES), 1)
    group = lane // 4

    slot = iota((8, LANES), 0)
    own = [iota((8, LANES), 1) // 4 == slot + 8 * block for block in range(rows // 8)]

    def gather(ref):
        tiles = []
        for base in range(0, K, 8):
            out = jnp.zeros((8, LANES), F32)
            for k in range(8):
                spread = jnp.zeros((8, LANES), F32)
                for block, mine in enumerate(own):
                    eight = ref[base + k, 8 * block : 8 * block + 8, :]
                    moved = pltpu.roll(eight, 32 * block + 2, 1, stride=4, stride_axis=0)
                    spread = jnp.where(mine, moved, spread)
                for by in (4, 2, 1):
                    spread = spread + roll(spread, by, 0)
                out = jnp.where(slot == k, spread, out)
            tiles.append(out)
        return jnp.concatenate(tiles, axis=0)

    def mirrored(x):
        index = (LANES - iota(x.shape, 1)) % LANES
        return jnp.take_along_axis(x, index, axis=1)

    def tracer_rows(out_ref, tracer, ref, picks, change=lambda x: x):
        for i, j in enumerate(picks):
            at = (2 * tracer + i) * K
            out_ref[at : at + K, :] = change(strided(ref, j))

    south, north, fold = (0, 1), (rows - 2, rows - 1), (rows - 2, rows - 3)
    is_top = lax.axis_index("lat") == lat_size - 1
    for tracer, ref in enumerate((t_ref, s_ref)):
        copies[tracer].wait()
        side_ref[tracer * K : (tracer + 1) * K, :] = gather(ref)
        tracer_rows(fold_ref, tracer, ref, fold, mirrored)
        if more:
            tracer_rows(lat_ref, tracer, ref, north)
            tracer_rows(more[0], tracer, ref, south)
        else:
            for i in range(2):
                at = (2 * tracer + i) * K
                lat_ref[at : at + K, :] = jnp.where(is_top, strided(ref, south[i]), strided(ref, north[i]))

    copies[2].wait()
    side_ref[2 * K : 3 * K, :] = gather(c_ref)
    copies[3].wait()
    counts = n_ref[...].astype(F32)
    moved = jnp.concatenate([roll(counts[j : j + 1], 4 * j + 2) for j in range(rows)], axis=0)
    line = jnp.sum(
        jnp.where(iota((rows, LANES), 1) // 4 == iota((rows, LANES), 0), moved, 0.0), axis=0, keepdims=True
    )
    side_ref[3 * K :, :] = jnp.broadcast_to(line, (8, LANES))

    def tally(picks):
        return jnp.concatenate(
            [counts[j : j + 1] for j in picks] + [jnp.zeros((8 - len(picks), LANES), F32)], axis=0
        )

    fold_ref[4 * K :, :] = mirrored(tally(fold))
    first = jnp.zeros((levels, LANES), F32)
    for i, (ref, j) in enumerate((ref, j) for ref in (t_ref, s_ref) for j in fold):
        first = jnp.where(lane == i, roll(strided(ref, j), i), first)
    column_ref[:K, :] = first
    column_ref[K : K + 8, :] = tally(fold)
    if more:
        lat_ref[5 * K :, :] = tally(north)
        more[0][4 * K : 5 * K, :] = jnp.zeros((K, LANES), F32)
        more[0][5 * K :, :] = tally(south)
    else:
        lat_ref[5 * K :, :] = jnp.where(is_top, tally(south), tally(north))
    copies[4].wait()
    lat_ref[4 * K : 5 * K, :] = strided(m_ref, rows - 1)
    for i, j in enumerate((0, rows - 2, rows - 1)):
        own_ref[i * K : (i + 1) * K, :] = strided(m_ref, j)


NAMES = ("t", "s", "r", "tz", "sz", "rz")


def interior_kernel(levels, rows, t_ref, s_ref, c_ref, m_ref, n_ref, pt_ref, ps_ref):
    shape = (levels, LANES)
    level = iota(shape, 0)
    last_lane = iota((1, LANES), 1) == LANES - 1
    factors = level_factors(levels)
    zero = jnp.zeros(shape, F32)

    def step(j, carry):
        prev, m1, d2, limited2, base2, wg2, m2, acc2, acc1 = carry
        t, s, c, m = (strided(ref, j) for ref in (t_ref, s_ref, c_ref, m_ref))
        n = n_ref[pl.ds(j, 1), :]
        here = column_row(t, s, n, factors, level)
        east = shifted(here, -1)
        wet = level < jnp.minimum(n, jnp.where(last_lane, 0, east["n"]))
        steps = [face_step(here, east, wet, q) for q in "ts"]
        base, wg, forward = face_base(here, east, c, wet, steps)
        inside = level < n
        acc = []
        for q, d, flux in zip("ts", steps, base):
            limited = minmod(roll(d, 1), d)
            flux = flux + wg * jnp.where(forward, limited, roll(limited, -1))
            acc.append(jnp.where(inside, here[q], 0.0) + roll(flux, 1) - flux)
        wet = level < jnp.minimum(prev["n"], n)
        d1 = [face_step(prev, here, wet, q) for q in "ts"]
        base1, wg1, _ = face_base(prev, here, m1, wet, d1)
        limited1 = [minmod(x, y) for x, y in zip(d2, d1)]
        forward2 = m2 > 0.0
        flux2 = [b + wg2 * jnp.where(forward2, x, y) for b, x, y in zip(base2, limited2, limited1)]
        done = [x - f for x, f in zip(acc2, flux2)]
        acc1 = [x + f for x, f in zip(acc1, flux2)]
        at = (j + rows - 2) % rows
        put(pt_ref, at, done[0])
        put(ps_ref, at, done[1])
        return here, m, d1, limited1, base1, wg1, m1, acc1, acc

    nothing = [zero, zero]
    start = dict({name: zero for name in NAMES}, n=jnp.zeros((1, LANES), jnp.int32))
    carry = (start, zero, nothing, nothing, nothing, zero, zero, nothing, nothing)

    def block(i, carry):
        for u in range(UNROLL):
            carry = step(i * UNROLL + u, carry)
        return carry

    carry = lax.fori_loop(0, rows // UNROLL, block, carry)
    _, _, _, limited2, base2, wg2, m2, acc2, acc1 = carry
    flux2 = [b + wg2 * jnp.where(m2 > 0.0, x, 0.0) for b, x in zip(base2, limited2)]
    for ref, a2, a1, f in zip((pt_ref, ps_ref), acc2, acc1, flux2):
        put(ref, rows - 2, a2 - f)
        put(ref, rows - 1, a1 + f)


def edge_kernel(
    levels, rows, lat_size, lon_size, pt_ref, ps_ref, side_ref, t_ref, s_ref, n_ref, own_ref,
    core_in, inter_in, below_in, above_in, fold_in, column_in, own_column, t_out, s_out,
    t_new, s_new, sems,
):
    shape = (levels, LANES)
    level = iota(shape, 0).astype(F32)
    lane = iota(shape, 1)
    place = lane % 4
    factors = level_factors(levels)
    K = levels
    row_at = lax.axis_index("lat")
    is_top, is_bottom = row_at == lat_size - 1, row_at == 0
    is_odd = lax.axis_index("lon") % 2 == 1

    def faces(cells, speeds):
        wets = [level < jnp.minimum(a["n"], b["n"]) for a, b in zip(cells, cells[1:])]
        d = [[face_step(a, b, w, q) for q in "ts"] for a, b, w in zip(cells, cells[1:], wets)]
        limited = [[minmod(x, y) for x, y in zip(d[i], d[i + 1])] for i in (0, 1)]
        base, wg, forward = face_base(cells[1], cells[2], speeds[1], wets[1], d[1])
        flux = [b + wg * jnp.where(forward, x, y) for b, x, y in zip(base, *limited)]
        first = last = None
        if speeds[0] is not None:
            _, wg0 = weights(speeds[0], wets[0])
            first = [wg0 * jnp.where(speeds[0] > 0.0, 0.0, x) for x in limited[0]]
        if speeds[2] is not None:
            _, wg2 = weights(speeds[2], wets[2])
            last = [wg2 * jnp.where(speeds[2] > 0.0, x, 0.0) for x in limited[1]]
        return first, flux, last

    def cell_row(t, s, n):
        return column_row(t, s, n, factors, iota(shape, 0))

    own, core, inter = side_ref[...], core_in[...], inter_in[...]
    west, east = jnp.where(is_odd, core, inter), jnp.where(is_odd, inter, core)

    def side(left, right):
        both = jnp.where(iota(left.shape, 1) % 4 < 2, left, right)
        row = cell_row(both[:K], both[K : 2 * K], both[3 * K : 3 * K + 1])
        cells = [row] + [shifted(row, -i) for i in (1, 2, 3)]
        speed = both[2 * K : 3 * K]
        return faces(cells, [roll(speed, -i) for i in range(3)])

    _, west_flux, west_last = side(west, own)
    east_first, east_flux, _ = side(own, east)
    lon = []
    for fw, lw, fe, le in zip(west_flux, west_last, east_flux, east_first):
        group = jnp.where(
            place == 0,
            -le,
            jnp.where(place == 1, roll(le - fe, 1), jnp.where(place == 2, roll(fw - lw, 2), roll(lw, 3))),
        )
        lon.append(group)

    counts = n_ref[...].astype(F32)

    def own_row(j):
        return cell_row(strided(t_ref, j), strided(s_ref, j), counts[j : j + 1])

    def sent_row(array, which, at_counts):
        t, s = array[which * K : (which + 1) * K], array[(2 + which) * K : (3 + which) * K]
        return cell_row(t, s, array[at_counts + which : at_counts + which + 1])

    below = jnp.where(is_bottom, 0.0, below_in[...])
    cells = [sent_row(below, 0, 5 * K), sent_row(below, 1, 5 * K), own_row(0), own_row(1)]
    _, south_flux, south_last = faces(cells, [None, below[4 * K : 5 * K], own_ref[:K]])

    pivot = (lax.axis_index("lon") * 2) % lon_size == 0
    column = jnp.where(pivot, own_column[...], column_in[...])
    parts = [roll(column[:K], -i) for i in range(4)] + [column[K : K + 8]]
    fold = fold_in[...]
    fold = jnp.where(iota(fold.shape, 1) == 0, jnp.concatenate(parts, axis=0), fold)
    above = above_in[...]
    above = jnp.where(is_top, fold, jnp.concatenate([above[: 4 * K], above[5 * K :]], axis=0))
    cells = [own_row(rows - 2), own_row(rows - 1), sent_row(above, 0, 4 * K), sent_row(above, 1, 4 * K)]
    north_first, north_flux, _ = faces(cells, [own_ref[K : 2 * K], own_ref[2 * K :], None])

    slot = iota((8, LANES), 0)
    last = LANES // 4 - 1
    own_lanes = [last - iota((8, LANES), 1) // 4 == slot + 8 * block for block in range(rows // 8)]
    reverse = 4 * (last - lane // 4) + place
    copies = []
    for q, (p_ref, new_ref, out_ref) in enumerate(((pt_ref, t_new, t_out), (ps_ref, s_new, s_out))):
        sides = jnp.take_along_axis(lon[q], reverse, axis=1)
        for k in range(levels):
            line = jnp.broadcast_to(sides[k : k + 1], (8, LANES))
            for block, mine in enumerate(own_lanes):
                moved = pltpu.roll(jnp.where(mine, line, 0.0), 32 * block + 2, 1, stride=4, stride_axis=0)
                at = slice(8 * block, 8 * block + 8)
                new_ref[k, at, :] = p_ref[k, at, :] + moved
        extra = {
            0: south_flux[q] - south_last[q],
            1: south_last[q],
            rows - 2: -north_first[q],
            rows - 1: north_first[q] - north_flux[q],
        }
        for j, value in extra.items():
            put(new_ref, j, strided(new_ref, j) + value)
        copies.append(pltpu.make_async_copy(new_ref, out_ref, sems.at[q]))
        copies[q].start()
    for copy in copies:
        copy.wait()


def body(nlat, nlon, t, s, c, m, n):
    levels, rows, _ = t.shape
    vmem, hbm = pl.BlockSpec(memory_space=pltpu.VMEM), pl.BlockSpec(memory_space=pltpu.HBM)
    f = functools.partial
    out = lambda *shape: jax.ShapeDtypeStruct(shape, F32)
    K = levels
    params = pltpu.CompilerParams(vmem_limit_bytes=VMEM)
    swap = nlat == 2
    field, lat_shape = out(rows, K, LANES), out(5 * K + 8, LANES)
    shapes = [out(*t.shape)] * 4 + [jax.ShapeDtypeStruct(n.shape, n.dtype)]
    shapes += [out(3 * K + 8, LANES), lat_shape, out(4 * K + 8, LANES), out(5 * K, LANES), out(3 * K, LANES)]
    shapes += [] if swap else [lat_shape]
    t_v, s_v, c_v, m_v, n_v, side, lat, fold, column, own, *more = pl.pallas_call(
        f(pack_kernel, levels, rows, nlat),
        out_shape=tuple(shapes),
        in_specs=[hbm] * 5,
        out_specs=(vmem,) * len(shapes),
        scratch_shapes=[pltpu.SemaphoreType.DMA((5,))],
        compiler_params=params,
        name="pack",
    )(*[pltpu.with_memory_space_constraint(x, pltpu.HBM) for x in (t, s, c, m, n)])

    def across(array, partner):
        to = {(j, i): (j, i ^ 1 if i ^ 1 < nlon else i) for j in range(nlat - 1) for i in range(nlon)}
        top = nlat - 1
        for i in range(nlon):
            to[top, i] = (top, partner(i) % nlon)
        for i in range(nlon):
            if to[top, i] == (top, i) and to.get((0, i), (0, i)) != (0, i):
                other = to[0, i]
                to[top, i], to[0, i], to[other] = (0, i), other, (top, i)
        pairs = [(i * nlat + j, to[j, i][1] * nlat + to[j, i][0]) for i in range(nlon) for j in range(nlat)]
        return lax.ppermute(array, ("lon", "lat"), pairs)

    ring, rung = range(nlon), range(nlat)
    core_in = lax.ppermute(side, "lon", [(i, i ^ 1) for i in ring])
    inter_in = lax.ppermute(side, "lon", [(i, (i + (1 if i % 2 else -1)) % nlon) for i in ring])
    below_in = above_in = lax.ppermute(lat, "lat", [(i, (i + 1) % nlat) for i in rung])
    if not swap:
        above_in = lax.ppermute(more[0], "lat", [(i, (i - 1) % nlat) for i in rung])
    fold_in = across(fold, lambda i: nlon - 1 - i)
    column_in = across(column, lambda i: nlon - i)

    pt, ps = pl.pallas_call(
        f(interior_kernel, levels, rows),
        out_shape=(out(*t.shape),) * 2,
        in_specs=[vmem] * 5,
        out_specs=(vmem,) * 2,
        cost_estimate=pl.CostEstimate(flops=40_000_000, bytes_accessed=2_000_000, transcendentals=0),
        compiler_params=params,
        name="interior",
    )(t_v, s_v, c_v, m_v, n_v)

    return pl.pallas_call(
        f(edge_kernel, levels, rows, nlat, nlon),
        out_shape=(out(*t.shape),) * 2,
        in_specs=[vmem] * 14,
        out_specs=(hbm,) * 2,
        scratch_shapes=[pltpu.VMEM(t.shape, F32)] * 2 + [pltpu.SemaphoreType.DMA((2,))],
        compiler_params=params,
        name="edge",
    )(pt, ps, side, t_v, s_v, n_v, own, core_in, inter_in, below_in, above_in, fold_in, column_in, column)


def solution(mesh):
    spec = P(None, "lat", "lon")
    return jax.shard_map(
        functools.partial(body, mesh.shape["lat"], mesh.shape["lon"]),
        mesh=mesh,
        in_specs=(spec,) * 4 + (P("lat", "lon"),),
        out_specs=(spec,) * 2,
        check_vma=False,
    )
```

```python
import functools

import jax
import jax.numpy as jnp
from jax import lax
from jax.experimental import pallas as pl
from jax.experimental.pallas import tpu as pltpu
from jax.sharding import PartitionSpec as P

heat_swelling_alpha = 0.1655
coef_beta = 0.76554
cabbeling_parameter = 0.05952
lambda_salt = 0.00054914
thermobaric_parameter = 0.0001497
press_salt = 1.109e-05
cross_coupling_contribution = 0.0024341
total_depth = 5000.0
kappa_iso = 0.1
strat_min = 0.1

LANES = 128
VMEM = 8 * 1024 * 1024
UNROLL = 8
HEAD = 8
F32 = jnp.float32


def iota(shape, axis):
    return lax.broadcasted_iota(jnp.int32, shape, axis)


def roll(array, shift, axis=1):
    size = array.shape[axis]
    return pltpu.roll(array, shift % size, axis)


def minmod(x, y):
    return jnp.maximum(jnp.minimum(x, jnp.maximum(y, 0.0)), jnp.minimum(y, 0.0))


def level_factors(levels):
    depth = total_depth * (iota((levels, LANES), 0).astype(F32) + 0.5) / levels
    heat = -heat_swelling_alpha * (1.0 + thermobaric_parameter * depth)
    salt = coef_beta * (1.0 - press_salt * depth)
    return heat, salt


def density(t, s, factors):
    heat, salt = factors
    return t * (
        heat
        - (0.5 * heat_swelling_alpha * cabbeling_parameter) * t
        - cross_coupling_contribution * s
    ) + s * (salt - (0.5 * coef_beta * lambda_salt) * s)


def vertical(q, level):
    levels = q.shape[0]
    step = roll(q, -1, 0) - q
    below = roll(step, 1, 0)
    return jnp.where(level == levels - 1, below, step) + jnp.where(level == 0, step, below)


def column_row(t, s, n, factors, level):
    r = density(t, s, factors)
    return {
        "t": t,
        "s": s,
        "r": r,
        "tz": vertical(t, level),
        "sz": vertical(s, level),
        "rz": vertical(r, level),
        "n": n,
    }


def shifted(row, by):
    return {name: roll(value, by) for name, value in row.items()}


def weights(c, wet):
    size = jnp.abs(c)
    return jnp.where(wet, c, 0.0), jnp.where(wet, 0.5 * (size - c * c), 0.0)


def face_step(a, b, wet, name):
    return jnp.where(wet, b[name] - a[name], 0.0)


def face_base(a, b, c, wet, steps):
    wc, wg = weights(c, wet)
    steep = (a["r"] - b["r"]) / jnp.maximum(a["rz"] + b["rz"], 4.0 * strat_min)
    tilt = jnp.where(wet, jnp.clip(steep, -0.25, 0.25), 0.0) * (-kappa_iso)
    forward = c > 0.0
    base = [
        wc * jnp.where(forward, a[q], b[q]) - kappa_iso * d + tilt * (a[q + "z"] + b[q + "z"])
        for q, d in zip("ts", steps)
    ]
    return base, wg, forward


def strided(ref, row):
    levels, rows, _ = ref.shape
    return ref.reshape(levels * rows, LANES)[pl.ds(row, levels, stride=rows), :]


def put(ref, row, value):
    levels, rows, _ = ref.shape
    ref.reshape(levels * rows, LANES)[pl.ds(row, levels, stride=rows), :] = value


def pack_kernel(
    levels, rows, lat_size, t_hbm, s_hbm, c_hbm, m_hbm, n_hbm,
    t_ref, s_ref, c_ref, m_ref, n_ref, side_ref, lat_ref, far_ref, column_ref, own_ref, *more,
):
    *more, sems = more
    K = levels
    pairs = ((t_hbm, t_ref), (s_hbm, s_ref), (c_hbm, c_ref), (n_hbm, n_ref), (m_hbm, m_ref))
    copies = [pltpu.make_async_copy(src, dst, sems.at[i]) for i, (src, dst) in enumerate(pairs)]
    for copy in copies:
        copy.start()
    lane = iota((levels, LANES), 1)
    group = lane // 4

    slot = iota((8, LANES), 0)
    own = [iota((8, LANES), 1) // 4 == slot + 8 * block for block in range(rows // 8)]

    def gather(ref):
        tiles = []
        for base in range(0, K, 8):
            out = jnp.zeros((8, LANES), F32)
            for k in range(8):
                spread = jnp.zeros((8, LANES), F32)
                for block, mine in enumerate(own):
                    eight = ref[base + k, 8 * block : 8 * block + 8, :]
                    moved = pltpu.roll(eight, 32 * block + 2, 1, stride=4, stride_axis=0)
                    spread = jnp.where(mine, moved, spread)
                for by in (4, 2, 1):
                    spread = spread + roll(spread, by, 0)
                out = jnp.where(slot == k, spread, out)
            tiles.append(out)
        return jnp.concatenate(tiles, axis=0)

    def put_side(at, value):
        size = value.shape[0]
        side_ref[at : at + size, :] = value
        far_ref[4 * K + 8 + at : 4 * K + 8 + at + size, :] = value

    def mirrored(x):
        index = (LANES - iota(x.shape, 1)) % LANES
        return jnp.take_along_axis(x, index, axis=1)

    def tracer_rows(out_ref, tracer, ref, picks, change=lambda x: x):
        for i, j in enumerate(picks):
            at = (2 * tracer + i) * K
            out_ref[at : at + K, :] = change(strided(ref, j))

    south, north, fold = (0, 1), (rows - 2, rows - 1), (rows - 2, rows - 3)
    is_top = lax.axis_index("lat") == lat_size - 1
    for tracer, ref in enumerate((t_ref, s_ref)):
        copies[tracer].wait()
        put_side(tracer * K, gather(ref))
        tracer_rows(far_ref, tracer, ref, fold, mirrored)
        if more:
            tracer_rows(lat_ref, tracer, ref, north)
            tracer_rows(more[0], tracer, ref, south)
        else:
            for i in range(2):
                at = (2 * tracer + i) * K
                lat_ref[at : at + K, :] = jnp.where(is_top, strided(ref, south[i]), strided(ref, north[i]))

    copies[2].wait()
    put_side(2 * K, gather(c_ref))
    copies[3].wait()
    counts = n_ref[...].astype(F32)
    moved = jnp.concatenate([roll(counts[j : j + 1], 4 * j + 2) for j in range(rows)], axis=0)
    line = jnp.sum(
        jnp.where(iota((rows, LANES), 1) // 4 == iota((rows, LANES), 0), moved, 0.0), axis=0, keepdims=True
    )
    put_side(3 * K, jnp.broadcast_to(line, (8, LANES)))

    def tally(picks):
        return jnp.concatenate(
            [counts[j : j + 1] for j in picks] + [jnp.zeros((8 - len(picks), LANES), F32)], axis=0
        )

    far_ref[4 * K : 4 * K + 8, :] = mirrored(tally(fold))
    first = jnp.zeros((levels, LANES), F32)
    for i, (ref, j) in enumerate((ref, j) for ref in (t_ref, s_ref) for j in fold):
        first = jnp.where(lane == i, roll(strided(ref, j), i), first)
    column_ref[:K, :] = first
    column_ref[K : K + 8, :] = tally(fold)
    if more:
        lat_ref[5 * K :, :] = tally(north)
        more[0][4 * K : 5 * K, :] = jnp.zeros((K, LANES), F32)
        more[0][5 * K :, :] = tally(south)
    else:
        lat_ref[5 * K :, :] = jnp.where(is_top, tally(south), tally(north))
    copies[4].wait()
    lat_ref[4 * K : 5 * K, :] = strided(m_ref, rows - 1)
    for i, j in enumerate((0, rows - 2, rows - 1)):
        own_ref[i * K : (i + 1) * K, :] = strided(m_ref, j)


def relay_kernel(far_ref, _, out_ref):
    K = out_ref.shape[0] - 8
    lane = iota((K, LANES), 1)
    out = far_ref[:K, :]
    for i in (1, 2, 3):
        out = jnp.where(lane == i, roll(far_ref[i * K : (i + 1) * K, :], i), out)
    out_ref[:K, :] = out
    out_ref[K:, :] = far_ref[4 * K : 4 * K + 8, :]


NAMES = ("t", "s", "r", "tz", "sz", "rz")
STATE = 19


def south_kernel(levels, rows, last, lat_size, on_top, t_ref, s_ref, c_ref, m_ref, n_ref, *more):
    pt_ref, ps_ref, state_out = more[3:6]

    @pl.when((lax.axis_index("lat") == lat_size - 1) == on_top)
    def _():
        interior_kernel(levels, rows, 0, last, t_ref, s_ref, c_ref, m_ref, n_ref, pt_ref, ps_ref, state_out)


def interior_kernel(levels, rows, first, last, t_ref, s_ref, c_ref, m_ref, n_ref, *more):
    if first:
        _, _, _, state_in, pt_ref, ps_ref = more
    else:
        pt_ref, ps_ref, state_out = more
    shape = (levels, LANES)
    level = iota(shape, 0)
    last_lane = iota((1, LANES), 1) == LANES - 1
    factors = level_factors(levels)
    zero = jnp.zeros(shape, F32)

    def step(j, carry):
        prev, m1, d2, limited2, base2, wg2, m2, acc2, acc1 = carry
        t, s, c, m = (strided(ref, j) for ref in (t_ref, s_ref, c_ref, m_ref))
        n = n_ref[pl.ds(j, 1), :]
        here = column_row(t, s, n, factors, level)
        east = shifted(here, -1)
        wet = level < jnp.minimum(n, jnp.where(last_lane, 0, east["n"]))
        steps = [face_step(here, east, wet, q) for q in "ts"]
        base, wg, forward = face_base(here, east, c, wet, steps)
        inside = level < n
        acc = []
        for q, d, flux in zip("ts", steps, base):
            limited = minmod(roll(d, 1), d)
            flux = flux + wg * jnp.where(forward, limited, roll(limited, -1))
            acc.append(jnp.where(inside, here[q], 0.0) + roll(flux, 1) - flux)
        wet = level < jnp.minimum(prev["n"], n)
        d1 = [face_step(prev, here, wet, q) for q in "ts"]
        base1, wg1, _ = face_base(prev, here, m1, wet, d1)
        limited1 = [minmod(x, y) for x, y in zip(d2, d1)]
        forward2 = m2 > 0.0
        flux2 = [b + wg2 * jnp.where(forward2, x, y) for b, x, y in zip(base2, limited2, limited1)]
        done = [x - f for x, f in zip(acc2, flux2)]
        acc1 = [x + f for x, f in zip(acc1, flux2)]
        at = (j + rows - 2) % rows
        put(pt_ref, at, done[0])
        put(ps_ref, at, done[1])
        return here, m, d1, limited1, base1, wg1, m1, acc1, acc

    def pack(carry):
        prev, m1, d2, limited2, base2, wg2, m2, acc2, acc1 = carry
        return [prev[name] for name in NAMES] + [m1, *d2, *limited2, *base2, wg2, m2, *acc2, *acc1]

    def unpack(flat, n):
        prev = dict(zip(NAMES, flat), n=n)
        m1, d2, limited2, base2, wg2, m2, acc2, acc1 = (
            flat[6], flat[7:9], flat[9:11], flat[11:13], flat[13], flat[14], flat[15:17], flat[17:19]
        )
        return prev, m1, d2, limited2, base2, wg2, m2, acc2, acc1

    if first:
        carry = unpack([state_in[i] for i in range(STATE)], n_ref[first - 1 : first, :])
    else:
        carry = unpack([zero] * STATE, jnp.zeros((1, LANES), jnp.int32))

    def block(i, carry):
        for u in range(UNROLL):
            carry = step(first + i * UNROLL + u, carry)
        return carry

    carry = lax.fori_loop(0, (last - first) // UNROLL, block, carry)
    if last < rows:
        for i, value in enumerate(pack(carry)):
            state_out[i] = value
        return
    _, _, _, limited2, base2, wg2, m2, acc2, acc1 = carry
    flux2 = [b + wg2 * jnp.where(m2 > 0.0, x, 0.0) for b, x in zip(base2, limited2)]
    for ref, a2, a1, f in zip((pt_ref, ps_ref), acc2, acc1, flux2):
        put(ref, rows - 2, a2 - f)
        put(ref, rows - 1, a1 + f)


def edge_kernel(
    levels, rows, lat_size, lon_size, pt_ref, ps_ref, side_ref, t_ref, s_ref, n_ref, own_ref,
    near_in, core_in, far_in, below_in, above_in, column_in, relay_in, own_column, t_out, s_out,
    t_new, s_new, sems,
):
    shape = (levels, LANES)
    level = iota(shape, 0).astype(F32)
    lane = iota(shape, 1)
    place = lane % 4
    factors = level_factors(levels)
    K = levels
    row_at = lax.axis_index("lat")
    is_top, is_bottom = row_at == lat_size - 1, row_at == 0
    lon_at = lax.axis_index("lon")
    is_odd = lon_at % 2 == 1
    wraps = (lon_at == 0) | (lon_at == lon_size - 1)

    def faces(cells, speeds):
        wets = [level < jnp.minimum(a["n"], b["n"]) for a, b in zip(cells, cells[1:])]
        d = [[face_step(a, b, w, q) for q in "ts"] for a, b, w in zip(cells, cells[1:], wets)]
        limited = [[minmod(x, y) for x, y in zip(d[i], d[i + 1])] for i in (0, 1)]
        base, wg, forward = face_base(cells[1], cells[2], speeds[1], wets[1], d[1])
        flux = [b + wg * jnp.where(forward, x, y) for b, x, y in zip(base, *limited)]
        first = last = None
        if speeds[0] is not None:
            _, wg0 = weights(speeds[0], wets[0])
            first = [wg0 * jnp.where(speeds[0] > 0.0, 0.0, x) for x in limited[0]]
        if speeds[2] is not None:
            _, wg2 = weights(speeds[2], wets[2])
            last = [wg2 * jnp.where(speeds[2] > 0.0, x, 0.0) for x in limited[1]]
        return first, flux, last

    def cell_row(t, s, n):
        return column_row(t, s, n, factors, iota(shape, 0))

    own, core = side_ref[...], core_in[...]
    inter = jnp.where(is_top & ~wraps, near_in[...], far_in[4 * K + 8 :, :])
    west, east = jnp.where(is_odd, core, inter), jnp.where(is_odd, inter, core)

    def side(left, right):
        both = jnp.where(iota(left.shape, 1) % 4 < 2, left, right)
        row = cell_row(both[:K], both[K : 2 * K], both[3 * K : 3 * K + 1])
        cells = [row] + [shifted(row, -i) for i in (1, 2, 3)]
        speed = both[2 * K : 3 * K]
        return faces(cells, [roll(speed, -i) for i in range(3)])

    _, west_flux, west_last = side(west, own)
    east_first, east_flux, _ = side(own, east)
    lon = []
    for fw, lw, fe, le in zip(west_flux, west_last, east_flux, east_first):
        group = jnp.where(
            place == 0,
            -le,
            jnp.where(place == 1, roll(le - fe, 1), jnp.where(place == 2, roll(fw - lw, 2), roll(lw, 3))),
        )
        lon.append(group)

    counts = n_ref[...].astype(F32)

    def own_row(j):
        return cell_row(strided(t_ref, j), strided(s_ref, j), counts[j : j + 1])

    def sent_row(array, which, at_counts):
        t, s = array[which * K : (which + 1) * K], array[(2 + which) * K : (3 + which) * K]
        return cell_row(t, s, array[at_counts + which : at_counts + which + 1])

    below = jnp.where(is_bottom, 0.0, below_in[...])
    cells = [sent_row(below, 0, 5 * K), sent_row(below, 1, 5 * K), own_row(0), own_row(1)]
    _, south_flux, south_last = faces(cells, [None, below[4 * K : 5 * K], own_ref[:K]])

    pivot = (lon_at * 2) % lon_size == 0
    column = jnp.where(is_odd, relay_in[...], jnp.where(pivot, own_column[: K + 8, :], column_in[: K + 8, :]))
    parts = [roll(column[:K], -i) for i in range(4)] + [column[K : K + 8]]
    fold = far_in[: 4 * K + 8, :]
    fold = jnp.where(iota(fold.shape, 1) == 0, jnp.concatenate(parts, axis=0), fold)
    above = above_in[...]
    above = jnp.where(is_top, fold, jnp.concatenate([above[: 4 * K], above[5 * K :]], axis=0))
    cells = [own_row(rows - 2), own_row(rows - 1), sent_row(above, 0, 4 * K), sent_row(above, 1, 4 * K)]
    north_first, north_flux, _ = faces(cells, [own_ref[K : 2 * K], own_ref[2 * K :], None])

    slot = iota((8, LANES), 0)
    last = LANES // 4 - 1
    own_lanes = [last - iota((8, LANES), 1) // 4 == slot + 8 * block for block in range(rows // 8)]
    reverse = 4 * (last - lane // 4) + place
    copies = []
    for q, (p_ref, new_ref, out_ref) in enumerate(((pt_ref, t_new, t_out), (ps_ref, s_new, s_out))):
        sides = jnp.take_along_axis(lon[q], reverse, axis=1)
        for k in range(levels):
            line = jnp.broadcast_to(sides[k : k + 1], (8, LANES))
            for block, mine in enumerate(own_lanes):
                moved = pltpu.roll(jnp.where(mine, line, 0.0), 32 * block + 2, 1, stride=4, stride_axis=0)
                at = slice(8 * block, 8 * block + 8)
                new_ref[k, at, :] = p_ref[k, at, :] + moved
        extra = {
            0: south_flux[q] - south_last[q],
            1: south_last[q],
            rows - 2: -north_first[q],
            rows - 1: north_first[q] - north_flux[q],
        }
        for j, value in extra.items():
            put(new_ref, j, strided(new_ref, j) + value)
        copies.append(pltpu.make_async_copy(new_ref, out_ref, sems.at[q]))
        copies[q].start()
    for copy in copies:
        copy.wait()


def body(nlat, nlon, t, s, c, m, n):
    levels, rows, _ = t.shape
    vmem, hbm = pl.BlockSpec(memory_space=pltpu.VMEM), pl.BlockSpec(memory_space=pltpu.HBM)
    f = functools.partial
    out = lambda *shape: jax.ShapeDtypeStruct(shape, F32)
    K = levels
    params = pltpu.CompilerParams(vmem_limit_bytes=VMEM)
    swap = nlat == 2
    field, lat_shape = out(rows, K, LANES), out(5 * K + 8, LANES)
    shapes = [out(*t.shape)] * 4 + [jax.ShapeDtypeStruct(n.shape, n.dtype)]
    shapes += [out(3 * K + 8, LANES), lat_shape, out(7 * K + 16, LANES), out(4 * K, LANES), out(3 * K, LANES)]
    shapes += [] if swap else [lat_shape]
    t_v, s_v, c_v, m_v, n_v, side, lat, far, column, own, *more = pl.pallas_call(
        f(pack_kernel, levels, rows, nlat),
        out_shape=tuple(shapes),
        in_specs=[hbm] * 5,
        out_specs=(vmem,) * len(shapes),
        scratch_shapes=[pltpu.SemaphoreType.DMA((5,))],
        compiler_params=params,
        name="pack",
    )(*[pltpu.with_memory_space_constraint(x, pltpu.HBM) for x in (t, s, c, m, n)])

    top = nlat - 1

    def exchange(array, top_to, others_to, helper=lambda i: i):
        to = {(j, i): (j, others_to(i)) for j in range(top) for i in range(nlon)}
        for i in range(nlon):
            partner, via = top_to(i), helper(i)
            if partner is not None:
                to[top, i] = (top, partner)
            elif to.get((0, via)) == (0, via ^ 1) and to.get((0, via ^ 1)) == (0, via):
                to[top, i], to[0, via], to[0, via ^ 1] = (0, via), (0, via ^ 1), (top, i)
            else:
                to[top, i] = (top, i)
        pairs = [(i * nlat + j, to[j, i][1] * nlat + to[j, i][0]) for i in range(nlon) for j in range(nlat)]
        return lax.ppermute(array, ("lon", "lat"), pairs)

    def chips(i):
        return (i + (1 if i % 2 else -1)) % nlon

    def columns(i):
        if i % 2:
            return i ^ 1 if columns(i ^ 1) == i else None
        return i ^ 1 if 2 * i % nlon == 0 else nlon - i

    ring, rung = range(nlon), range(nlat)
    far_in = exchange(far, lambda i: nlon - 1 - i, chips)

    middle = HEAD
    fields = (t_v, s_v, c_v, m_v, n_v)
    results = (out(*t.shape), out(*t.shape), out(STATE, K, LANES))
    cost = pl.CostEstimate(flops=20_000_000, bytes_accessed=1_000_000, transcendentals=0)
    pt, ps, state, lat, side, column = pl.pallas_call(
        f(south_kernel, levels, rows, middle, nlat, False),
        out_shape=results + tuple(out(*x.shape) for x in (lat, side, column)),
        in_specs=[vmem] * 8,
        out_specs=(vmem,) * 6,
        input_output_aliases={5: 3, 6: 4, 7: 5},
        cost_estimate=cost,
        compiler_params=params,
        name="south_of_others",
    )(*fields, lat, side, column)
    below_in = above_in = lax.ppermute(lat, "lat", [(i, (i + 1) % nlat) for i in rung])
    if not swap:
        above_in = lax.ppermute(more[0], "lat", [(i, (i - 1) % nlat) for i in rung])
    near_in = exchange(
        side,
        lambda i: chips(i) if 0 < i < nlon - 1 else None,
        lambda i: i ^ 1,
        lambda i: i + nlon // 4 if i == 0 else i - nlon // 4,
    )
    core_in = lax.ppermute(side, "lon", [(i, i ^ 1) for i in ring])
    column_in = exchange(column, columns, lambda i: i ^ 1)

    pt, ps, state = pl.pallas_call(
        f(south_kernel, levels, rows, middle, nlat, True),
        out_shape=results,
        in_specs=[vmem] * 8,
        out_specs=(vmem,) * 3,
        input_output_aliases={5: 0, 6: 1, 7: 2},
        cost_estimate=cost,
        compiler_params=params,
        name="south_of_top",
    )(*fields, pt, ps, state)
    relay = pl.pallas_call(
        relay_kernel,
        out_shape=out(K + 8, LANES),
        in_specs=[vmem] * 2,
        out_specs=vmem,
        compiler_params=params,
        name="relay",
    )(far_in, state)
    relay_in = lax.ppermute(relay, "lon", [(i, i ^ 1) for i in ring])

    pt, ps = pl.pallas_call(
        f(interior_kernel, levels, rows, middle, rows),
        out_shape=(out(*t.shape), out(*t.shape)),
        in_specs=[vmem] * 9,
        out_specs=(vmem,) * 2,
        input_output_aliases={5: 0, 6: 1},
        cost_estimate=pl.CostEstimate(flops=20_000_000, bytes_accessed=1_000_000, transcendentals=0),
        compiler_params=params,
        name="interior_north",
    )(*fields, pt, ps, relay, state)

    return pl.pallas_call(
        f(edge_kernel, levels, rows, nlat, nlon),
        out_shape=(out(*t.shape),) * 2,
        in_specs=[vmem] * 15,
        out_specs=(hbm,) * 2,
        scratch_shapes=[pltpu.VMEM(t.shape, F32)] * 2 + [pltpu.SemaphoreType.DMA((2,))],
        compiler_params=params,
        name="edge",
    )(pt, ps, side, t_v, s_v, n_v, own, near_in, core_in, far_in, below_in, above_in, column_in, relay_in, column)


def solution(mesh):
    spec = P(None, "lat", "lon")
    return jax.shard_map(
        functools.partial(body, mesh.shape["lat"], mesh.shape["lon"]),
        mesh=mesh,
        in_specs=(spec,) * 4 + (P("lat", "lon"),),
        out_specs=(spec,) * 2,
        check_vma=False,
    )
```

```python
import functools

import jax
import jax.numpy as jnp
from jax import lax
from jax.experimental import pallas as pl
from jax.experimental.pallas import tpu as pltpu
from jax.sharding import PartitionSpec as P

heat_swelling_alpha = 0.1655
coef_beta = 0.76554
cabbeling_parameter = 0.05952
lambda_salt = 0.00054914
thermobaric_parameter = 0.0001497
press_salt = 1.109e-05
cross_coupling_contribution = 0.0024341
total_depth = 5000.0
kappa_iso = 0.1
strat_min = 0.1

LANES = 128
VMEM = 8 * 1024 * 1024
UNROLL = 8
HEAD = 16
SPARE = 8
F32 = jnp.float32


def iota(shape, axis):
    return lax.broadcasted_iota(jnp.int32, shape, axis)


def roll(array, shift, axis=1):
    size = array.shape[axis]
    return pltpu.roll(array, shift % size, axis)


def minmod(x, y):
    return jnp.maximum(jnp.minimum(x, jnp.maximum(y, 0.0)), jnp.minimum(y, 0.0))


def level_factors(levels):
    depth = total_depth * (iota((levels, LANES), 0).astype(F32) + 0.5) / levels
    heat = -heat_swelling_alpha * (1.0 + thermobaric_parameter * depth)
    salt = coef_beta * (1.0 - press_salt * depth)
    return heat, salt


def density(t, s, factors):
    heat, salt = factors
    return t * (
        heat
        - (0.5 * heat_swelling_alpha * cabbeling_parameter) * t
        - cross_coupling_contribution * s
    ) + s * (salt - (0.5 * coef_beta * lambda_salt) * s)


def vertical(q, level):
    levels = q.shape[0]
    step = roll(q, -1, 0) - q
    below = roll(step, 1, 0)
    return jnp.where(level == levels - 1, below, step) + jnp.where(level == 0, step, below)


def column_row(t, s, n, factors, level):
    r = density(t, s, factors)
    return {
        "t": t,
        "s": s,
        "r": r,
        "tz": vertical(t, level),
        "sz": vertical(s, level),
        "rz": vertical(r, level),
        "n": n,
    }


def shifted(row, by):
    return {name: roll(value, by) for name, value in row.items()}


def weights(c, wet):
    size = jnp.abs(c)
    return jnp.where(wet, c, 0.0), jnp.where(wet, 0.5 * (size - c * c), 0.0)


def face_step(a, b, wet, name):
    return jnp.where(wet, b[name] - a[name], 0.0)


def face_base(a, b, c, wet, steps):
    wc, wg = weights(c, wet)
    steep = (a["r"] - b["r"]) / jnp.maximum(a["rz"] + b["rz"], 4.0 * strat_min)
    tilt = jnp.where(wet, jnp.clip(steep, -0.25, 0.25), 0.0) * (-kappa_iso)
    forward = c > 0.0
    base = [
        wc * jnp.where(forward, a[q], b[q]) - kappa_iso * d + tilt * (a[q + "z"] + b[q + "z"])
        for q, d in zip("ts", steps)
    ]
    return base, wg, forward


def strided(ref, row):
    levels, rows, _ = ref.shape
    return ref.reshape(levels * rows, LANES)[pl.ds(row, levels, stride=rows), :]


def put(ref, row, value):
    levels, rows, _ = ref.shape
    ref.reshape(levels * rows, LANES)[pl.ds(row, levels, stride=rows), :] = value


def pack_kernel(
    levels, rows, lat_size, t_hbm, s_hbm, c_hbm, m_hbm, n_hbm,
    t_ref, s_ref, c_ref, m_ref, n_ref, side_ref, core_ref, chip_ref, lat_ref, far_ref, column_ref, own_ref, *more,
):
    *more, sems = more
    K = levels
    pairs = ((t_hbm, t_ref), (s_hbm, s_ref), (c_hbm, c_ref), (n_hbm, n_ref), (m_hbm, m_ref))
    pairs = [(src, dst if dst is n_ref else dst.at[:, :rows]) for src, dst in pairs]
    copies = [pltpu.make_async_copy(src, dst, sems.at[i]) for i, (src, dst) in enumerate(pairs)]
    for copy in copies:
        copy.start()
    lane = iota((levels, LANES), 1)
    group = lane // 4

    slot = iota((8, LANES), 0)
    own = [iota((8, LANES), 1) // 4 == slot + 8 * block for block in range(rows // 8)]

    def gather(ref):
        tiles = []
        for base in range(0, K, 8):
            out = jnp.zeros((8, LANES), F32)
            for k in range(8):
                spread = jnp.zeros((8, LANES), F32)
                for block, mine in enumerate(own):
                    eight = ref[base + k, 8 * block : 8 * block + 8, :]
                    moved = pltpu.roll(eight, 32 * block + 2, 1, stride=4, stride_axis=0)
                    spread = jnp.where(mine, moved, spread)
                for by in (4, 2, 1):
                    spread = spread + roll(spread, by, 0)
                out = jnp.where(slot == k, spread, out)
            tiles.append(out)
        return jnp.concatenate(tiles, axis=0)

    def mirrored(x):
        index = (LANES - iota(x.shape, 1)) % LANES
        return jnp.take_along_axis(x, index, axis=1)

    def tracer_rows(out_ref, tracer, ref, picks, change=lambda x: x):
        for i, j in enumerate(picks):
            at = (2 * tracer + i) * K
            out_ref[at : at + K, :] = change(strided(ref, j))

    south, north, fold = (0, 1), (rows - 2, rows - 1), (rows - 2, rows - 3)
    is_top = lax.axis_index("lat") == lat_size - 1
    is_odd = lax.axis_index("lon") % 2 == 1
    place = iota((levels, LANES), 1) % 4
    sides = []
    for tracer, ref in enumerate((t_ref, s_ref)):
        copies[tracer].wait()
        sides.append(gather(ref))
        tracer_rows(far_ref, tracer, ref, fold, mirrored)
        if more:
            tracer_rows(lat_ref, tracer, ref, north)
            tracer_rows(more[0], tracer, ref, south)
        else:
            for i in range(2):
                at = (2 * tracer + i) * K
                lat_ref[at : at + K, :] = jnp.where(is_top, strided(ref, south[i]), strided(ref, north[i]))

    copies[2].wait()
    sides.append(gather(c_ref))
    copies[3].wait()
    counts = n_ref[...].astype(F32)
    moved = jnp.concatenate([roll(counts[j : j + 1], 4 * j + 2) for j in range(rows)], axis=0)
    line = jnp.sum(
        jnp.where(iota((rows, LANES), 1) // 4 == iota((rows, LANES), 0), moved, 0.0), axis=0, keepdims=True
    )
    heat, salt, speed = sides
    line = jnp.broadcast_to(line, (levels, LANES))
    for i, value in enumerate((heat, salt, speed)):
        side_ref[i * K : (i + 1) * K, :] = value
    side_ref[3 * K :, :] = line[:8]
    to_east = jnp.where(place < 2, heat, roll(salt, 2)), jnp.where(place == 2, roll(speed, 1), line)
    to_west = jnp.where(place < 2, roll(salt, -2), heat), line
    for i, (e, w) in enumerate(zip(to_east, to_west)):
        core_ref[i * K : (i + 1) * K, :] = jnp.where(is_odd, w, e)
        chip = jnp.where(is_odd, e, w)
        chip_ref[i * K : (i + 1) * K, :] = chip
        far_ref[4 * K + 8 + i * K : 4 * K + 8 + (i + 1) * K, :] = chip

    def tally(picks):
        return jnp.concatenate(
            [counts[j : j + 1] for j in picks] + [jnp.zeros((8 - len(picks), LANES), F32)], axis=0
        )

    far_ref[4 * K : 4 * K + 8, :] = mirrored(tally(fold))
    first = jnp.zeros((levels, LANES), F32)
    for i, (ref, j) in enumerate((ref, j) for ref in (t_ref, s_ref) for j in fold):
        first = jnp.where(lane == i, roll(strided(ref, j), i), first)
    column_ref[:K, :] = first
    column_ref[K : K + 8, :] = tally(fold)
    if more:
        lat_ref[5 * K :, :] = tally(north)
        more[0][4 * K : 5 * K, :] = jnp.zeros((K, LANES), F32)
        more[0][5 * K :, :] = tally(south)
    else:
        lat_ref[5 * K :, :] = jnp.where(is_top, tally(south), tally(north))
    copies[4].wait()
    lat_ref[4 * K : 5 * K, :] = strided(m_ref, rows - 1)
    for i, j in enumerate((0, rows - 2, rows - 1)):
        own_ref[i * K : (i + 1) * K, :] = strided(m_ref, j)


def relay_kernel(far_ref, _, out_ref):
    K = out_ref.shape[0] - 8
    lane = iota((K, LANES), 1)
    out = far_ref[:K, :]
    for i in (1, 2, 3):
        out = jnp.where(lane == i, roll(far_ref[i * K : (i + 1) * K, :], i), out)
    out_ref[:K, :] = out
    out_ref[K:, :] = far_ref[4 * K : 4 * K + 8, :]


NAMES = ("t", "s", "r", "tz", "sz", "rz")
STATE = 19


def south_kernel(levels, rows, last, early, t_ref, s_ref, c_ref, m_ref, n_ref, *more):
    *more, pt_ref, ps_ref, state_out = more[:-1] if early else more
    at_origin = (lax.axis_index("lat") == 0) & (lax.axis_index("lon") < 2)

    @pl.when(at_origin if early else jnp.logical_not(at_origin))
    def _():
        interior_kernel(levels, rows, 0, last, t_ref, s_ref, c_ref, m_ref, n_ref, pt_ref, ps_ref, state_out)


def interior_kernel(levels, rows, first, last, t_ref, s_ref, c_ref, m_ref, n_ref, *more):
    if first:
        _, _, _, state_in, pt_ref, ps_ref = more
    else:
        pt_ref, ps_ref, state_out = more
    shape = (levels, LANES)
    level = iota(shape, 0)
    last_lane = iota((1, LANES), 1) == LANES - 1
    factors = level_factors(levels)
    zero = jnp.zeros(shape, F32)

    def step(j, carry):
        prev, m1, d2, limited2, base2, wg2, m2, acc2, acc1 = carry
        t, s, c, m = (strided(ref, j) for ref in (t_ref, s_ref, c_ref, m_ref))
        n = n_ref[pl.ds(j, 1), :]
        here = column_row(t, s, n, factors, level)
        east = shifted(here, -1)
        wet = level < jnp.minimum(n, jnp.where(last_lane, 0, east["n"]))
        steps = [face_step(here, east, wet, q) for q in "ts"]
        base, wg, forward = face_base(here, east, c, wet, steps)
        inside = level < n
        acc = []
        for q, d, flux in zip("ts", steps, base):
            limited = minmod(roll(d, 1), d)
            flux = flux + wg * jnp.where(forward, limited, roll(limited, -1))
            acc.append(jnp.where(inside, here[q], 0.0) + roll(flux, 1) - flux)
        wet = level < jnp.minimum(prev["n"], n)
        d1 = [face_step(prev, here, wet, q) for q in "ts"]
        base1, wg1, _ = face_base(prev, here, m1, wet, d1)
        limited1 = [minmod(x, y) for x, y in zip(d2, d1)]
        forward2 = m2 > 0.0
        flux2 = [b + wg2 * jnp.where(forward2, x, y) for b, x, y in zip(base2, limited2, limited1)]
        done = [x - f for x, f in zip(acc2, flux2)]
        acc1 = [x + f for x, f in zip(acc1, flux2)]
        at = (j + rows - 2) % rows
        put(pt_ref, at, done[0])
        put(ps_ref, at, done[1])
        return here, m, d1, limited1, base1, wg1, m1, acc1, acc

    def pack(carry):
        prev, m1, d2, limited2, base2, wg2, m2, acc2, acc1 = carry
        return [prev[name] for name in NAMES] + [m1, *d2, *limited2, *base2, wg2, m2, *acc2, *acc1]

    def unpack(flat, n):
        prev = dict(zip(NAMES, flat), n=n)
        m1, d2, limited2, base2, wg2, m2, acc2, acc1 = (
            flat[6], flat[7:9], flat[9:11], flat[11:13], flat[13], flat[14], flat[15:17], flat[17:19]
        )
        return prev, m1, d2, limited2, base2, wg2, m2, acc2, acc1

    if first:
        carry = unpack([state_in[i] for i in range(STATE)], n_ref[first - 1 : first, :])
    else:
        carry = unpack([zero] * STATE, jnp.zeros((1, LANES), jnp.int32))

    def block(i, carry):
        for u in range(UNROLL):
            carry = step(first + i * UNROLL + u, carry)
        return carry

    carry = lax.fori_loop(0, (last - first) // UNROLL, block, carry)
    if last < rows:
        for i, value in enumerate(pack(carry)):
            state_out[i] = value
        return
    _, _, _, limited2, base2, wg2, m2, acc2, acc1 = carry
    flux2 = [b + wg2 * jnp.where(m2 > 0.0, x, 0.0) for b, x in zip(base2, limited2)]
    for ref, a2, a1, f in zip((pt_ref, ps_ref), acc2, acc1, flux2):
        put(ref, rows - 2, a2 - f)
        put(ref, rows - 1, a1 + f)


def edge_kernel(
    levels, rows, lat_size, lon_size, pt_ref, ps_ref, side_ref, t_ref, s_ref, n_ref, own_ref,
    near_in, core_in, far_in, below_in, above_in, column_in, relay_in, own_column, t_out, s_out,
    t_new, s_new, sems,
):
    shape = (levels, LANES)
    level = iota(shape, 0).astype(F32)
    lane = iota(shape, 1)
    place = lane % 4
    factors = level_factors(levels)
    K = levels
    row_at = lax.axis_index("lat")
    is_top, is_bottom = row_at == lat_size - 1, row_at == 0
    lon_at = lax.axis_index("lon")
    is_odd = lon_at % 2 == 1
    wraps = (lon_at == 0) | (lon_at == lon_size - 1)

    def faces(cells, speeds):
        wets = [level < jnp.minimum(a["n"], b["n"]) for a, b in zip(cells, cells[1:])]
        d = [[face_step(a, b, w, q) for q in "ts"] for a, b, w in zip(cells, cells[1:], wets)]
        limited = [[minmod(x, y) for x, y in zip(d[i], d[i + 1])] for i in (0, 1)]
        base, wg, forward = face_base(cells[1], cells[2], speeds[1], wets[1], d[1])
        flux = [b + wg * jnp.where(forward, x, y) for b, x, y in zip(base, *limited)]
        first = last = None
        if speeds[0] is not None:
            _, wg0 = weights(speeds[0], wets[0])
            first = [wg0 * jnp.where(speeds[0] > 0.0, 0.0, x) for x in limited[0]]
        if speeds[2] is not None:
            _, wg2 = weights(speeds[2], wets[2])
            last = [wg2 * jnp.where(speeds[2] > 0.0, x, 0.0) for x in limited[1]]
        return first, flux, last

    def cell_row(t, s, n):
        return column_row(t, s, n, factors, iota(shape, 0))

    own_t, own_s, own_c = (side_ref[i * K : (i + 1) * K, :] for i in range(3))
    own_n = side_ref[3 * K : 3 * K + 1, :]
    core = core_in[...]
    chip = jnp.where(is_top & ~wraps, near_in[...], far_in[4 * K + 8 :, :])
    west, east = jnp.where(is_odd, core, chip), jnp.where(is_odd, chip, core)
    first_two = place < 2

    def side(t, s, n, speed):
        row = cell_row(t, s, n)
        cells = [row] + [shifted(row, -i) for i in (1, 2, 3)]
        return faces(cells, [roll(speed, -i) for i in range(3)])

    _, west_flux, west_last = side(
        jnp.where(first_two, west[:K], own_t),
        jnp.where(first_two, roll(west[:K], -2), own_s),
        jnp.where(first_two[:1], west[K : K + 1], own_n),
        jnp.where(place == 1, roll(west[K:], -1), own_c),
    )
    east_first, east_flux, _ = side(
        jnp.where(first_two, own_t, east[:K]),
        jnp.where(first_two, own_s, roll(east[:K], 2)),
        jnp.where(first_two[:1], own_n, east[K : K + 1]),
        own_c,
    )
    lon = []
    for fw, lw, fe, le in zip(west_flux, west_last, east_flux, east_first):
        group = jnp.where(
            place == 0,
            -le,
            jnp.where(place == 1, roll(le - fe, 1), jnp.where(place == 2, roll(fw - lw, 2), roll(lw, 3))),
        )
        lon.append(group)

    counts = n_ref[...].astype(F32)

    def own_row(j):
        return cell_row(strided(t_ref, j), strided(s_ref, j), counts[j : j + 1])

    def sent_row(array, which, at_counts):
        t, s = array[which * K : (which + 1) * K], array[(2 + which) * K : (3 + which) * K]
        return cell_row(t, s, array[at_counts + which : at_counts + which + 1])

    below = jnp.where(is_bottom, 0.0, below_in[...])
    cells = [sent_row(below, 0, 5 * K), sent_row(below, 1, 5 * K), own_row(0), own_row(1)]
    _, south_flux, south_last = faces(cells, [None, below[4 * K : 5 * K], own_ref[:K]])

    pivot = (lon_at * 2) % lon_size == 0
    column = jnp.where(is_odd, relay_in[...], jnp.where(pivot, own_column[: K + 8, :], column_in[: K + 8, :]))
    parts = [roll(column[:K], -i) for i in range(4)] + [column[K : K + 8]]
    fold = far_in[: 4 * K + 8, :]
    fold = jnp.where(iota(fold.shape, 1) == 0, jnp.concatenate(parts, axis=0), fold)
    above = above_in[...]
    above = jnp.where(is_top, fold, jnp.concatenate([above[: 4 * K], above[5 * K :]], axis=0))
    cells = [own_row(rows - 2), own_row(rows - 1), sent_row(above, 0, 4 * K), sent_row(above, 1, 4 * K)]
    north_first, north_flux, _ = faces(cells, [own_ref[K : 2 * K], own_ref[2 * K :], None])

    slot = iota((8, LANES), 0)
    last = LANES // 4 - 1
    own_lanes = [last - iota((8, LANES), 1) // 4 == slot + 8 * block for block in range(rows // 8)]
    reverse = 4 * (last - lane // 4) + place
    copies = []
    for q, (p_ref, new_ref, out_ref) in enumerate(((pt_ref, t_new, t_out), (ps_ref, s_new, s_out))):
        sides = jnp.take_along_axis(lon[q], reverse, axis=1)
        for k in range(levels):
            line = jnp.broadcast_to(sides[k : k + 1], (8, LANES))
            for block, mine in enumerate(own_lanes):
                moved = pltpu.roll(jnp.where(mine, line, 0.0), 32 * block + 2, 1, stride=4, stride_axis=0)
                at = slice(8 * block, 8 * block + 8)
                new_ref[k, at, :] = p_ref[k, at, :] + moved
        extra = {
            0: south_flux[q] - south_last[q],
            1: south_last[q],
            rows - 2: -north_first[q],
            rows - 1: north_first[q] - north_flux[q],
        }
        for j, value in extra.items():
            put(new_ref, j, strided(new_ref, j) + value)
        copies.append(pltpu.make_async_copy(new_ref.at[:, :rows], out_ref, sems.at[q]))
        copies[q].start()
    for copy in copies:
        copy.wait()


def body(nlat, nlon, t, s, c, m, n):
    levels, rows, _ = t.shape
    vmem, hbm = pl.BlockSpec(memory_space=pltpu.VMEM), pl.BlockSpec(memory_space=pltpu.HBM)
    f = functools.partial
    out = lambda *shape: jax.ShapeDtypeStruct(shape, F32)
    K = levels
    params = pltpu.CompilerParams(vmem_limit_bytes=VMEM)
    swap = nlat == 2
    field, lat_shape = out(rows, K, LANES), out(5 * K + 8, LANES)
    room = out(levels, rows + SPARE, LANES)
    shapes = [room] * 4 + [jax.ShapeDtypeStruct(n.shape, n.dtype)]
    shapes += [out(3 * K + 8, LANES), out(2 * K, LANES), out(2 * K, LANES), lat_shape, out(6 * K + 8, LANES)]
    shapes += [out(2 * K + 8, LANES), out(3 * K, LANES)]
    shapes += [] if swap else [lat_shape]
    t_v, s_v, c_v, m_v, n_v, side, core, chip, lat, far, column, own, *more = pl.pallas_call(
        f(pack_kernel, levels, rows, nlat),
        out_shape=tuple(shapes),
        in_specs=[hbm] * 5,
        out_specs=(vmem,) * len(shapes),
        scratch_shapes=[pltpu.SemaphoreType.DMA((5,))],
        compiler_params=params,
        name="pack",
    )(*[pltpu.with_memory_space_constraint(x, pltpu.HBM) for x in (t, s, c, m, n)])

    top = nlat - 1

    def exchange(array, top_to, others_to, helper=lambda i: i):
        to = {(j, i): (j, others_to(i)) for j in range(top) for i in range(nlon)}
        for i in range(nlon):
            partner, via = top_to(i), helper(i)
            if partner is not None:
                to[top, i] = (top, partner)
            elif to.get((0, via)) == (0, via ^ 1) and to.get((0, via ^ 1)) == (0, via):
                to[top, i], to[0, via], to[0, via ^ 1] = (0, via), (0, via ^ 1), (top, i)
            else:
                to[top, i] = (top, i)
        pairs = [(i * nlat + j, to[j, i][1] * nlat + to[j, i][0]) for i in range(nlon) for j in range(nlat)]
        return lax.ppermute(array, ("lon", "lat"), pairs)

    def chips(i):
        return (i + (1 if i % 2 else -1)) % nlon

    columns = {i: i ^ 1 if 2 * i % nlon == 0 else nlon - i for i in range(0, nlon, 2)}
    lone = [i for i in range(1, nlon, 2) if columns[i - 1] != i]
    columns |= {i: i - 1 for i in range(1, nlon, 2) if i not in lone}
    for part in ([i for i in lone if 2 * i < nlon], [i for i in lone if 2 * i > nlon]):
        columns |= dict(zip(part, part[1:] + part[:1]))

    middle = HEAD
    fields = (t_v, s_v, c_v, m_v, n_v)
    south_out = (room, room, out(STATE, K, LANES))
    cost = pl.CostEstimate(flops=20_000_000, bytes_accessed=1_000_000, transcendentals=0)
    pt, ps, state, far = pl.pallas_call(
        f(south_kernel, levels, rows, middle, True),
        out_shape=south_out + (out(*far.shape),),
        in_specs=[vmem] * 6,
        out_specs=(vmem,) * 4,
        input_output_aliases={5: 3},
        cost_estimate=cost,
        compiler_params=params,
        name="south_at_origin",
    )(*fields, far)

    ring, rung = range(nlon), range(nlat)
    far_in = exchange(far, lambda i: nlon - 1 - i, chips)
    below_in = above_in = lax.ppermute(lat, "lat", [(i, (i + 1) % nlat) for i in rung])
    if not swap:
        above_in = lax.ppermute(more[0], "lat", [(i, (i - 1) % nlat) for i in rung])
    near_in = exchange(
        chip,
        lambda i: chips(i) if 0 < i < nlon - 1 else None,
        lambda i: i ^ 1,
        lambda i: i + nlon // 4 if i == 0 else i - nlon // 4,
    )
    core_in = lax.ppermute(core, "lon", [(i, i ^ 1) for i in ring])
    column_in = exchange(column, columns.get, lambda i: i ^ 1)

    pt, ps, state = pl.pallas_call(
        f(south_kernel, levels, rows, middle, False),
        out_shape=south_out,
        in_specs=[vmem] * 8,
        out_specs=(vmem,) * 3,
        input_output_aliases={5: 0, 6: 1, 7: 2},
        cost_estimate=cost,
        compiler_params=params,
        name="south_elsewhere",
    )(*fields, pt, ps, state)
    relay = pl.pallas_call(
        relay_kernel,
        out_shape=out(K + 8, LANES),
        in_specs=[vmem] * 2,
        out_specs=vmem,
        compiler_params=params,
        name="relay",
    )(far_in, state)
    relay_in = lax.ppermute(relay, "lon", [(i, i ^ 1) for i in ring])

    pt, ps = pl.pallas_call(
        f(interior_kernel, levels, rows, middle, rows),
        out_shape=(room, room),
        in_specs=[vmem] * 9,
        out_specs=(vmem,) * 2,
        input_output_aliases={5: 0, 6: 1},
        cost_estimate=pl.CostEstimate(flops=20_000_000, bytes_accessed=1_000_000, transcendentals=0),
        compiler_params=params,
        name="interior_north",
    )(*fields, pt, ps, relay, state)

    return pl.pallas_call(
        f(edge_kernel, levels, rows, nlat, nlon),
        out_shape=(out(*t.shape),) * 2,
        in_specs=[vmem] * 15,
        out_specs=(hbm,) * 2,
        scratch_shapes=[pltpu.VMEM(room.shape, F32)] * 2 + [pltpu.SemaphoreType.DMA((2,))],
        compiler_params=params,
        name="edge",
    )(pt, ps, side, t_v, s_v, n_v, own, near_in, core_in, far_in, below_in, above_in, column_in, relay_in, column)


def solution(mesh):
    spec = P(None, "lat", "lon")
    return jax.shard_map(
        functools.partial(body, mesh.shape["lat"], mesh.shape["lon"]),
        mesh=mesh,
        in_specs=(spec,) * 4 + (P("lat", "lon"),),
        out_specs=(spec,) * 2,
        check_vma=False,
    )
```

```python
import functools

import jax
import jax.numpy as jnp
from jax import lax
from jax.experimental import pallas as pl
from jax.experimental.pallas import tpu as pltpu
from jax.sharding import PartitionSpec as P

heat_swelling_alpha = 0.1655
coef_beta = 0.76554
cabbeling_parameter = 0.05952
lambda_salt = 0.00054914
thermobaric_parameter = 0.0001497
press_salt = 1.109e-05
cross_coupling_contribution = 0.0024341
total_depth = 5000.0
kappa_iso = 0.1
strat_min = 0.1

LANES = 128
VMEM = 8 * 1024 * 1024
UNROLL = 8
HEAD = 16
SPARE = 8
F32 = jnp.float32


def iota(shape, axis):
    return lax.broadcasted_iota(jnp.int32, shape, axis)


def roll(array, shift, axis=1):
    size = array.shape[axis]
    return pltpu.roll(array, shift % size, axis)


def minmod(x, y):
    return jnp.maximum(jnp.minimum(x, jnp.maximum(y, 0.0)), jnp.minimum(y, 0.0))


def level_factors(levels):
    depth = total_depth * (iota((levels, LANES), 0).astype(F32) + 0.5) / levels
    heat = -heat_swelling_alpha * (1.0 + thermobaric_parameter * depth)
    salt = coef_beta * (1.0 - press_salt * depth)
    return heat, salt


def density(t, s, factors):
    heat, salt = factors
    return t * (
        heat
        - (0.5 * heat_swelling_alpha * cabbeling_parameter) * t
        - cross_coupling_contribution * s
    ) + s * (salt - (0.5 * coef_beta * lambda_salt) * s)


def vertical(q, level):
    levels = q.shape[0]
    step = roll(q, -1, 0) - q
    below = roll(step, 1, 0)
    return jnp.where(level == levels - 1, below, step) + jnp.where(level == 0, step, below)


def column_row(t, s, n, factors, level):
    r = density(t, s, factors)
    return {
        "t": t,
        "s": s,
        "r": r,
        "tz": vertical(t, level),
        "sz": vertical(s, level),
        "rz": vertical(r, level),
        "n": n,
    }


def shifted(row, by):
    return {name: roll(value, by) for name, value in row.items()}


def weights(c, wet):
    size = jnp.abs(c)
    return jnp.where(wet, c, 0.0), jnp.where(wet, 0.5 * (size - c * c), 0.0)


def face_step(a, b, wet, name):
    return jnp.where(wet, b[name] - a[name], 0.0)


def face_base(a, b, c, wet, steps):
    wc, wg = weights(c, wet)
    steep = (a["r"] - b["r"]) / jnp.maximum(a["rz"] + b["rz"], 4.0 * strat_min)
    tilt = jnp.where(wet, jnp.clip(steep, -0.25, 0.25), 0.0) * (-kappa_iso)
    forward = c > 0.0
    base = [
        wc * jnp.where(forward, a[q], b[q]) - kappa_iso * d + tilt * (a[q + "z"] + b[q + "z"])
        for q, d in zip("ts", steps)
    ]
    return base, wg, forward


def strided(ref, row):
    levels, rows, _ = ref.shape
    return ref.reshape(levels * rows, LANES)[pl.ds(row, levels, stride=rows), :]


def put(ref, row, value):
    levels, rows, _ = ref.shape
    ref.reshape(levels * rows, LANES)[pl.ds(row, levels, stride=rows), :] = value


def pack_kernel(
    levels, rows, lat_size, t_hbm, s_hbm, c_hbm, m_hbm, n_hbm,
    t_ref, s_ref, c_ref, m_ref, n_ref, side_ref, core_ref, chip_ref, lat_ref, far_ref, column_ref, own_ref, *more,
):
    *more, sems = more
    K = levels
    pairs = ((t_hbm, t_ref), (s_hbm, s_ref), (c_hbm, c_ref), (n_hbm, n_ref), (m_hbm, m_ref))
    pairs = [(src, dst if dst is n_ref else dst.at[:, :rows]) for src, dst in pairs]
    copies = [pltpu.make_async_copy(src, dst, sems.at[i]) for i, (src, dst) in enumerate(pairs)]
    for copy in copies:
        copy.start()
    lane = iota((levels, LANES), 1)
    group = lane // 4

    slot = iota((8, LANES), 0)
    own = [iota((8, LANES), 1) // 4 == slot + 8 * block for block in range(rows // 8)]

    def gather(ref):
        tiles = []
        for base in range(0, K, 8):
            out = jnp.zeros((8, LANES), F32)
            for k in range(8):
                spread = jnp.zeros((8, LANES), F32)
                for block, mine in enumerate(own):
                    eight = ref[base + k, 8 * block : 8 * block + 8, :]
                    moved = pltpu.roll(eight, 32 * block + 2, 1, stride=4, stride_axis=0)
                    spread = jnp.where(mine, moved, spread)
                for by in (4, 2, 1):
                    spread = spread + roll(spread, by, 0)
                out = jnp.where(slot == k, spread, out)
            tiles.append(out)
        return jnp.concatenate(tiles, axis=0)

    def mirrored(x):
        index = (LANES - iota(x.shape, 1)) % LANES
        return jnp.take_along_axis(x, index, axis=1)

    def tracer_rows(out_ref, tracer, ref, picks, change=lambda x: x):
        for i, j in enumerate(picks):
            at = (2 * tracer + i) * K
            out_ref[at : at + K, :] = change(strided(ref, j))

    south, north, fold = (0, 1), (rows - 2, rows - 1), (rows - 2, rows - 3)
    is_top = lax.axis_index("lat") == lat_size - 1
    is_odd = lax.axis_index("lon") % 2 == 1
    place = iota((levels, LANES), 1) % 4
    sides = []
    for tracer, ref in enumerate((t_ref, s_ref)):
        copies[tracer].wait()
        sides.append(gather(ref))
        tracer_rows(far_ref, tracer, ref, fold, mirrored)
        if more:
            tracer_rows(lat_ref, tracer, ref, north)
            tracer_rows(more[0], tracer, ref, south)
        else:
            for i in range(2):
                at = (2 * tracer + i) * K
                lat_ref[at : at + K, :] = jnp.where(is_top, strided(ref, south[i]), strided(ref, north[i]))

    copies[2].wait()
    sides.append(gather(c_ref))
    copies[3].wait()
    counts = n_ref[...].astype(F32)
    moved = jnp.concatenate([roll(counts[j : j + 1], 4 * j + 2) for j in range(rows)], axis=0)
    line = jnp.sum(
        jnp.where(iota((rows, LANES), 1) // 4 == iota((rows, LANES), 0), moved, 0.0), axis=0, keepdims=True
    )
    heat, salt, speed = sides
    line = jnp.broadcast_to(line, (levels, LANES))
    for i, value in enumerate((heat, salt, speed)):
        side_ref[i * K : (i + 1) * K, :] = value
    side_ref[3 * K :, :] = line[:8]
    to_east = jnp.where(place < 2, heat, roll(salt, 2)), jnp.where(place == 2, roll(speed, 1), line)
    to_west = jnp.where(place < 2, roll(salt, -2), heat), line
    for i, (e, w) in enumerate(zip(to_east, to_west)):
        core_ref[i * K : (i + 1) * K, :] = jnp.where(is_odd, w, e)
        chip = jnp.where(is_odd, e, w)
        chip_ref[i * K : (i + 1) * K, :] = chip
        far_ref[4 * K + 8 + i * K : 4 * K + 8 + (i + 1) * K, :] = chip

    def tally(picks):
        return jnp.concatenate(
            [counts[j : j + 1] for j in picks] + [jnp.zeros((8 - len(picks), LANES), F32)], axis=0
        )

    far_ref[4 * K : 4 * K + 8, :] = mirrored(tally(fold))
    first = jnp.zeros((levels, LANES), F32)
    for i, (ref, j) in enumerate((ref, j) for ref in (t_ref, s_ref) for j in fold):
        first = jnp.where(lane == i, roll(strided(ref, j), i), first)
    column_ref[:K, :] = first
    column_ref[K : K + 8, :] = tally(fold)
    if more:
        lat_ref[5 * K :, :] = tally(north)
        more[0][4 * K : 5 * K, :] = jnp.zeros((K, LANES), F32)
        more[0][5 * K :, :] = tally(south)
    else:
        lat_ref[5 * K :, :] = jnp.where(is_top, tally(south), tally(north))
    copies[4].wait()
    lat_ref[4 * K : 5 * K, :] = strided(m_ref, rows - 1)
    for i, j in enumerate((0, rows - 2, rows - 1)):
        own_ref[i * K : (i + 1) * K, :] = strided(m_ref, j)


def relay_kernel(far_ref, _, out_ref):
    K = out_ref.shape[0] - 8
    lane = iota((K, LANES), 1)
    out = far_ref[:K, :]
    for i in (1, 2, 3):
        out = jnp.where(lane == i, roll(far_ref[i * K : (i + 1) * K, :], i), out)
    out_ref[:K, :] = out
    out_ref[K:, :] = far_ref[4 * K : 4 * K + 8, :]


NAMES = ("t", "s", "r", "tz", "sz", "rz")
STATE = 19


def south_kernel(levels, rows, last, early, t_ref, s_ref, c_ref, m_ref, n_ref, *more):
    *more, pt_ref, ps_ref, state_out = more[:-1] if early else more
    at_origin = (lax.axis_index("lat") == 0) & (lax.axis_index("lon") < 2)

    @pl.when(at_origin if early else jnp.logical_not(at_origin))
    def _():
        interior_kernel(levels, rows, 0, last, t_ref, s_ref, c_ref, m_ref, n_ref, pt_ref, ps_ref, state_out)


def interior_kernel(levels, rows, first, last, t_ref, s_ref, c_ref, m_ref, n_ref, *more):
    if first:
        _, _, _, state_in, pt_ref, ps_ref = more
    else:
        pt_ref, ps_ref, state_out = more
    shape = (levels, LANES)
    level = iota(shape, 0)
    last_lane = iota((1, LANES), 1) == LANES - 1
    factors = level_factors(levels)
    zero = jnp.zeros(shape, F32)

    def step(j, carry):
        prev, m1, d2, limited2, base2, wg2, m2, acc2, acc1 = carry
        t, s, c, m = (strided(ref, j) for ref in (t_ref, s_ref, c_ref, m_ref))
        n = n_ref[pl.ds(j, 1), :]
        here = column_row(t, s, n, factors, level)
        east = shifted(here, -1)
        wet = level < jnp.minimum(n, jnp.where(last_lane, 0, east["n"]))
        steps = [face_step(here, east, wet, q) for q in "ts"]
        base, wg, forward = face_base(here, east, c, wet, steps)
        inside = level < n
        acc = []
        for q, d, flux in zip("ts", steps, base):
            limited = minmod(roll(d, 1), d)
            flux = flux + wg * jnp.where(forward, limited, roll(limited, -1))
            acc.append(jnp.where(inside, here[q], 0.0) + roll(flux, 1) - flux)
        wet = level < jnp.minimum(prev["n"], n)
        d1 = [face_step(prev, here, wet, q) for q in "ts"]
        base1, wg1, _ = face_base(prev, here, m1, wet, d1)
        limited1 = [minmod(x, y) for x, y in zip(d2, d1)]
        forward2 = m2 > 0.0
        flux2 = [b + wg2 * jnp.where(forward2, x, y) for b, x, y in zip(base2, limited2, limited1)]
        done = [x - f for x, f in zip(acc2, flux2)]
        acc1 = [x + f for x, f in zip(acc1, flux2)]
        at = (j + rows - 2) % rows
        put(pt_ref, at, done[0])
        put(ps_ref, at, done[1])
        return here, m, d1, limited1, base1, wg1, m1, acc1, acc

    def pack(carry):
        prev, m1, d2, limited2, base2, wg2, m2, acc2, acc1 = carry
        return [prev[name] for name in NAMES] + [m1, *d2, *limited2, *base2, wg2, m2, *acc2, *acc1]

    def unpack(flat, n):
        prev = dict(zip(NAMES, flat), n=n)
        m1, d2, limited2, base2, wg2, m2, acc2, acc1 = (
            flat[6], flat[7:9], flat[9:11], flat[11:13], flat[13], flat[14], flat[15:17], flat[17:19]
        )
        return prev, m1, d2, limited2, base2, wg2, m2, acc2, acc1

    if first:
        carry = unpack([state_in[i] for i in range(STATE)], n_ref[first - 1 : first, :])
    else:
        carry = unpack([zero] * STATE, jnp.zeros((1, LANES), jnp.int32))

    def block(i, carry):
        for u in range(UNROLL):
            carry = step(first + i * UNROLL + u, carry)
        return carry

    carry = lax.fori_loop(0, (last - first) // UNROLL, block, carry)
    if last < rows:
        for i, value in enumerate(pack(carry)):
            state_out[i] = value
        return
    _, _, _, limited2, base2, wg2, m2, acc2, acc1 = carry
    flux2 = [b + wg2 * jnp.where(m2 > 0.0, x, 0.0) for b, x in zip(base2, limited2)]
    for ref, a2, a1, f in zip((pt_ref, ps_ref), acc2, acc1, flux2):
        put(ref, rows - 2, a2 - f)
        put(ref, rows - 1, a1 + f)


def edge_faces(cells, speeds):
    level = iota(cells[0]["t"].shape, 0).astype(F32)
    wets = [level < jnp.minimum(a["n"], b["n"]) for a, b in zip(cells, cells[1:])]
    d = [[face_step(a, b, w, q) for q in "ts"] for a, b, w in zip(cells, cells[1:], wets)]
    limited = [[minmod(x, y) for x, y in zip(d[i], d[i + 1])] for i in (0, 1)]
    base, wg, forward = face_base(cells[1], cells[2], speeds[1], wets[1], d[1])
    flux = [b + wg * jnp.where(forward, x, y) for b, x, y in zip(base, *limited)]
    first = last = None
    if speeds[0] is not None:
        _, wg0 = weights(speeds[0], wets[0])
        first = [wg0 * jnp.where(speeds[0] > 0.0, 0.0, x) for x in limited[0]]
    if speeds[2] is not None:
        _, wg2 = weights(speeds[2], wets[2])
        last = [wg2 * jnp.where(speeds[2] > 0.0, x, 0.0) for x in limited[1]]
    return first, flux, last


def longitude_kernel(
    levels, rows, lat_size, lon_size, pt_ref, ps_ref, side_ref, near_in, core_in, far_in, t_new, s_new
):
    shape = (levels, LANES)
    lane = iota(shape, 1)
    place = lane % 4
    factors = level_factors(levels)
    K = levels
    is_top = lax.axis_index("lat") == lat_size - 1
    lon_at = lax.axis_index("lon")
    is_odd = lon_at % 2 == 1
    wraps = (lon_at == 0) | (lon_at == lon_size - 1)

    def cell_row(t, s, n):
        return column_row(t, s, n, factors, iota(shape, 0))

    own_t, own_s, own_c = (side_ref[i * K : (i + 1) * K, :] for i in range(3))
    own_n = side_ref[3 * K : 3 * K + 1, :]
    core = core_in[...]
    chip = jnp.where(is_top & ~wraps, near_in[...], far_in[4 * K + 8 :, :])
    west, east = jnp.where(is_odd, core, chip), jnp.where(is_odd, chip, core)
    first_two = place < 2

    def side(t, s, n, speed):
        row = cell_row(t, s, n)
        cells = [row] + [shifted(row, -i) for i in (1, 2, 3)]
        return edge_faces(cells, [roll(speed, -i) for i in range(3)])

    _, west_flux, west_last = side(
        jnp.where(first_two, west[:K], own_t),
        jnp.where(first_two, roll(west[:K], -2), own_s),
        jnp.where(first_two[:1], west[K : K + 1], own_n),
        jnp.where(place == 1, roll(west[K:], -1), own_c),
    )
    east_first, east_flux, _ = side(
        jnp.where(first_two, own_t, east[:K]),
        jnp.where(first_two, own_s, roll(east[:K], 2)),
        jnp.where(first_two[:1], own_n, east[K : K + 1]),
        own_c,
    )
    lon = []
    for fw, lw, fe, le in zip(west_flux, west_last, east_flux, east_first):
        group = jnp.where(
            place == 0,
            -le,
            jnp.where(place == 1, roll(le - fe, 1), jnp.where(place == 2, roll(fw - lw, 2), roll(lw, 3))),
        )
        lon.append(group)

    slot = iota((8, LANES), 0)
    last = LANES // 4 - 1
    own_lanes = [last - iota((8, LANES), 1) // 4 == slot + 8 * block for block in range(rows // 8)]
    reverse = 4 * (last - lane // 4) + place
    for q, (p_ref, new_ref) in enumerate(((pt_ref, t_new), (ps_ref, s_new))):
        sides = jnp.take_along_axis(lon[q], reverse, axis=1)
        for k in range(levels):
            line = jnp.broadcast_to(sides[k : k + 1], (8, LANES))
            for block, mine in enumerate(own_lanes):
                moved = pltpu.roll(jnp.where(mine, line, 0.0), 32 * block + 2, 1, stride=4, stride_axis=0)
                at = slice(8 * block, 8 * block + 8)
                new_ref[k, at, :] = p_ref[k, at, :] + moved


def latitude_kernel(
    levels, rows, lat_size, lon_size, t_new, s_new, t_ref, s_ref, n_ref, own_ref,
    far_in, below_in, above_in, column_in, relay_in, own_column, t_out, s_out, ends_ref, sems,
):
    shape = (levels, LANES)
    factors = level_factors(levels)
    K = levels
    row_at = lax.axis_index("lat")
    is_top, is_bottom = row_at == lat_size - 1, row_at == 0
    lon_at = lax.axis_index("lon")
    is_odd = lon_at % 2 == 1
    middle = pl.ds(8, rows - 16)
    copies = [
        pltpu.make_async_copy(new_ref.at[:, middle], out_ref.at[:, middle], sems.at[q])
        for q, (new_ref, out_ref) in enumerate(((t_new, t_out), (s_new, s_out)))
    ]
    for copy in copies:
        copy.start()

    def cell_row(t, s, n):
        return column_row(t, s, n, factors, iota(shape, 0))

    counts = n_ref[...].astype(F32)

    def own_row(j):
        return cell_row(strided(t_ref, j), strided(s_ref, j), counts[j : j + 1])

    def sent_row(array, which, at_counts):
        t, s = array[which * K : (which + 1) * K], array[(2 + which) * K : (3 + which) * K]
        return cell_row(t, s, array[at_counts + which : at_counts + which + 1])

    below = jnp.where(is_bottom, 0.0, below_in[...])
    cells = [sent_row(below, 0, 5 * K), sent_row(below, 1, 5 * K), own_row(0), own_row(1)]
    _, south_flux, south_last = edge_faces(cells, [None, below[4 * K : 5 * K], own_ref[:K]])

    pivot = (lon_at * 2) % lon_size == 0
    column = jnp.where(is_odd, relay_in[...], jnp.where(pivot, own_column[: K + 8, :], column_in[: K + 8, :]))
    parts = [roll(column[:K], -i) for i in range(4)] + [column[K : K + 8]]
    fold = far_in[: 4 * K + 8, :]
    fold = jnp.where(iota(fold.shape, 1) == 0, jnp.concatenate(parts, axis=0), fold)
    above = above_in[...]
    above = jnp.where(is_top, fold, jnp.concatenate([above[: 4 * K], above[5 * K :]], axis=0))
    cells = [own_row(rows - 2), own_row(rows - 1), sent_row(above, 0, 4 * K), sent_row(above, 1, 4 * K)]
    north_first, north_flux, _ = edge_faces(cells, [own_ref[K : 2 * K], own_ref[2 * K :], None])

    for q, (new_ref, out_ref) in enumerate(((t_new, t_out), (s_new, s_out))):
        ends = ends_ref.at[q]
        ends[:, :8, :] = new_ref[:, :8, :]
        ends[:, 8:16, :] = new_ref[:, rows - 8 : rows, :]
        extra = {
            0: south_flux[q] - south_last[q],
            1: south_last[q],
            14: -north_first[q],
            15: north_first[q] - north_flux[q],
        }
        for j, value in extra.items():
            put(ends, j, strided(ends, j) + value)
        for i, at in enumerate((0, rows - 8)):
            copy = pltpu.make_async_copy(
                ends.at[:, pl.ds(8 * i, 8)], out_ref.at[:, pl.ds(at, 8)], sems.at[2 + 2 * q + i]
            )
            copy.start()
            copies.append(copy)
    for copy in copies:
        copy.wait()


def body(nlat, nlon, t, s, c, m, n):
    levels, rows, _ = t.shape
    vmem, hbm = pl.BlockSpec(memory_space=pltpu.VMEM), pl.BlockSpec(memory_space=pltpu.HBM)
    f = functools.partial
    out = lambda *shape: jax.ShapeDtypeStruct(shape, F32)
    K = levels
    params = pltpu.CompilerParams(vmem_limit_bytes=VMEM)
    swap = nlat == 2
    field, lat_shape = out(rows, K, LANES), out(5 * K + 8, LANES)
    room = out(levels, rows + SPARE, LANES)
    shapes = [room] * 4 + [jax.ShapeDtypeStruct(n.shape, n.dtype)]
    shapes += [out(3 * K + 8, LANES), out(2 * K, LANES), out(2 * K, LANES), lat_shape, out(6 * K + 8, LANES)]
    shapes += [out(2 * K + 8, LANES), out(3 * K, LANES)]
    shapes += [] if swap else [lat_shape]
    t_v, s_v, c_v, m_v, n_v, side, core, chip, lat, far, column, own, *more = pl.pallas_call(
        f(pack_kernel, levels, rows, nlat),
        out_shape=tuple(shapes),
        in_specs=[hbm] * 5,
        out_specs=(vmem,) * len(shapes),
        scratch_shapes=[pltpu.SemaphoreType.DMA((5,))],
        compiler_params=params,
        name="pack",
    )(*[pltpu.with_memory_space_constraint(x, pltpu.HBM) for x in (t, s, c, m, n)])

    top = nlat - 1

    def exchange(array, top_to, others_to, helper=lambda i: i):
        to = {(j, i): (j, others_to(i)) for j in range(top) for i in range(nlon)}
        for i in range(nlon):
            partner, via = top_to(i), helper(i)
            if partner is not None:
                to[top, i] = (top, partner)
            elif to.get((0, via)) == (0, via ^ 1) and to.get((0, via ^ 1)) == (0, via):
                to[top, i], to[0, via], to[0, via ^ 1] = (0, via), (0, via ^ 1), (top, i)
            else:
                to[top, i] = (top, i)
        pairs = [(i * nlat + j, to[j, i][1] * nlat + to[j, i][0]) for i in range(nlon) for j in range(nlat)]
        return lax.ppermute(array, ("lon", "lat"), pairs)

    def chips(i):
        return (i + (1 if i % 2 else -1)) % nlon

    columns = {i: i ^ 1 if 2 * i % nlon == 0 else nlon - i for i in range(0, nlon, 2)}
    lone = [i for i in range(1, nlon, 2) if columns[i - 1] != i]
    columns |= {i: i - 1 for i in range(1, nlon, 2) if i not in lone}
    for part in ([i for i in lone if 2 * i < nlon], [i for i in lone if 2 * i > nlon]):
        columns |= dict(zip(part, part[1:] + part[:1]))

    middle = HEAD
    fields = (t_v, s_v, c_v, m_v, n_v)
    south_out = (room, room, out(STATE, K, LANES))
    cost = pl.CostEstimate(flops=20_000_000, bytes_accessed=1_000_000, transcendentals=0)
    pt, ps, state, far = pl.pallas_call(
        f(south_kernel, levels, rows, middle, True),
        out_shape=south_out + (out(*far.shape),),
        in_specs=[vmem] * 6,
        out_specs=(vmem,) * 4,
        input_output_aliases={5: 3},
        cost_estimate=cost,
        compiler_params=params,
        name="south_at_origin",
    )(*fields, far)

    ring, rung = range(nlon), range(nlat)
    far_in = exchange(far, lambda i: nlon - 1 - i, chips)
    below_in = above_in = lax.ppermute(lat, "lat", [(i, (i + 1) % nlat) for i in rung])
    if not swap:
        above_in = lax.ppermute(more[0], "lat", [(i, (i - 1) % nlat) for i in rung])
    near_in = exchange(
        chip,
        lambda i: chips(i) if 0 < i < nlon - 1 else None,
        lambda i: i ^ 1,
        lambda i: i + nlon // 4 if i == 0 else i - nlon // 4,
    )
    core_in = lax.ppermute(core, "lon", [(i, i ^ 1) for i in ring])
    column_in = exchange(column, columns.get, lambda i: i ^ 1)

    pt, ps, state = pl.pallas_call(
        f(south_kernel, levels, rows, middle, False),
        out_shape=south_out,
        in_specs=[vmem] * 8,
        out_specs=(vmem,) * 3,
        input_output_aliases={5: 0, 6: 1, 7: 2},
        cost_estimate=cost,
        compiler_params=params,
        name="south_elsewhere",
    )(*fields, pt, ps, state)
    relay = pl.pallas_call(
        relay_kernel,
        out_shape=out(K + 8, LANES),
        in_specs=[vmem] * 2,
        out_specs=vmem,
        compiler_params=params,
        name="relay",
    )(far_in, state)
    relay_in = lax.ppermute(relay, "lon", [(i, i ^ 1) for i in ring])

    pt, ps = pl.pallas_call(
        f(interior_kernel, levels, rows, middle, rows),
        out_shape=(room, room),
        in_specs=[vmem] * 9,
        out_specs=(vmem,) * 2,
        input_output_aliases={5: 0, 6: 1},
        cost_estimate=pl.CostEstimate(flops=20_000_000, bytes_accessed=1_000_000, transcendentals=0),
        compiler_params=params,
        name="interior_north",
    )(*fields, pt, ps, relay, state)

    t_new, s_new = pl.pallas_call(
        f(longitude_kernel, levels, rows, nlat, nlon),
        out_shape=(room, room),
        in_specs=[vmem] * 6,
        out_specs=(vmem,) * 2,
        input_output_aliases={0: 0, 1: 1},
        cost_estimate=pl.CostEstimate(flops=5_000_000, bytes_accessed=1_000_000, transcendentals=0),
        compiler_params=params,
        name="longitude_edges",
    )(pt, ps, side, near_in, core_in, far_in)

    return pl.pallas_call(
        f(latitude_kernel, levels, rows, nlat, nlon),
        out_shape=(out(*t.shape),) * 2,
        in_specs=[vmem] * 12,
        out_specs=(hbm,) * 2,
        scratch_shapes=[pltpu.VMEM((2, K, 24, LANES), F32), pltpu.SemaphoreType.DMA((6,))],
        compiler_params=params,
        name="latitude_edges",
    )(t_new, s_new, t_v, s_v, n_v, own, far_in, below_in, above_in, column_in, relay_in, column)


def solution(mesh):
    spec = P(None, "lat", "lon")
    return jax.shard_map(
        functools.partial(body, mesh.shape["lat"], mesh.shape["lon"]),
        mesh=mesh,
        in_specs=(spec,) * 4 + (P("lat", "lon"),),
        out_specs=(spec,) * 2,
        check_vma=False,
    )
```

```python
import functools

import jax
import jax.numpy as jnp
from jax import lax
from jax.experimental import pallas as pl
from jax.experimental.pallas import tpu as pltpu
from jax.sharding import PartitionSpec as P

heat_swelling_alpha = 0.1655
coef_beta = 0.76554
cabbeling_parameter = 0.05952
lambda_salt = 0.00054914
thermobaric_parameter = 0.0001497
press_salt = 1.109e-05
cross_coupling_contribution = 0.0024341
total_depth = 5000.0
kappa_iso = 0.1
strat_min = 0.1

LANES = 128
VMEM = 8 * 1024 * 1024
UNROLL = 8
HEAD = 24
SPARE = 8
F32 = jnp.float32


def iota(shape, axis):
    return lax.broadcasted_iota(jnp.int32, shape, axis)


def roll(array, shift, axis=1):
    size = array.shape[axis]
    return pltpu.roll(array, shift % size, axis)


def minmod(x, y):
    return jnp.maximum(jnp.minimum(x, jnp.maximum(y, 0.0)), jnp.minimum(y, 0.0))


def level_factors(levels):
    depth = total_depth * (iota((levels, LANES), 0).astype(F32) + 0.5) / levels
    heat = -heat_swelling_alpha * (1.0 + thermobaric_parameter * depth)
    salt = coef_beta * (1.0 - press_salt * depth)
    return heat, salt


def density(t, s, factors):
    heat, salt = factors
    return t * (
        heat
        - (0.5 * heat_swelling_alpha * cabbeling_parameter) * t
        - cross_coupling_contribution * s
    ) + s * (salt - (0.5 * coef_beta * lambda_salt) * s)


def vertical(q, level):
    levels = q.shape[0]
    step = roll(q, -1, 0) - q
    below = roll(step, 1, 0)
    return jnp.where(level == levels - 1, below, step) + jnp.where(level == 0, step, below)


def column_row(t, s, n, factors, level):
    r = density(t, s, factors)
    return {
        "t": t,
        "s": s,
        "r": r,
        "tz": vertical(t, level),
        "sz": vertical(s, level),
        "rz": vertical(r, level),
        "n": n,
    }


def shifted(row, by):
    return {name: roll(value, by) for name, value in row.items()}


def weights(c, wet):
    size = jnp.abs(c)
    return jnp.where(wet, c, 0.0), jnp.where(wet, 0.5 * (size - c * c), 0.0)


def face_step(a, b, wet, name):
    return jnp.where(wet, b[name] - a[name], 0.0)


def face_base(a, b, c, wet, steps):
    wc, wg = weights(c, wet)
    steep = (a["r"] - b["r"]) / jnp.maximum(a["rz"] + b["rz"], 4.0 * strat_min)
    tilt = jnp.where(wet, jnp.clip(steep, -0.25, 0.25), 0.0) * (-kappa_iso)
    forward = c > 0.0
    base = [
        wc * jnp.where(forward, a[q], b[q]) - kappa_iso * d + tilt * (a[q + "z"] + b[q + "z"])
        for q, d in zip("ts", steps)
    ]
    return base, wg, forward


def strided(ref, row):
    levels, rows, _ = ref.shape
    return ref.reshape(levels * rows, LANES)[pl.ds(row, levels, stride=rows), :]


def put(ref, row, value):
    levels, rows, _ = ref.shape
    ref.reshape(levels * rows, LANES)[pl.ds(row, levels, stride=rows), :] = value


def pack_kernel(
    levels, rows, lat_size, t_hbm, s_hbm, c_hbm, m_hbm, n_hbm,
    t_ref, s_ref, c_ref, m_ref, n_ref, side_ref, core_ref, chip_ref, lat_ref, far_ref, column_ref, own_ref, *more,
):
    *more, sems = more
    K = levels
    pairs = ((t_hbm, t_ref), (s_hbm, s_ref), (c_hbm, c_ref), (n_hbm, n_ref), (m_hbm, m_ref))
    pairs = [(src, dst if dst is n_ref else dst.at[:, :rows]) for src, dst in pairs]
    copies = [pltpu.make_async_copy(src, dst, sems.at[i]) for i, (src, dst) in enumerate(pairs)]
    for copy in copies:
        copy.start()
    lane = iota((levels, LANES), 1)
    group = lane // 4

    group = lane // 4

    def gather(ref):
        out = jnp.zeros((levels, LANES), F32)
        for j in range(rows):
            out = jnp.where(group == j, roll(strided(ref, j), 4 * j + 2), out)
        return out

    def mirrored(x):
        index = (LANES - iota(x.shape, 1)) % LANES
        return jnp.take_along_axis(x, index, axis=1)

    def tracer_rows(out_ref, tracer, ref, picks, change=lambda x: x):
        for i, j in enumerate(picks):
            at = (2 * tracer + i) * K
            out_ref[at : at + K, :] = change(strided(ref, j))

    south, north, fold = (0, 1), (rows - 2, rows - 1), (rows - 2, rows - 3)
    is_top = lax.axis_index("lat") == lat_size - 1
    is_odd = lax.axis_index("lon") % 2 == 1
    place = iota((levels, LANES), 1) % 4
    sides = []
    for tracer, ref in enumerate((t_ref, s_ref)):
        copies[tracer].wait()
        sides.append(gather(ref))
        tracer_rows(far_ref, tracer, ref, fold, mirrored)
        if more:
            tracer_rows(lat_ref, tracer, ref, north)
            tracer_rows(more[0], tracer, ref, south)
        else:
            for i in range(2):
                at = (2 * tracer + i) * K
                lat_ref[at : at + K, :] = jnp.where(is_top, strided(ref, south[i]), strided(ref, north[i]))

    copies[2].wait()
    sides.append(gather(c_ref))
    copies[3].wait()
    counts = n_ref[...].astype(F32)
    moved = jnp.concatenate([roll(counts[j : j + 1], 4 * j + 2) for j in range(rows)], axis=0)
    line = jnp.sum(
        jnp.where(iota((rows, LANES), 1) // 4 == iota((rows, LANES), 0), moved, 0.0), axis=0, keepdims=True
    )
    heat, salt, speed = sides
    line = jnp.broadcast_to(line, (levels, LANES))
    for i, value in enumerate((heat, salt, speed)):
        side_ref[i * K : (i + 1) * K, :] = value
    side_ref[3 * K :, :] = line[:8]
    to_east = jnp.where(place < 2, heat, roll(salt, 2)), jnp.where(place == 2, roll(speed, 1), line)
    to_west = jnp.where(place < 2, roll(salt, -2), heat), line
    for i, (e, w) in enumerate(zip(to_east, to_west)):
        core_ref[i * K : (i + 1) * K, :] = jnp.where(is_odd, w, e)
        chip = jnp.where(is_odd, e, w)
        chip_ref[i * K : (i + 1) * K, :] = chip
        far_ref[4 * K + 8 + i * K : 4 * K + 8 + (i + 1) * K, :] = chip

    def tally(picks):
        return jnp.concatenate(
            [counts[j : j + 1] for j in picks] + [jnp.zeros((8 - len(picks), LANES), F32)], axis=0
        )

    far_ref[4 * K : 4 * K + 8, :] = mirrored(tally(fold))
    first = jnp.zeros((levels, LANES), F32)
    for i, (ref, j) in enumerate((ref, j) for ref in (t_ref, s_ref) for j in fold):
        first = jnp.where(lane == i, roll(strided(ref, j), i), first)
    column_ref[:K, :] = first
    column_ref[K : K + 8, :] = tally(fold)
    if more:
        lat_ref[5 * K :, :] = tally(north)
        more[0][4 * K : 5 * K, :] = jnp.zeros((K, LANES), F32)
        more[0][5 * K :, :] = tally(south)
    else:
        lat_ref[5 * K :, :] = jnp.where(is_top, tally(south), tally(north))
    copies[4].wait()
    lat_ref[4 * K : 5 * K, :] = strided(m_ref, rows - 1)
    for i, j in enumerate((0, rows - 2, rows - 1)):
        own_ref[i * K : (i + 1) * K, :] = strided(m_ref, j)


def relay_kernel(far_ref, _, out_ref):
    K = out_ref.shape[0] - 8
    lane = iota((K, LANES), 1)
    out = far_ref[:K, :]
    for i in (1, 2, 3):
        out = jnp.where(lane == i, roll(far_ref[i * K : (i + 1) * K, :], i), out)
    out_ref[:K, :] = out
    out_ref[K:, :] = far_ref[4 * K : 4 * K + 8, :]


NAMES = ("t", "s", "r", "tz", "sz", "rz")
STATE = 19


def south_kernel(levels, rows, last, early, t_ref, s_ref, c_ref, m_ref, n_ref, *more):
    *more, pt_ref, ps_ref, state_out = more[:-1] if early else more
    at_origin = (lax.axis_index("lat") == 0) & (lax.axis_index("lon") < 2)

    @pl.when(at_origin if early else jnp.logical_not(at_origin))
    def _():
        interior_kernel(levels, rows, 0, last, t_ref, s_ref, c_ref, m_ref, n_ref, pt_ref, ps_ref, state_out)


def interior_kernel(levels, rows, first, last, t_ref, s_ref, c_ref, m_ref, n_ref, *more):
    if first:
        _, _, _, state_in, pt_ref, ps_ref = more
    else:
        pt_ref, ps_ref, state_out = more
    shape = (levels, LANES)
    level = iota(shape, 0)
    last_lane = iota((1, LANES), 1) == LANES - 1
    factors = level_factors(levels)
    zero = jnp.zeros(shape, F32)

    def step(j, carry):
        prev, m1, d2, limited2, base2, wg2, m2, acc2, acc1 = carry
        t, s, c, m = (strided(ref, j) for ref in (t_ref, s_ref, c_ref, m_ref))
        n = n_ref[pl.ds(j, 1), :]
        here = column_row(t, s, n, factors, level)
        east = shifted(here, -1)
        wet = level < jnp.minimum(n, jnp.where(last_lane, 0, east["n"]))
        steps = [face_step(here, east, wet, q) for q in "ts"]
        base, wg, forward = face_base(here, east, c, wet, steps)
        inside = level < n
        acc = []
        for q, d, flux in zip("ts", steps, base):
            limited = minmod(roll(d, 1), d)
            flux = flux + wg * jnp.where(forward, limited, roll(limited, -1))
            acc.append(jnp.where(inside, here[q], 0.0) + roll(flux, 1) - flux)
        wet = level < jnp.minimum(prev["n"], n)
        d1 = [face_step(prev, here, wet, q) for q in "ts"]
        base1, wg1, _ = face_base(prev, here, m1, wet, d1)
        limited1 = [minmod(x, y) for x, y in zip(d2, d1)]
        forward2 = m2 > 0.0
        flux2 = [b + wg2 * jnp.where(forward2, x, y) for b, x, y in zip(base2, limited2, limited1)]
        done = [x - f for x, f in zip(acc2, flux2)]
        acc1 = [x + f for x, f in zip(acc1, flux2)]
        at = (j + rows - 2) % rows
        put(pt_ref, at, done[0])
        put(ps_ref, at, done[1])
        return here, m, d1, limited1, base1, wg1, m1, acc1, acc

    def pack(carry):
        prev, m1, d2, limited2, base2, wg2, m2, acc2, acc1 = carry
        return [prev[name] for name in NAMES] + [m1, *d2, *limited2, *base2, wg2, m2, *acc2, *acc1]

    def unpack(flat, n):
        prev = dict(zip(NAMES, flat), n=n)
        m1, d2, limited2, base2, wg2, m2, acc2, acc1 = (
            flat[6], flat[7:9], flat[9:11], flat[11:13], flat[13], flat[14], flat[15:17], flat[17:19]
        )
        return prev, m1, d2, limited2, base2, wg2, m2, acc2, acc1

    if first:
        carry = unpack([state_in[i] for i in range(STATE)], n_ref[first - 1 : first, :])
    else:
        carry = unpack([zero] * STATE, jnp.zeros((1, LANES), jnp.int32))

    def block(i, carry):
        for u in range(UNROLL):
            carry = step(first + i * UNROLL + u, carry)
        return carry

    carry = lax.fori_loop(0, (last - first) // UNROLL, block, carry)
    if last < rows:
        for i, value in enumerate(pack(carry)):
            state_out[i] = value
        return
    _, _, _, limited2, base2, wg2, m2, acc2, acc1 = carry
    flux2 = [b + wg2 * jnp.where(m2 > 0.0, x, 0.0) for b, x in zip(base2, limited2)]
    for ref, a2, a1, f in zip((pt_ref, ps_ref), acc2, acc1, flux2):
        put(ref, rows - 2, a2 - f)
        put(ref, rows - 1, a1 + f)


def edge_faces(cells, speeds):
    level = iota(cells[0]["t"].shape, 0).astype(F32)
    wets = [level < jnp.minimum(a["n"], b["n"]) for a, b in zip(cells, cells[1:])]
    d = [[face_step(a, b, w, q) for q in "ts"] for a, b, w in zip(cells, cells[1:], wets)]
    limited = [[minmod(x, y) for x, y in zip(d[i], d[i + 1])] for i in (0, 1)]
    base, wg, forward = face_base(cells[1], cells[2], speeds[1], wets[1], d[1])
    flux = [b + wg * jnp.where(forward, x, y) for b, x, y in zip(base, *limited)]
    first = last = None
    if speeds[0] is not None:
        _, wg0 = weights(speeds[0], wets[0])
        first = [wg0 * jnp.where(speeds[0] > 0.0, 0.0, x) for x in limited[0]]
    if speeds[2] is not None:
        _, wg2 = weights(speeds[2], wets[2])
        last = [wg2 * jnp.where(speeds[2] > 0.0, x, 0.0) for x in limited[1]]
    return first, flux, last


def longitude_kernel(
    levels, rows, lat_size, lon_size, pt_ref, ps_ref, side_ref, near_in, core_in, far_in, t_new, s_new
):
    shape = (levels, LANES)
    lane = iota(shape, 1)
    place = lane % 4
    factors = level_factors(levels)
    K = levels
    is_top = lax.axis_index("lat") == lat_size - 1
    lon_at = lax.axis_index("lon")
    is_odd = lon_at % 2 == 1
    wraps = (lon_at == 0) | (lon_at == lon_size - 1)

    def cell_row(t, s, n):
        return column_row(t, s, n, factors, iota(shape, 0))

    own_t, own_s, own_c = (side_ref[i * K : (i + 1) * K, :] for i in range(3))
    own_n = side_ref[3 * K : 3 * K + 1, :]
    core = core_in[...]
    chip = jnp.where(is_top & ~wraps, near_in[...], far_in[4 * K + 8 :, :])
    west, east = jnp.where(is_odd, core, chip), jnp.where(is_odd, chip, core)
    first_two = place < 2

    def side(t, s, n, speed):
        row = cell_row(t, s, n)
        cells = [row] + [shifted(row, -i) for i in (1, 2, 3)]
        return edge_faces(cells, [roll(speed, -i) for i in range(3)])

    _, west_flux, west_last = side(
        jnp.where(first_two, west[:K], own_t),
        jnp.where(first_two, roll(west[:K], -2), own_s),
        jnp.where(first_two[:1], west[K : K + 1], own_n),
        jnp.where(place == 1, roll(west[K:], -1), own_c),
    )
    east_first, east_flux, _ = side(
        jnp.where(first_two, own_t, east[:K]),
        jnp.where(first_two, own_s, roll(east[:K], 2)),
        jnp.where(first_two[:1], own_n, east[K : K + 1]),
        own_c,
    )
    lon = []
    for fw, lw, fe, le in zip(west_flux, west_last, east_flux, east_first):
        group = jnp.where(
            place == 0,
            -le,
            jnp.where(place == 1, roll(le - fe, 1), jnp.where(place == 2, roll(fw - lw, 2), roll(lw, 3))),
        )
        lon.append(group)

    edge_lanes = (lane >= LANES - 2) | (lane < 2)
    for q, (p_ref, new_ref) in enumerate(((pt_ref, t_new), (ps_ref, s_new))):
        for j in range(rows):
            moved = jnp.where(edge_lanes, roll(lon[q], LANES - 2 - 4 * j), 0.0)
            put(new_ref, j, strided(p_ref, j) + moved)


def latitude_kernel(
    levels, rows, lat_size, lon_size, t_new, s_new, t_ref, s_ref, n_ref, own_ref,
    far_in, below_in, above_in, column_in, relay_in, own_column, t_out, s_out, ends_ref, sems,
):
    shape = (levels, LANES)
    factors = level_factors(levels)
    K = levels
    row_at = lax.axis_index("lat")
    is_top, is_bottom = row_at == lat_size - 1, row_at == 0
    lon_at = lax.axis_index("lon")
    is_odd = lon_at % 2 == 1
    middle = pl.ds(8, rows - 16)
    copies = [
        pltpu.make_async_copy(new_ref.at[:, middle], out_ref.at[:, middle], sems.at[q])
        for q, (new_ref, out_ref) in enumerate(((t_new, t_out), (s_new, s_out)))
    ]
    for copy in copies:
        copy.start()

    def cell_row(t, s, n):
        return column_row(t, s, n, factors, iota(shape, 0))

    counts = n_ref[...].astype(F32)

    def own_row(j):
        return cell_row(strided(t_ref, j), strided(s_ref, j), counts[j : j + 1])

    def sent_row(array, which, at_counts):
        t, s = array[which * K : (which + 1) * K], array[(2 + which) * K : (3 + which) * K]
        return cell_row(t, s, array[at_counts + which : at_counts + which + 1])

    below = jnp.where(is_bottom, 0.0, below_in[...])
    cells = [sent_row(below, 0, 5 * K), sent_row(below, 1, 5 * K), own_row(0), own_row(1)]
    _, south_flux, south_last = edge_faces(cells, [None, below[4 * K : 5 * K], own_ref[:K]])

    pivot = (lon_at * 2) % lon_size == 0
    column = jnp.where(is_odd, relay_in[...], jnp.where(pivot, own_column[: K + 8, :], column_in[: K + 8, :]))
    parts = [roll(column[:K], -i) for i in range(4)] + [column[K : K + 8]]
    fold = far_in[: 4 * K + 8, :]
    fold = jnp.where(iota(fold.shape, 1) == 0, jnp.concatenate(parts, axis=0), fold)
    above = above_in[...]
    above = jnp.where(is_top, fold, jnp.concatenate([above[: 4 * K], above[5 * K :]], axis=0))
    cells = [own_row(rows - 2), own_row(rows - 1), sent_row(above, 0, 4 * K), sent_row(above, 1, 4 * K)]
    north_first, north_flux, _ = edge_faces(cells, [own_ref[K : 2 * K], own_ref[2 * K :], None])

    for q, (new_ref, out_ref) in enumerate(((t_new, t_out), (s_new, s_out))):
        ends = ends_ref.at[q]
        ends[:, :8, :] = new_ref[:, :8, :]
        ends[:, 8:16, :] = new_ref[:, rows - 8 : rows, :]
        extra = {
            0: south_flux[q] - south_last[q],
            1: south_last[q],
            14: -north_first[q],
            15: north_first[q] - north_flux[q],
        }
        for j, value in extra.items():
            put(ends, j, strided(ends, j) + value)
        for i, at in enumerate((0, rows - 8)):
            copy = pltpu.make_async_copy(
                ends.at[:, pl.ds(8 * i, 8)], out_ref.at[:, pl.ds(at, 8)], sems.at[2 + 2 * q + i]
            )
            copy.start()
            copies.append(copy)
    for copy in copies:
        copy.wait()


def body(nlat, nlon, t, s, c, m, n):
    levels, rows, _ = t.shape
    vmem, hbm = pl.BlockSpec(memory_space=pltpu.VMEM), pl.BlockSpec(memory_space=pltpu.HBM)
    f = functools.partial
    out = lambda *shape: jax.ShapeDtypeStruct(shape, F32)
    K = levels
    params = pltpu.CompilerParams(vmem_limit_bytes=VMEM)
    swap = nlat == 2
    field, lat_shape = out(rows, K, LANES), out(5 * K + 8, LANES)
    room = out(levels, rows + SPARE, LANES)
    shapes = [room] * 4 + [jax.ShapeDtypeStruct(n.shape, n.dtype)]
    shapes += [out(3 * K + 8, LANES), out(2 * K, LANES), out(2 * K, LANES), lat_shape, out(6 * K + 8, LANES)]
    shapes += [out(2 * K + 8, LANES), out(3 * K, LANES)]
    shapes += [] if swap else [lat_shape]
    t_v, s_v, c_v, m_v, n_v, side, core, chip, lat, far, column, own, *more = pl.pallas_call(
        f(pack_kernel, levels, rows, nlat),
        out_shape=tuple(shapes),
        in_specs=[hbm] * 5,
        out_specs=(vmem,) * len(shapes),
        scratch_shapes=[pltpu.SemaphoreType.DMA((5,))],
        compiler_params=params,
        name="pack",
    )(*[pltpu.with_memory_space_constraint(x, pltpu.HBM) for x in (t, s, c, m, n)])

    top = nlat - 1

    def exchange(array, top_to, others_to, helper=lambda i: i):
        to = {(j, i): (j, others_to(i)) for j in range(top) for i in range(nlon)}
        for i in range(nlon):
            partner, via = top_to(i), helper(i)
            if partner is not None:
                to[top, i] = (top, partner)
            elif to.get((0, via)) == (0, via ^ 1) and to.get((0, via ^ 1)) == (0, via):
                to[top, i], to[0, via], to[0, via ^ 1] = (0, via), (0, via ^ 1), (top, i)
            else:
                to[top, i] = (top, i)
        pairs = [(i * nlat + j, to[j, i][1] * nlat + to[j, i][0]) for i in range(nlon) for j in range(nlat)]
        return lax.ppermute(array, ("lon", "lat"), pairs)

    def chips(i):
        return (i + (1 if i % 2 else -1)) % nlon

    columns = {i: i ^ 1 if 2 * i % nlon == 0 else nlon - i for i in range(0, nlon, 2)}
    lone = [i for i in range(1, nlon, 2) if columns[i - 1] != i]
    columns |= {i: i - 1 for i in range(1, nlon, 2) if i not in lone}
    for part in ([i for i in lone if 2 * i < nlon], [i for i in lone if 2 * i > nlon]):
        columns |= dict(zip(part, part[1:] + part[:1]))

    middle = HEAD
    fields = (t_v, s_v, c_v, m_v, n_v)
    south_out = (room, room, out(STATE, K, LANES))
    cost = pl.CostEstimate(flops=20_000_000, bytes_accessed=1_000_000, transcendentals=0)
    pt, ps, state, far = pl.pallas_call(
        f(south_kernel, levels, rows, middle, True),
        out_shape=south_out + (out(*far.shape),),
        in_specs=[vmem] * 6,
        out_specs=(vmem,) * 4,
        input_output_aliases={5: 3},
        cost_estimate=cost,
        compiler_params=params,
        name="south_at_origin",
    )(*fields, far)

    ring, rung = range(nlon), range(nlat)
    far_in = exchange(far, lambda i: nlon - 1 - i, chips)
    below_in = above_in = lax.ppermute(lat, "lat", [(i, (i + 1) % nlat) for i in rung])
    if not swap:
        above_in = lax.ppermute(more[0], "lat", [(i, (i - 1) % nlat) for i in rung])
    near_in = exchange(
        chip,
        lambda i: chips(i) if 0 < i < nlon - 1 else None,
        lambda i: i ^ 1,
        lambda i: i + nlon // 4 if i == 0 else i - nlon // 4,
    )
    core_in = lax.ppermute(core, "lon", [(i, i ^ 1) for i in ring])
    column_in = exchange(column, columns.get, lambda i: i ^ 1)

    pt, ps, state = pl.pallas_call(
        f(south_kernel, levels, rows, middle, False),
        out_shape=south_out,
        in_specs=[vmem] * 8,
        out_specs=(vmem,) * 3,
        input_output_aliases={5: 0, 6: 1, 7: 2},
        cost_estimate=cost,
        compiler_params=params,
        name="south_elsewhere",
    )(*fields, pt, ps, state)
    relay = pl.pallas_call(
        relay_kernel,
        out_shape=out(K + 8, LANES),
        in_specs=[vmem] * 2,
        out_specs=vmem,
        compiler_params=params,
        name="relay",
    )(far_in, state)
    relay_in = lax.ppermute(relay, "lon", [(i, i ^ 1) for i in ring])

    pt, ps = pl.pallas_call(
        f(interior_kernel, levels, rows, middle, rows),
        out_shape=(room, room),
        in_specs=[vmem] * 9,
        out_specs=(vmem,) * 2,
        input_output_aliases={5: 0, 6: 1},
        cost_estimate=pl.CostEstimate(flops=20_000_000, bytes_accessed=1_000_000, transcendentals=0),
        compiler_params=params,
        name="interior_north",
    )(*fields, pt, ps, relay, state)

    t_new, s_new = pl.pallas_call(
        f(longitude_kernel, levels, rows, nlat, nlon),
        out_shape=(room, room),
        in_specs=[vmem] * 6,
        out_specs=(vmem,) * 2,
        input_output_aliases={0: 0, 1: 1},
        cost_estimate=pl.CostEstimate(flops=5_000_000, bytes_accessed=1_000_000, transcendentals=0),
        compiler_params=params,
        name="longitude_edges",
    )(pt, ps, side, near_in, core_in, far_in)

    return pl.pallas_call(
        f(latitude_kernel, levels, rows, nlat, nlon),
        out_shape=(out(*t.shape),) * 2,
        in_specs=[vmem] * 12,
        out_specs=(hbm,) * 2,
        scratch_shapes=[pltpu.VMEM((2, K, 24, LANES), F32), pltpu.SemaphoreType.DMA((6,))],
        compiler_params=params,
        name="latitude_edges",
    )(t_new, s_new, t_v, s_v, n_v, own, far_in, below_in, above_in, column_in, relay_in, column)


def solution(mesh):
    spec = P(None, "lat", "lon")
    return jax.shard_map(
        functools.partial(body, mesh.shape["lat"], mesh.shape["lon"]),
        mesh=mesh,
        in_specs=(spec,) * 4 + (P("lat", "lon"),),
        out_specs=(spec,) * 2,
        check_vma=False,
    )
```

```python
import functools

import jax
import jax.numpy as jnp
from jax import lax
from jax.experimental import pallas as pl
from jax.experimental.pallas import tpu as pltpu
from jax.sharding import PartitionSpec as P

heat_swelling_alpha = 0.1655
coef_beta = 0.76554
cabbeling_parameter = 0.05952
lambda_salt = 0.00054914
thermobaric_parameter = 0.0001497
press_salt = 1.109e-05
cross_coupling_contribution = 0.0024341
total_depth = 5000.0
kappa_iso = 0.1
strat_min = 0.1

LANES = 128
VMEM = 8 * 1024 * 1024
UNROLL = 8
HEAD = 24
SPARE = 8
F32 = jnp.float32


def iota(shape, axis):
    return lax.broadcasted_iota(jnp.int32, shape, axis)


def roll(array, shift, axis=1):
    size = array.shape[axis]
    return pltpu.roll(array, shift % size, axis)


def minmod(x, y):
    return jnp.maximum(jnp.minimum(x, jnp.maximum(y, 0.0)), jnp.minimum(y, 0.0))


def level_factors(levels):
    depth = total_depth * (iota((levels, LANES), 0).astype(F32) + 0.5) / levels
    heat = -heat_swelling_alpha * (1.0 + thermobaric_parameter * depth)
    salt = coef_beta * (1.0 - press_salt * depth)
    return heat, salt


def density(t, s, factors):
    heat, salt = factors
    return t * (
        heat
        - (0.5 * heat_swelling_alpha * cabbeling_parameter) * t
        - cross_coupling_contribution * s
    ) + s * (salt - (0.5 * coef_beta * lambda_salt) * s)


def vertical(q, level):
    levels = q.shape[0]
    step = roll(q, -1, 0) - q
    below = roll(step, 1, 0)
    return jnp.where(level == levels - 1, below, step) + jnp.where(level == 0, step, below)


def column_row(t, s, n, factors, level):
    r = density(t, s, factors)
    return {
        "t": t,
        "s": s,
        "r": r,
        "tz": vertical(t, level),
        "sz": vertical(s, level),
        "rz": vertical(r, level),
        "n": n,
    }


def shifted(row, by):
    return {name: roll(value, by) for name, value in row.items()}


def weights(c, wet):
    size = jnp.abs(c)
    return jnp.where(wet, c, 0.0), jnp.where(wet, 0.5 * (size - c * c), 0.0)


def face_step(a, b, wet, name):
    return jnp.where(wet, b[name] - a[name], 0.0)


def face_base(a, b, c, wet, steps):
    wc, wg = weights(c, wet)
    steep = (a["r"] - b["r"]) / jnp.maximum(a["rz"] + b["rz"], 4.0 * strat_min)
    tilt = jnp.where(wet, jnp.clip(steep, -0.25, 0.25), 0.0) * (-kappa_iso)
    forward = c > 0.0
    base = [
        wc * jnp.where(forward, a[q], b[q]) - kappa_iso * d + tilt * (a[q + "z"] + b[q + "z"])
        for q, d in zip("ts", steps)
    ]
    return base, wg, forward


def strided(ref, row):
    levels, rows, _ = ref.shape
    return ref.reshape(levels * rows, LANES)[pl.ds(row, levels, stride=rows), :]


def put(ref, row, value):
    levels, rows, _ = ref.shape
    ref.reshape(levels * rows, LANES)[pl.ds(row, levels, stride=rows), :] = value


def pack_kernel(
    levels, rows, lat_size, t_hbm, s_hbm, c_hbm, m_hbm, n_hbm,
    t_ref, s_ref, c_ref, m_ref, n_ref, side_ref, core_ref, chip_ref, lat_ref, far_ref, column_ref, own_ref, *more,
):
    *more, sems = more
    K = levels
    pairs = ((t_hbm, t_ref), (s_hbm, s_ref), (c_hbm, c_ref), (n_hbm, n_ref), (m_hbm, m_ref))
    pairs = [(src, dst if dst is n_ref else dst.at[:, :rows]) for src, dst in pairs]
    copies = [pltpu.make_async_copy(src, dst, sems.at[i]) for i, (src, dst) in enumerate(pairs)]
    for copy in copies:
        copy.start()
    lane = iota((levels, LANES), 1)
    group = lane // 4

    group = lane // 4

    def gather(ref):
        out = jnp.zeros((levels, LANES), F32)
        for j in range(rows):
            out = jnp.where(group == j, roll(strided(ref, j), 4 * j + 2), out)
        return out

    def mirrored(x):
        index = (LANES - iota(x.shape, 1)) % LANES
        return jnp.take_along_axis(x, index, axis=1)

    def tracer_rows(out_ref, tracer, ref, picks, change=lambda x: x):
        for i, j in enumerate(picks):
            at = (2 * tracer + i) * K
            out_ref[at : at + K, :] = change(strided(ref, j))

    south, north, fold = (0, 1), (rows - 2, rows - 1), (rows - 2, rows - 3)
    is_top = lax.axis_index("lat") == lat_size - 1
    is_odd = lax.axis_index("lon") % 2 == 1
    place = iota((levels, LANES), 1) % 4
    sides = []
    for tracer, ref in enumerate((t_ref, s_ref)):
        copies[tracer].wait()
        sides.append(gather(ref))
        tracer_rows(far_ref, tracer, ref, fold, mirrored)
        if more:
            tracer_rows(lat_ref, tracer, ref, north)
            tracer_rows(more[0], tracer, ref, south)
        else:
            for i in range(2):
                at = (2 * tracer + i) * K
                lat_ref[at : at + K, :] = jnp.where(is_top, strided(ref, south[i]), strided(ref, north[i]))

    copies[2].wait()
    sides.append(gather(c_ref))
    copies[3].wait()
    counts = n_ref[...].astype(F32)
    moved = jnp.concatenate([roll(counts[j : j + 1], 4 * j + 2) for j in range(rows)], axis=0)
    line = jnp.sum(
        jnp.where(iota((rows, LANES), 1) // 4 == iota((rows, LANES), 0), moved, 0.0), axis=0, keepdims=True
    )
    heat, salt, speed = sides
    line = jnp.broadcast_to(line, (levels, LANES))
    for i, value in enumerate((heat, salt, speed)):
        side_ref[i * K : (i + 1) * K, :] = value
    side_ref[3 * K :, :] = line[:8]
    to_east = jnp.where(place < 2, heat, roll(salt, 2)), jnp.where(place == 2, roll(speed, 1), line)
    to_west = jnp.where(place < 2, roll(salt, -2), heat), line
    for i, (e, w) in enumerate(zip(to_east, to_west)):
        core_ref[i * K : (i + 1) * K, :] = jnp.where(is_odd, w, e)
        chip = jnp.where(is_odd, e, w)
        chip_ref[i * K : (i + 1) * K, :] = chip
        far_ref[4 * K + 8 + i * K : 4 * K + 8 + (i + 1) * K, :] = chip

    def tally(picks):
        return jnp.concatenate(
            [counts[j : j + 1] for j in picks] + [jnp.zeros((8 - len(picks), LANES), F32)], axis=0
        )

    far_ref[4 * K : 4 * K + 8, :] = mirrored(tally(fold))
    first = jnp.zeros((levels, LANES), F32)
    for i, (ref, j) in enumerate((ref, j) for ref in (t_ref, s_ref) for j in fold):
        first = jnp.where(lane == i, roll(strided(ref, j), i), first)
    column_ref[:K, :] = first
    column_ref[K : K + 8, :] = tally(fold)
    if more:
        lat_ref[5 * K :, :] = tally(north)
        more[0][4 * K : 5 * K, :] = jnp.zeros((K, LANES), F32)
        more[0][5 * K :, :] = tally(south)
    else:
        lat_ref[5 * K :, :] = jnp.where(is_top, tally(south), tally(north))
    copies[4].wait()
    lat_ref[4 * K : 5 * K, :] = strided(m_ref, rows - 1)
    for i, j in enumerate((0, rows - 2, rows - 1)):
        own_ref[i * K : (i + 1) * K, :] = strided(m_ref, j)


def relay_kernel(far_ref, _, out_ref):
    K = out_ref.shape[0] - 8
    lane = iota((K, LANES), 1)
    out = far_ref[:K, :]
    for i in (1, 2, 3):
        out = jnp.where(lane == i, roll(far_ref[i * K : (i + 1) * K, :], i), out)
    out_ref[:K, :] = out
    out_ref[K:, :] = far_ref[4 * K : 4 * K + 8, :]


NAMES = ("t", "s", "r", "tz", "sz", "rz")
STATE = 19


def south_kernel(levels, rows, last, early, t_ref, s_ref, c_ref, m_ref, n_ref, *more):
    *more, pt_ref, ps_ref, state_out = more[:-1] if early else more
    at_origin = (lax.axis_index("lat") == 0) & (lax.axis_index("lon") < 2)

    @pl.when(at_origin if early else jnp.logical_not(at_origin))
    def _():
        interior_kernel(levels, rows, 0, last, t_ref, s_ref, c_ref, m_ref, n_ref, pt_ref, ps_ref, state_out)


def interior_kernel(levels, rows, first, last, t_ref, s_ref, c_ref, m_ref, n_ref, *more):
    if first:
        _, _, _, state_in, pt_ref, ps_ref = more
    else:
        pt_ref, ps_ref, state_out = more
    shape = (levels, LANES)
    level = iota(shape, 0)
    last_lane = iota((1, LANES), 1) == LANES - 1
    factors = level_factors(levels)
    zero = jnp.zeros(shape, F32)

    def step(j, carry):
        prev, m1, d2, limited2, base2, wg2, m2, acc2, acc1 = carry
        t, s, c, m = (strided(ref, j) for ref in (t_ref, s_ref, c_ref, m_ref))
        n = n_ref[pl.ds(j, 1), :]
        here = column_row(t, s, n, factors, level)
        east = shifted(here, -1)
        wet = level < jnp.minimum(n, jnp.where(last_lane, 0, east["n"]))
        steps = [face_step(here, east, wet, q) for q in "ts"]
        base, wg, forward = face_base(here, east, c, wet, steps)
        inside = level < n
        acc = []
        for q, d, flux in zip("ts", steps, base):
            limited = minmod(roll(d, 1), d)
            flux = flux + wg * jnp.where(forward, limited, roll(limited, -1))
            acc.append(jnp.where(inside, here[q], 0.0) + roll(flux, 1) - flux)
        wet = level < jnp.minimum(prev["n"], n)
        d1 = [face_step(prev, here, wet, q) for q in "ts"]
        base1, wg1, _ = face_base(prev, here, m1, wet, d1)
        limited1 = [minmod(x, y) for x, y in zip(d2, d1)]
        forward2 = m2 > 0.0
        flux2 = [b + wg2 * jnp.where(forward2, x, y) for b, x, y in zip(base2, limited2, limited1)]
        done = [x - f for x, f in zip(acc2, flux2)]
        acc1 = [x + f for x, f in zip(acc1, flux2)]
        at = (j + rows - 2) % rows
        put(pt_ref, at, done[0])
        put(ps_ref, at, done[1])
        return here, m, d1, limited1, base1, wg1, m1, acc1, acc

    def pack(carry):
        prev, m1, d2, limited2, base2, wg2, m2, acc2, acc1 = carry
        return [prev[name] for name in NAMES] + [m1, *d2, *limited2, *base2, wg2, m2, *acc2, *acc1]

    def unpack(flat, n):
        prev = dict(zip(NAMES, flat), n=n)
        m1, d2, limited2, base2, wg2, m2, acc2, acc1 = (
            flat[6], flat[7:9], flat[9:11], flat[11:13], flat[13], flat[14], flat[15:17], flat[17:19]
        )
        return prev, m1, d2, limited2, base2, wg2, m2, acc2, acc1

    if first:
        carry = unpack([state_in[i] for i in range(STATE)], n_ref[first - 1 : first, :])
    else:
        carry = unpack([zero] * STATE, jnp.zeros((1, LANES), jnp.int32))

    def block(i, carry):
        for u in range(UNROLL):
            carry = step(first + i * UNROLL + u, carry)
        return carry

    carry = lax.fori_loop(0, (last - first) // UNROLL, block, carry)
    if last < rows:
        for i, value in enumerate(pack(carry)):
            state_out[i] = value
        return
    _, _, _, limited2, base2, wg2, m2, acc2, acc1 = carry
    flux2 = [b + wg2 * jnp.where(m2 > 0.0, x, 0.0) for b, x in zip(base2, limited2)]
    for ref, a2, a1, f in zip((pt_ref, ps_ref), acc2, acc1, flux2):
        put(ref, rows - 2, a2 - f)
        put(ref, rows - 1, a1 + f)


def edge_faces(cells, speeds):
    level = iota(cells[0]["t"].shape, 0).astype(F32)
    wets = [level < jnp.minimum(a["n"], b["n"]) for a, b in zip(cells, cells[1:])]
    d = [[face_step(a, b, w, q) for q in "ts"] for a, b, w in zip(cells, cells[1:], wets)]
    limited = [[minmod(x, y) for x, y in zip(d[i], d[i + 1])] for i in (0, 1)]
    base, wg, forward = face_base(cells[1], cells[2], speeds[1], wets[1], d[1])
    flux = [b + wg * jnp.where(forward, x, y) for b, x, y in zip(base, *limited)]
    first = last = None
    if speeds[0] is not None:
        _, wg0 = weights(speeds[0], wets[0])
        first = [wg0 * jnp.where(speeds[0] > 0.0, 0.0, x) for x in limited[0]]
    if speeds[2] is not None:
        _, wg2 = weights(speeds[2], wets[2])
        last = [wg2 * jnp.where(speeds[2] > 0.0, x, 0.0) for x in limited[1]]
    return first, flux, last


def longitude_kernel(
    levels, rows, lat_size, lon_size, pt_ref, ps_ref, side_ref, near_in, core_in, far_in, t_new, s_new, ends_ref
):
    shape = (levels, LANES)
    lane = iota(shape, 1)
    place = lane % 4
    factors = level_factors(levels)
    K = levels
    is_top = lax.axis_index("lat") == lat_size - 1
    lon_at = lax.axis_index("lon")
    is_odd = lon_at % 2 == 1
    wraps = (lon_at == 0) | (lon_at == lon_size - 1)

    def cell_row(t, s, n):
        return column_row(t, s, n, factors, iota(shape, 0))

    own_t, own_s, own_c = (side_ref[i * K : (i + 1) * K, :] for i in range(3))
    own_n = side_ref[3 * K : 3 * K + 1, :]
    core = core_in[...]
    chip = jnp.where(is_top & ~wraps, near_in[...], far_in[4 * K + 8 :, :])
    west, east = jnp.where(is_odd, core, chip), jnp.where(is_odd, chip, core)
    first_two = place < 2

    def side(t, s, n, speed):
        row = cell_row(t, s, n)
        cells = [row] + [shifted(row, -i) for i in (1, 2, 3)]
        return edge_faces(cells, [roll(speed, -i) for i in range(3)])

    _, west_flux, west_last = side(
        jnp.where(first_two, west[:K], own_t),
        jnp.where(first_two, roll(west[:K], -2), own_s),
        jnp.where(first_two[:1], west[K : K + 1], own_n),
        jnp.where(place == 1, roll(west[K:], -1), own_c),
    )
    east_first, east_flux, _ = side(
        jnp.where(first_two, own_t, east[:K]),
        jnp.where(first_two, own_s, roll(east[:K], 2)),
        jnp.where(first_two[:1], own_n, east[K : K + 1]),
        own_c,
    )
    lon = []
    for fw, lw, fe, le in zip(west_flux, west_last, east_flux, east_first):
        group = jnp.where(
            place == 0,
            -le,
            jnp.where(place == 1, roll(le - fe, 1), jnp.where(place == 2, roll(fw - lw, 2), roll(lw, 3))),
        )
        lon.append(group)

    edge_lanes = (lane >= LANES - 2) | (lane < 2)
    for q, (p_ref, new_ref) in enumerate(((pt_ref, t_new), (ps_ref, s_new))):
        for j in range(rows):
            moved = jnp.where(edge_lanes, roll(lon[q], LANES - 2 - 4 * j), 0.0)
            value = strided(p_ref, j) + moved
            if j < 8:
                put(ends_ref.at[q], j, value)
            elif j >= rows - 8:
                put(ends_ref.at[q], j - rows + 16, value)
            else:
                put(new_ref, j, value)


def latitude_kernel(
    levels, rows, lat_size, lon_size, t_new, s_new, _, t_ref, s_ref, n_ref, own_ref,
    far_in, below_in, above_in, column_in, relay_in, own_column, t_out, s_out, ends_ref, sems,
):
    shape = (levels, LANES)
    factors = level_factors(levels)
    K = levels
    row_at = lax.axis_index("lat")
    is_top, is_bottom = row_at == lat_size - 1, row_at == 0
    lon_at = lax.axis_index("lon")
    is_odd = lon_at % 2 == 1
    middle = pl.ds(8, rows - 16)
    copies = [
        pltpu.make_async_copy(new_ref.at[:, middle], out_ref.at[:, middle], sems.at[q])
        for q, (new_ref, out_ref) in enumerate(((t_new, t_out), (s_new, s_out)))
    ]
    for copy in copies:
        copy.start()

    def cell_row(t, s, n):
        return column_row(t, s, n, factors, iota(shape, 0))

    counts = n_ref[...].astype(F32)

    def own_row(j):
        return cell_row(strided(t_ref, j), strided(s_ref, j), counts[j : j + 1])

    def sent_row(array, which, at_counts):
        t, s = array[which * K : (which + 1) * K], array[(2 + which) * K : (3 + which) * K]
        return cell_row(t, s, array[at_counts + which : at_counts + which + 1])

    below = jnp.where(is_bottom, 0.0, below_in[...])
    cells = [sent_row(below, 0, 5 * K), sent_row(below, 1, 5 * K), own_row(0), own_row(1)]
    _, south_flux, south_last = edge_faces(cells, [None, below[4 * K : 5 * K], own_ref[:K]])

    pivot = (lon_at * 2) % lon_size == 0
    column = jnp.where(is_odd, relay_in[...], jnp.where(pivot, own_column[: K + 8, :], column_in[: K + 8, :]))
    parts = [roll(column[:K], -i) for i in range(4)] + [column[K : K + 8]]
    fold = far_in[: 4 * K + 8, :]
    fold = jnp.where(iota(fold.shape, 1) == 0, jnp.concatenate(parts, axis=0), fold)
    above = above_in[...]
    above = jnp.where(is_top, fold, jnp.concatenate([above[: 4 * K], above[5 * K :]], axis=0))
    cells = [own_row(rows - 2), own_row(rows - 1), sent_row(above, 0, 4 * K), sent_row(above, 1, 4 * K)]
    north_first, north_flux, _ = edge_faces(cells, [own_ref[K : 2 * K], own_ref[2 * K :], None])

    for q, out_ref in enumerate((t_out, s_out)):
        ends = ends_ref.at[q]
        extra = {
            0: south_flux[q] - south_last[q],
            1: south_last[q],
            14: -north_first[q],
            15: north_first[q] - north_flux[q],
        }
        for j, value in extra.items():
            put(ends, j, strided(ends, j) + value)
        for i, at in enumerate((0, rows - 8)):
            copy = pltpu.make_async_copy(
                ends.at[:, pl.ds(8 * i, 8)], out_ref.at[:, pl.ds(at, 8)], sems.at[2 + 2 * q + i]
            )
            copy.start()
            copies.append(copy)
    for copy in copies:
        copy.wait()


def body(nlat, nlon, t, s, c, m, n):
    levels, rows, _ = t.shape
    vmem, hbm = pl.BlockSpec(memory_space=pltpu.VMEM), pl.BlockSpec(memory_space=pltpu.HBM)
    f = functools.partial
    out = lambda *shape: jax.ShapeDtypeStruct(shape, F32)
    K = levels
    params = pltpu.CompilerParams(vmem_limit_bytes=VMEM)
    swap = nlat == 2
    field, lat_shape = out(rows, K, LANES), out(5 * K + 8, LANES)
    room = out(levels, rows + SPARE, LANES)
    shapes = [room] * 4 + [jax.ShapeDtypeStruct(n.shape, n.dtype)]
    shapes += [out(3 * K + 8, LANES), out(2 * K, LANES), out(2 * K, LANES), lat_shape, out(6 * K + 8, LANES)]
    shapes += [out(2 * K + 8, LANES), out(3 * K, LANES)]
    shapes += [] if swap else [lat_shape]
    t_v, s_v, c_v, m_v, n_v, side, core, chip, lat, far, column, own, *more = pl.pallas_call(
        f(pack_kernel, levels, rows, nlat),
        out_shape=tuple(shapes),
        in_specs=[hbm] * 5,
        out_specs=(vmem,) * len(shapes),
        scratch_shapes=[pltpu.SemaphoreType.DMA((5,))],
        compiler_params=params,
        name="pack",
    )(*[pltpu.with_memory_space_constraint(x, pltpu.HBM) for x in (t, s, c, m, n)])

    top = nlat - 1

    def exchange(array, top_to, others_to, helper=lambda i: i):
        to = {(j, i): (j, others_to(i)) for j in range(top) for i in range(nlon)}
        for i in range(nlon):
            partner, via = top_to(i), helper(i)
            if partner is not None:
                to[top, i] = (top, partner)
            elif to.get((0, via)) == (0, via ^ 1) and to.get((0, via ^ 1)) == (0, via):
                to[top, i], to[0, via], to[0, via ^ 1] = (0, via), (0, via ^ 1), (top, i)
            else:
                to[top, i] = (top, i)
        pairs = [(i * nlat + j, to[j, i][1] * nlat + to[j, i][0]) for i in range(nlon) for j in range(nlat)]
        return lax.ppermute(array, ("lon", "lat"), pairs)

    def chips(i):
        return (i + (1 if i % 2 else -1)) % nlon

    columns = {i: i ^ 1 if 2 * i % nlon == 0 else nlon - i for i in range(0, nlon, 2)}
    lone = [i for i in range(1, nlon, 2) if columns[i - 1] != i]
    columns |= {i: i - 1 for i in range(1, nlon, 2) if i not in lone}
    for part in ([i for i in lone if 2 * i < nlon], [i for i in lone if 2 * i > nlon]):
        columns |= dict(zip(part, part[1:] + part[:1]))

    middle = HEAD
    fields = (t_v, s_v, c_v, m_v, n_v)
    south_out = (room, room, out(STATE, K, LANES))
    cost = pl.CostEstimate(flops=20_000_000, bytes_accessed=1_000_000, transcendentals=0)
    pt, ps, state, far = pl.pallas_call(
        f(south_kernel, levels, rows, middle, True),
        out_shape=south_out + (out(*far.shape),),
        in_specs=[vmem] * 6,
        out_specs=(vmem,) * 4,
        input_output_aliases={5: 3},
        cost_estimate=cost,
        compiler_params=params,
        name="south_at_origin",
    )(*fields, far)

    ring, rung = range(nlon), range(nlat)
    far_in = exchange(far, lambda i: nlon - 1 - i, chips)
    below_in = above_in = lax.ppermute(lat, "lat", [(i, (i + 1) % nlat) for i in rung])
    if not swap:
        above_in = lax.ppermute(more[0], "lat", [(i, (i - 1) % nlat) for i in rung])
    near_in = exchange(
        chip,
        lambda i: chips(i) if 0 < i < nlon - 1 else None,
        lambda i: i ^ 1,
        lambda i: i + nlon // 4 if i == 0 else i - nlon // 4,
    )
    core_in = lax.ppermute(core, "lon", [(i, i ^ 1) for i in ring])
    column_in = exchange(column, columns.get, lambda i: i ^ 1)

    pt, ps, state = pl.pallas_call(
        f(south_kernel, levels, rows, middle, False),
        out_shape=south_out,
        in_specs=[vmem] * 8,
        out_specs=(vmem,) * 3,
        input_output_aliases={5: 0, 6: 1, 7: 2},
        cost_estimate=cost,
        compiler_params=params,
        name="south_elsewhere",
    )(*fields, pt, ps, state)
    relay = pl.pallas_call(
        relay_kernel,
        out_shape=out(K + 8, LANES),
        in_specs=[vmem] * 2,
        out_specs=vmem,
        compiler_params=params,
        name="relay",
    )(far_in, state)
    relay_in = lax.ppermute(relay, "lon", [(i, i ^ 1) for i in ring])

    pt, ps = pl.pallas_call(
        f(interior_kernel, levels, rows, middle, rows),
        out_shape=(room, room),
        in_specs=[vmem] * 9,
        out_specs=(vmem,) * 2,
        input_output_aliases={5: 0, 6: 1},
        cost_estimate=pl.CostEstimate(flops=20_000_000, bytes_accessed=1_000_000, transcendentals=0),
        compiler_params=params,
        name="interior_north",
    )(*fields, pt, ps, relay, state)

    ends = out(2, K, 24, LANES)
    t_new, s_new, ends_new = pl.pallas_call(
        f(longitude_kernel, levels, rows, nlat, nlon),
        out_shape=(room, room, ends),
        in_specs=[vmem] * 6,
        out_specs=(vmem,) * 3,
        input_output_aliases={0: 0, 1: 1},
        cost_estimate=pl.CostEstimate(flops=5_000_000, bytes_accessed=1_000_000, transcendentals=0),
        compiler_params=params,
        name="longitude_edges",
    )(pt, ps, side, near_in, core_in, far_in)

    t_next, s_next, _ = pl.pallas_call(
        f(latitude_kernel, levels, rows, nlat, nlon),
        out_shape=(out(*t.shape), out(*t.shape), ends),
        in_specs=[vmem] * 13,
        out_specs=(hbm, hbm, vmem),
        input_output_aliases={2: 2},
        scratch_shapes=[pltpu.SemaphoreType.DMA((6,))],
        compiler_params=params,
        name="latitude_edges",
    )(t_new, s_new, ends_new, t_v, s_v, n_v, own, far_in, below_in, above_in, column_in, relay_in, column)
    return t_next, s_next


def solution(mesh):
    spec = P(None, "lat", "lon")
    return jax.shard_map(
        functools.partial(body, mesh.shape["lat"], mesh.shape["lon"]),
        mesh=mesh,
        in_specs=(spec,) * 4 + (P("lat", "lon"),),
        out_specs=(spec,) * 2,
        check_vma=False,
    )
```

```python
import functools

import jax
import jax.numpy as jnp
from jax import lax
from jax.experimental import pallas as pl
from jax.experimental.pallas import tpu as pltpu
from jax.sharding import PartitionSpec as P

heat_swelling_alpha = 0.1655
coef_beta = 0.76554
cabbeling_parameter = 0.05952
lambda_salt = 0.00054914
thermobaric_parameter = 0.0001497
press_salt = 1.109e-05
cross_coupling_contribution = 0.0024341
total_depth = 5000.0
kappa_iso = 0.1
strat_min = 0.1

LANES = 128
VMEM = 8 * 1024 * 1024
UNROLL = 8
HEAD = 24
SPARE = 8
F32 = jnp.float32


def iota(shape, axis):
    return lax.broadcasted_iota(jnp.int32, shape, axis)


def roll(array, shift, axis=1):
    size = array.shape[axis]
    return pltpu.roll(array, shift % size, axis)


def minmod(x, y):
    return jnp.maximum(jnp.minimum(x, jnp.maximum(y, 0.0)), jnp.minimum(y, 0.0))


def level_factors(levels):
    depth = total_depth * (iota((levels, LANES), 0).astype(F32) + 0.5) / levels
    heat = -heat_swelling_alpha * (1.0 + thermobaric_parameter * depth)
    salt = coef_beta * (1.0 - press_salt * depth)
    return heat, salt


def density(t, s, factors):
    heat, salt = factors
    return t * (
        heat
        - (0.5 * heat_swelling_alpha * cabbeling_parameter) * t
        - cross_coupling_contribution * s
    ) + s * (salt - (0.5 * coef_beta * lambda_salt) * s)


def vertical(q, level):
    levels = q.shape[0]
    step = roll(q, -1, 0) - q
    below = roll(step, 1, 0)
    return jnp.where(level == levels - 1, below, step) + jnp.where(level == 0, step, below)


def column_row(t, s, n, factors, level):
    r = density(t, s, factors)
    return {
        "t": t,
        "s": s,
        "r": r,
        "tz": vertical(t, level),
        "sz": vertical(s, level),
        "rz": vertical(r, level),
        "n": n,
    }


def shifted(row, by):
    return {name: roll(value, by) for name, value in row.items()}


def weights(c, wet):
    size = jnp.abs(c)
    return jnp.where(wet, c, 0.0), jnp.where(wet, 0.5 * (size - c * c), 0.0)


def face_step(a, b, wet, name):
    return jnp.where(wet, b[name] - a[name], 0.0)


def face_base(a, b, c, wet, steps):
    wc, wg = weights(c, wet)
    steep = (a["r"] - b["r"]) / jnp.maximum(a["rz"] + b["rz"], 4.0 * strat_min)
    tilt = jnp.where(wet, jnp.clip(steep, -0.25, 0.25), 0.0) * (-kappa_iso)
    forward = c > 0.0
    base = [
        wc * jnp.where(forward, a[q], b[q]) - kappa_iso * d + tilt * (a[q + "z"] + b[q + "z"])
        for q, d in zip("ts", steps)
    ]
    return base, wg, forward


def strided(ref, row):
    levels, rows, _ = ref.shape
    return ref.reshape(levels * rows, LANES)[pl.ds(row, levels, stride=rows), :]


def put(ref, row, value):
    levels, rows, _ = ref.shape
    ref.reshape(levels * rows, LANES)[pl.ds(row, levels, stride=rows), :] = value


def pack_kernel(
    levels, rows, lat_size, t_hbm, s_hbm, c_hbm, m_hbm, n_hbm,
    t_ref, s_ref, c_ref, m_ref, n_ref, side_ref, core_ref, chip_ref, lat_ref, far_ref, column_ref, own_ref, *more,
):
    *more, sems = more
    K = levels
    pairs = ((t_hbm, t_ref), (s_hbm, s_ref), (c_hbm, c_ref), (n_hbm, n_ref), (m_hbm, m_ref))
    pairs = [(src, dst if dst is n_ref else dst.at[:, :rows]) for src, dst in pairs]
    copies = [pltpu.make_async_copy(src, dst, sems.at[i]) for i, (src, dst) in enumerate(pairs)]
    for copy in copies:
        copy.start()
    lane = iota((levels, LANES), 1)
    group = lane // 4

    group = lane // 4

    def gather(ref):
        out = jnp.zeros((levels, LANES), F32)
        for j in range(rows):
            out = jnp.where(group == j, roll(strided(ref, j), 4 * j + 2), out)
        return out

    def mirrored(x):
        index = (LANES - iota(x.shape, 1)) % LANES
        return jnp.take_along_axis(x, index, axis=1)

    def tracer_rows(out_ref, tracer, ref, picks, change=lambda x: x):
        for i, j in enumerate(picks):
            at = (2 * tracer + i) * K
            out_ref[at : at + K, :] = change(strided(ref, j))

    south, north, fold = (0, 1), (rows - 2, rows - 1), (rows - 2, rows - 3)
    is_top = lax.axis_index("lat") == lat_size - 1
    is_odd = lax.axis_index("lon") % 2 == 1
    place = iota((levels, LANES), 1) % 4
    sides = []
    for tracer, ref in enumerate((t_ref, s_ref)):
        copies[tracer].wait()
        sides.append(gather(ref))
        tracer_rows(far_ref, tracer, ref, fold, mirrored)
        if more:
            tracer_rows(lat_ref, tracer, ref, north)
            tracer_rows(more[0], tracer, ref, south)
        else:
            for i in range(2):
                at = (2 * tracer + i) * K
                lat_ref[at : at + K, :] = jnp.where(is_top, strided(ref, south[i]), strided(ref, north[i]))

    copies[2].wait()
    sides.append(gather(c_ref))
    copies[3].wait()
    counts = n_ref[...].astype(F32)
    line = jnp.zeros((8, LANES), F32)
    for at in range(0, rows, 8):
        moved = pltpu.roll(counts[at : at + 8], 4 * at + 2, 1, stride=4, stride_axis=0)
        mine = iota((8, LANES), 1) // 4 == iota((8, LANES), 0) + at
        line = jnp.where(mine, moved, line)
    line = jnp.sum(line, axis=0, keepdims=True)
    heat, salt, speed = sides
    line = jnp.broadcast_to(line, (levels, LANES))
    for i, value in enumerate((heat, salt, speed)):
        side_ref[i * K : (i + 1) * K, :] = value
    side_ref[3 * K :, :] = line[:8]
    to_east = jnp.where(place < 2, heat, roll(salt, 2)), jnp.where(place == 2, roll(speed, 1), line)
    to_west = jnp.where(place < 2, roll(salt, -2), heat), line
    for i, (e, w) in enumerate(zip(to_east, to_west)):
        core_ref[i * K : (i + 1) * K, :] = jnp.where(is_odd, w, e)
        chip = jnp.where(is_odd, e, w)
        chip_ref[i * K : (i + 1) * K, :] = chip
        far_ref[4 * K + 8 + i * K : 4 * K + 8 + (i + 1) * K, :] = chip

    def tally(picks):
        return jnp.concatenate(
            [counts[j : j + 1] for j in picks] + [jnp.zeros((8 - len(picks), LANES), F32)], axis=0
        )

    far_ref[4 * K : 4 * K + 8, :] = mirrored(tally(fold))
    first = jnp.zeros((levels, LANES), F32)
    for i, (ref, j) in enumerate((ref, j) for ref in (t_ref, s_ref) for j in fold):
        first = jnp.where(lane == i, roll(strided(ref, j), i), first)
    column_ref[:K, :] = first
    column_ref[K : K + 8, :] = tally(fold)
    if more:
        lat_ref[5 * K :, :] = tally(north)
        more[0][4 * K : 5 * K, :] = jnp.zeros((K, LANES), F32)
        more[0][5 * K :, :] = tally(south)
    else:
        lat_ref[5 * K :, :] = jnp.where(is_top, tally(south), tally(north))
    copies[4].wait()
    lat_ref[4 * K : 5 * K, :] = strided(m_ref, rows - 1)
    for i, j in enumerate((0, rows - 2, rows - 1)):
        own_ref[i * K : (i + 1) * K, :] = strided(m_ref, j)


def relay_kernel(far_ref, _, out_ref):
    K = out_ref.shape[0] - 8
    lane = iota((K, LANES), 1)
    out = far_ref[:K, :]
    for i in (1, 2, 3):
        out = jnp.where(lane == i, roll(far_ref[i * K : (i + 1) * K, :], i), out)
    out_ref[:K, :] = out
    out_ref[K:, :] = far_ref[4 * K : 4 * K + 8, :]


NAMES = ("t", "s", "r", "tz", "sz", "rz")
STATE = 19


def south_kernel(levels, rows, last, early, t_ref, s_ref, c_ref, m_ref, n_ref, *more):
    *more, pt_ref, ps_ref, state_out = more[:-1] if early else more
    at_origin = (lax.axis_index("lat") == 0) & (lax.axis_index("lon") < 2)

    @pl.when(at_origin if early else jnp.logical_not(at_origin))
    def _():
        interior_kernel(levels, rows, 0, last, t_ref, s_ref, c_ref, m_ref, n_ref, pt_ref, ps_ref, state_out)


def interior_kernel(levels, rows, first, last, t_ref, s_ref, c_ref, m_ref, n_ref, *more):
    if first:
        _, _, _, state_in, pt_ref, ps_ref = more
    else:
        pt_ref, ps_ref, state_out = more
    shape = (levels, LANES)
    level = iota(shape, 0)
    last_lane = iota((1, LANES), 1) == LANES - 1
    factors = level_factors(levels)
    zero = jnp.zeros(shape, F32)

    def step(j, carry):
        prev, m1, d2, limited2, base2, wg2, m2, acc2, acc1 = carry
        t, s, c, m = (strided(ref, j) for ref in (t_ref, s_ref, c_ref, m_ref))
        n = n_ref[pl.ds(j, 1), :]
        here = column_row(t, s, n, factors, level)
        east = shifted(here, -1)
        wet = level < jnp.minimum(n, jnp.where(last_lane, 0, east["n"]))
        steps = [face_step(here, east, wet, q) for q in "ts"]
        base, wg, forward = face_base(here, east, c, wet, steps)
        inside = level < n
        acc = []
        for q, d, flux in zip("ts", steps, base):
            limited = minmod(roll(d, 1), d)
            flux = flux + wg * jnp.where(forward, limited, roll(limited, -1))
            acc.append(jnp.where(inside, here[q], 0.0) + roll(flux, 1) - flux)
        wet = level < jnp.minimum(prev["n"], n)
        d1 = [face_step(prev, here, wet, q) for q in "ts"]
        base1, wg1, _ = face_base(prev, here, m1, wet, d1)
        limited1 = [minmod(x, y) for x, y in zip(d2, d1)]
        forward2 = m2 > 0.0
        flux2 = [b + wg2 * jnp.where(forward2, x, y) for b, x, y in zip(base2, limited2, limited1)]
        done = [x - f for x, f in zip(acc2, flux2)]
        acc1 = [x + f for x, f in zip(acc1, flux2)]
        at = (j + rows - 2) % rows
        put(pt_ref, at, done[0])
        put(ps_ref, at, done[1])
        return here, m, d1, limited1, base1, wg1, m1, acc1, acc

    def pack(carry):
        prev, m1, d2, limited2, base2, wg2, m2, acc2, acc1 = carry
        return [prev[name] for name in NAMES] + [m1, *d2, *limited2, *base2, wg2, m2, *acc2, *acc1]

    def unpack(flat, n):
        prev = dict(zip(NAMES, flat), n=n)
        m1, d2, limited2, base2, wg2, m2, acc2, acc1 = (
            flat[6], flat[7:9], flat[9:11], flat[11:13], flat[13], flat[14], flat[15:17], flat[17:19]
        )
        return prev, m1, d2, limited2, base2, wg2, m2, acc2, acc1

    if first:
        carry = unpack([state_in[i] for i in range(STATE)], n_ref[first - 1 : first, :])
    else:
        carry = unpack([zero] * STATE, jnp.zeros((1, LANES), jnp.int32))

    def block(i, carry):
        for u in range(UNROLL):
            carry = step(first + i * UNROLL + u, carry)
        return carry

    carry = lax.fori_loop(0, (last - first) // UNROLL, block, carry)
    if last < rows:
        for i, value in enumerate(pack(carry)):
            state_out[i] = value
        return
    _, _, _, limited2, base2, wg2, m2, acc2, acc1 = carry
    flux2 = [b + wg2 * jnp.where(m2 > 0.0, x, 0.0) for b, x in zip(base2, limited2)]
    for ref, a2, a1, f in zip((pt_ref, ps_ref), acc2, acc1, flux2):
        put(ref, rows - 2, a2 - f)
        put(ref, rows - 1, a1 + f)


def edge_faces(cells, speeds):
    level = iota(cells[0]["t"].shape, 0).astype(F32)
    wets = [level < jnp.minimum(a["n"], b["n"]) for a, b in zip(cells, cells[1:])]
    d = [[face_step(a, b, w, q) for q in "ts"] for a, b, w in zip(cells, cells[1:], wets)]
    limited = [[minmod(x, y) for x, y in zip(d[i], d[i + 1])] for i in (0, 1)]
    base, wg, forward = face_base(cells[1], cells[2], speeds[1], wets[1], d[1])
    flux = [b + wg * jnp.where(forward, x, y) for b, x, y in zip(base, *limited)]
    first = last = None
    if speeds[0] is not None:
        _, wg0 = weights(speeds[0], wets[0])
        first = [wg0 * jnp.where(speeds[0] > 0.0, 0.0, x) for x in limited[0]]
    if speeds[2] is not None:
        _, wg2 = weights(speeds[2], wets[2])
        last = [wg2 * jnp.where(speeds[2] > 0.0, x, 0.0) for x in limited[1]]
    return first, flux, last


def longitude_kernel(
    levels, rows, lat_size, lon_size, pt_ref, ps_ref, side_ref, near_in, core_in, far_in, t_new, s_new
):
    shape = (levels, LANES)
    lane = iota(shape, 1)
    place = lane % 4
    factors = level_factors(levels)
    K = levels
    is_top = lax.axis_index("lat") == lat_size - 1
    lon_at = lax.axis_index("lon")
    is_odd = lon_at % 2 == 1
    wraps = (lon_at == 0) | (lon_at == lon_size - 1)

    def cell_row(t, s, n):
        return column_row(t, s, n, factors, iota(shape, 0))

    own_t, own_s, own_c = (side_ref[i * K : (i + 1) * K, :] for i in range(3))
    own_n = side_ref[3 * K : 3 * K + 1, :]
    core = core_in[...]
    chip = jnp.where(is_top & ~wraps, near_in[...], far_in[4 * K + 8 :, :])
    west, east = jnp.where(is_odd, core, chip), jnp.where(is_odd, chip, core)
    first_two = place < 2

    def side(t, s, n, speed):
        row = cell_row(t, s, n)
        cells = [row] + [shifted(row, -i) for i in (1, 2, 3)]
        return edge_faces(cells, [roll(speed, -i) for i in range(3)])

    _, west_flux, west_last = side(
        jnp.where(first_two, west[:K], own_t),
        jnp.where(first_two, roll(west[:K], -2), own_s),
        jnp.where(first_two[:1], west[K : K + 1], own_n),
        jnp.where(place == 1, roll(west[K:], -1), own_c),
    )
    east_first, east_flux, _ = side(
        jnp.where(first_two, own_t, east[:K]),
        jnp.where(first_two, own_s, roll(east[:K], 2)),
        jnp.where(first_two[:1], own_n, east[K : K + 1]),
        own_c,
    )
    lon = []
    for fw, lw, fe, le in zip(west_flux, west_last, east_flux, east_first):
        group = jnp.where(
            place == 0,
            -le,
            jnp.where(place == 1, roll(le - fe, 1), jnp.where(place == 2, roll(fw - lw, 2), roll(lw, 3))),
        )
        lon.append(group)

    edge_lanes = (lane >= LANES - 2) | (lane < 2)
    for q, (p_ref, new_ref) in enumerate(((pt_ref, t_new), (ps_ref, s_new))):
        for j in range(rows):
            moved = jnp.where(edge_lanes, roll(lon[q], LANES - 2 - 4 * j), 0.0)
            put(new_ref, j, strided(p_ref, j) + moved)


def latitude_kernel(
    levels, rows, lat_size, lon_size, t_new, s_new, t_ref, s_ref, n_ref, own_ref,
    far_in, below_in, above_in, column_in, relay_in, own_column, t_out, s_out, ends_ref, sems,
):
    shape = (levels, LANES)
    factors = level_factors(levels)
    K = levels
    row_at = lax.axis_index("lat")
    is_top, is_bottom = row_at == lat_size - 1, row_at == 0
    lon_at = lax.axis_index("lon")
    is_odd = lon_at % 2 == 1
    middle = pl.ds(8, rows - 16)
    copies = [
        pltpu.make_async_copy(new_ref.at[:, middle], out_ref.at[:, middle], sems.at[q])
        for q, (new_ref, out_ref) in enumerate(((t_new, t_out), (s_new, s_out)))
    ]
    for copy in copies:
        copy.start()

    def cell_row(t, s, n):
        return column_row(t, s, n, factors, iota(shape, 0))

    counts = n_ref[...].astype(F32)

    def own_row(j):
        return cell_row(strided(t_ref, j), strided(s_ref, j), counts[j : j + 1])

    def sent_row(array, which, at_counts):
        t, s = array[which * K : (which + 1) * K], array[(2 + which) * K : (3 + which) * K]
        return cell_row(t, s, array[at_counts + which : at_counts + which + 1])

    below = jnp.where(is_bottom, 0.0, below_in[...])
    cells = [sent_row(below, 0, 5 * K), sent_row(below, 1, 5 * K), own_row(0), own_row(1)]
    _, south_flux, south_last = edge_faces(cells, [None, below[4 * K : 5 * K], own_ref[:K]])

    pivot = (lon_at * 2) % lon_size == 0
    column = jnp.where(is_odd, relay_in[...], jnp.where(pivot, own_column[: K + 8, :], column_in[: K + 8, :]))
    parts = [roll(column[:K], -i) for i in range(4)] + [column[K : K + 8]]
    fold = far_in[: 4 * K + 8, :]
    fold = jnp.where(iota(fold.shape, 1) == 0, jnp.concatenate(parts, axis=0), fold)
    above = above_in[...]
    above = jnp.where(is_top, fold, jnp.concatenate([above[: 4 * K], above[5 * K :]], axis=0))
    cells = [own_row(rows - 2), own_row(rows - 1), sent_row(above, 0, 4 * K), sent_row(above, 1, 4 * K)]
    north_first, north_flux, _ = edge_faces(cells, [own_ref[K : 2 * K], own_ref[2 * K :], None])

    for q, (new_ref, out_ref) in enumerate(((t_new, t_out), (s_new, s_out))):
        ends = ends_ref.at[q]
        ends[:, :8, :] = new_ref[:, :8, :]
        ends[:, 8:16, :] = new_ref[:, rows - 8 : rows, :]
        extra = {
            0: south_flux[q] - south_last[q],
            1: south_last[q],
            14: -north_first[q],
            15: north_first[q] - north_flux[q],
        }
        for j, value in extra.items():
            put(ends, j, strided(ends, j) + value)
        for i, at in enumerate((0, rows - 8)):
            copy = pltpu.make_async_copy(
                ends.at[:, pl.ds(8 * i, 8)], out_ref.at[:, pl.ds(at, 8)], sems.at[2 + 2 * q + i]
            )
            copy.start()
            copies.append(copy)
    for copy in copies:
        copy.wait()


def body(nlat, nlon, t, s, c, m, n):
    levels, rows, _ = t.shape
    vmem, hbm = pl.BlockSpec(memory_space=pltpu.VMEM), pl.BlockSpec(memory_space=pltpu.HBM)
    f = functools.partial
    out = lambda *shape: jax.ShapeDtypeStruct(shape, F32)
    K = levels
    params = pltpu.CompilerParams(vmem_limit_bytes=VMEM)
    swap = nlat == 2
    field, lat_shape = out(rows, K, LANES), out(5 * K + 8, LANES)
    room = out(levels, rows + SPARE, LANES)
    shapes = [room] * 4 + [jax.ShapeDtypeStruct(n.shape, n.dtype)]
    shapes += [out(3 * K + 8, LANES), out(2 * K, LANES), out(2 * K, LANES), lat_shape, out(6 * K + 8, LANES)]
    shapes += [out(2 * K + 8, LANES), out(3 * K, LANES)]
    shapes += [] if swap else [lat_shape]
    t_v, s_v, c_v, m_v, n_v, side, core, chip, lat, far, column, own, *more = pl.pallas_call(
        f(pack_kernel, levels, rows, nlat),
        out_shape=tuple(shapes),
        in_specs=[hbm] * 5,
        out_specs=(vmem,) * len(shapes),
        scratch_shapes=[pltpu.SemaphoreType.DMA((5,))],
        compiler_params=params,
        name="pack",
    )(*[pltpu.with_memory_space_constraint(x, pltpu.HBM) for x in (t, s, c, m, n)])

    top = nlat - 1

    def exchange(array, top_to, others_to, helper=lambda i: i):
        to = {(j, i): (j, others_to(i)) for j in range(top) for i in range(nlon)}
        for i in range(nlon):
            partner, via = top_to(i), helper(i)
            if partner is not None:
                to[top, i] = (top, partner)
            elif to.get((0, via)) == (0, via ^ 1) and to.get((0, via ^ 1)) == (0, via):
                to[top, i], to[0, via], to[0, via ^ 1] = (0, via), (0, via ^ 1), (top, i)
            else:
                to[top, i] = (top, i)
        pairs = [(i * nlat + j, to[j, i][1] * nlat + to[j, i][0]) for i in range(nlon) for j in range(nlat)]
        return lax.ppermute(array, ("lon", "lat"), pairs)

    def chips(i):
        return (i + (1 if i % 2 else -1)) % nlon

    columns = {i: i ^ 1 if 2 * i % nlon == 0 else nlon - i for i in range(0, nlon, 2)}
    lone = [i for i in range(1, nlon, 2) if columns[i - 1] != i]
    columns |= {i: i - 1 for i in range(1, nlon, 2) if i not in lone}
    for part in ([i for i in lone if 2 * i < nlon], [i for i in lone if 2 * i > nlon]):
        columns |= dict(zip(part, part[1:] + part[:1]))

    middle = HEAD
    fields = (t_v, s_v, c_v, m_v, n_v)
    south_out = (room, room, out(STATE, K, LANES))
    cost = pl.CostEstimate(flops=20_000_000, bytes_accessed=1_000_000, transcendentals=0)
    pt, ps, state, far = pl.pallas_call(
        f(south_kernel, levels, rows, middle, True),
        out_shape=south_out + (out(*far.shape),),
        in_specs=[vmem] * 6,
        out_specs=(vmem,) * 4,
        input_output_aliases={5: 3},
        cost_estimate=cost,
        compiler_params=params,
        name="south_at_origin",
    )(*fields, far)

    ring, rung = range(nlon), range(nlat)
    far_in = exchange(far, lambda i: nlon - 1 - i, chips)
    below_in = above_in = lax.ppermute(lat, "lat", [(i, (i + 1) % nlat) for i in rung])
    if not swap:
        above_in = lax.ppermute(more[0], "lat", [(i, (i - 1) % nlat) for i in rung])
    near_in = exchange(
        chip,
        lambda i: chips(i) if 0 < i < nlon - 1 else None,
        lambda i: i ^ 1,
        lambda i: i + nlon // 4 if i == 0 else i - nlon // 4,
    )
    core_in = lax.ppermute(core, "lon", [(i, i ^ 1) for i in ring])
    column_in = exchange(column, columns.get, lambda i: i ^ 1)

    pt, ps, state = pl.pallas_call(
        f(south_kernel, levels, rows, middle, False),
        out_shape=south_out,
        in_specs=[vmem] * 8,
        out_specs=(vmem,) * 3,
        input_output_aliases={5: 0, 6: 1, 7: 2},
        cost_estimate=cost,
        compiler_params=params,
        name="south_elsewhere",
    )(*fields, pt, ps, state)
    relay = pl.pallas_call(
        relay_kernel,
        out_shape=out(K + 8, LANES),
        in_specs=[vmem] * 2,
        out_specs=vmem,
        compiler_params=params,
        name="relay",
    )(far_in, state)
    relay_in = lax.ppermute(relay, "lon", [(i, i ^ 1) for i in ring])

    pt, ps = pl.pallas_call(
        f(interior_kernel, levels, rows, middle, rows),
        out_shape=(room, room),
        in_specs=[vmem] * 9,
        out_specs=(vmem,) * 2,
        input_output_aliases={5: 0, 6: 1},
        cost_estimate=pl.CostEstimate(flops=20_000_000, bytes_accessed=1_000_000, transcendentals=0),
        compiler_params=params,
        name="interior_north",
    )(*fields, pt, ps, relay, state)

    t_new, s_new = pl.pallas_call(
        f(longitude_kernel, levels, rows, nlat, nlon),
        out_shape=(room, room),
        in_specs=[vmem] * 6,
        out_specs=(vmem,) * 2,
        input_output_aliases={0: 0, 1: 1},
        cost_estimate=pl.CostEstimate(flops=5_000_000, bytes_accessed=1_000_000, transcendentals=0),
        compiler_params=params,
        name="longitude_edges",
    )(pt, ps, side, near_in, core_in, far_in)

    return pl.pallas_call(
        f(latitude_kernel, levels, rows, nlat, nlon),
        out_shape=(out(*t.shape),) * 2,
        in_specs=[vmem] * 12,
        out_specs=(hbm,) * 2,
        scratch_shapes=[pltpu.VMEM((2, K, 24, LANES), F32), pltpu.SemaphoreType.DMA((6,))],
        compiler_params=params,
        name="latitude_edges",
    )(t_new, s_new, t_v, s_v, n_v, own, far_in, below_in, above_in, column_in, relay_in, column)


def solution(mesh):
    spec = P(None, "lat", "lon")
    return jax.shard_map(
        functools.partial(body, mesh.shape["lat"], mesh.shape["lon"]),
        mesh=mesh,
        in_specs=(spec,) * 4 + (P("lat", "lon"),),
        out_specs=(spec,) * 2,
        check_vma=False,
    )
```

```python
import functools

import jax
import jax.numpy as jnp
from jax import lax
from jax.experimental import pallas as pl
from jax.experimental.pallas import tpu as pltpu
from jax.sharding import PartitionSpec as P

heat_swelling_alpha = 0.1655
coef_beta = 0.76554
cabbeling_parameter = 0.05952
lambda_salt = 0.00054914
thermobaric_parameter = 0.0001497
press_salt = 1.109e-05
cross_coupling_contribution = 0.0024341
total_depth = 5000.0
kappa_iso = 0.1
strat_min = 0.1

LANES = 128
VMEM = 8 * 1024 * 1024
UNROLL = 8
HEAD = 24
SPARE = 8
F32 = jnp.float32


def iota(shape, axis):
    return lax.broadcasted_iota(jnp.int32, shape, axis)


def roll(array, shift, axis=1):
    size = array.shape[axis]
    return pltpu.roll(array, shift % size, axis)


def minmod(x, y):
    return jnp.maximum(jnp.minimum(x, jnp.maximum(y, 0.0)), jnp.minimum(y, 0.0))


def level_factors(levels):
    depth = total_depth * (iota((levels, LANES), 0).astype(F32) + 0.5) / levels
    heat = -heat_swelling_alpha * (1.0 + thermobaric_parameter * depth)
    salt = coef_beta * (1.0 - press_salt * depth)
    return heat, salt


def density(t, s, factors):
    heat, salt = factors
    return t * (
        heat
        - (0.5 * heat_swelling_alpha * cabbeling_parameter) * t
        - cross_coupling_contribution * s
    ) + s * (salt - (0.5 * coef_beta * lambda_salt) * s)


def vertical(q, level):
    levels = q.shape[0]
    step = roll(q, -1, 0) - q
    below = roll(step, 1, 0)
    return jnp.where(level == levels - 1, below, step) + jnp.where(level == 0, step, below)


def column_row(t, s, n, factors, level):
    r = density(t, s, factors)
    return {
        "t": t,
        "s": s,
        "r": r,
        "tz": vertical(t, level),
        "sz": vertical(s, level),
        "rz": vertical(r, level),
        "n": n,
    }


def shifted(row, by):
    return {name: roll(value, by) for name, value in row.items()}


def weights(c, wet):
    size = jnp.abs(c)
    return jnp.where(wet, c, 0.0), jnp.where(wet, 0.5 * (size - c * c), 0.0)


def face_step(a, b, wet, name):
    return jnp.where(wet, b[name] - a[name], 0.0)


def face_base(a, b, c, wet, steps):
    wc, wg = weights(c, wet)
    steep = (a["r"] - b["r"]) / jnp.maximum(a["rz"] + b["rz"], 4.0 * strat_min)
    tilt = jnp.where(wet, jnp.clip(steep, -0.25, 0.25), 0.0) * (-kappa_iso)
    forward = c > 0.0
    base = [
        wc * jnp.where(forward, a[q], b[q]) - kappa_iso * d + tilt * (a[q + "z"] + b[q + "z"])
        for q, d in zip("ts", steps)
    ]
    return base, wg, forward


def strided(ref, row):
    levels, rows, _ = ref.shape
    return ref.reshape(levels * rows, LANES)[pl.ds(row, levels, stride=rows), :]


def put(ref, row, value):
    levels, rows, _ = ref.shape
    ref.reshape(levels * rows, LANES)[pl.ds(row, levels, stride=rows), :] = value


def pack_kernel(
    levels, rows, lat_size, t_hbm, s_hbm, c_hbm, m_hbm, n_hbm,
    t_ref, s_ref, c_ref, m_ref, n_ref, side_ref, core_ref, chip_ref, lat_ref, far_ref, column_ref, own_ref, *more,
):
    *more, sems = more
    K = levels
    pairs = ((t_hbm, t_ref), (s_hbm, s_ref), (n_hbm, n_ref), (c_hbm, c_ref), (m_hbm, m_ref))
    pairs = [(src, dst if dst is n_ref else dst.at[:, :rows]) for src, dst in pairs]
    copies = [pltpu.make_async_copy(src, dst, sems.at[i]) for i, (src, dst) in enumerate(pairs)]
    for copy in copies:
        copy.start()
    lane = iota((levels, LANES), 1)
    group = lane // 4

    group = lane // 4

    def gather(ref):
        out = jnp.zeros((levels, LANES), F32)
        for j in range(rows):
            out = jnp.where(group == j, roll(strided(ref, j), 4 * j + 2), out)
        return out

    def mirrored(x):
        index = (LANES - iota(x.shape, 1)) % LANES
        return jnp.take_along_axis(x, index, axis=1)

    def tracer_rows(out_ref, tracer, ref, picks, change=lambda x: x):
        for i, j in enumerate(picks):
            at = (2 * tracer + i) * K
            out_ref[at : at + K, :] = change(strided(ref, j))

    south, north, fold = (0, 1), (rows - 2, rows - 1), (rows - 2, rows - 3)
    is_top = lax.axis_index("lat") == lat_size - 1
    is_odd = lax.axis_index("lon") % 2 == 1
    place = iota((levels, LANES), 1) % 4
    sides = []
    for tracer, ref in enumerate((t_ref, s_ref)):
        copies[tracer].wait()
        sides.append(gather(ref))
        tracer_rows(far_ref, tracer, ref, fold, mirrored)
        if more:
            tracer_rows(lat_ref, tracer, ref, north)
            tracer_rows(more[0], tracer, ref, south)
        else:
            for i in range(2):
                at = (2 * tracer + i) * K
                lat_ref[at : at + K, :] = jnp.where(is_top, strided(ref, south[i]), strided(ref, north[i]))

    copies[3].wait()
    sides.append(gather(c_ref))
    copies[2].wait()
    counts = n_ref[...].astype(F32)
    line = jnp.zeros((8, LANES), F32)
    for at in range(0, rows, 8):
        moved = pltpu.roll(counts[at : at + 8], 4 * at + 2, 1, stride=4, stride_axis=0)
        mine = iota((8, LANES), 1) // 4 == iota((8, LANES), 0) + at
        line = jnp.where(mine, moved, line)
    line = jnp.sum(line, axis=0, keepdims=True)
    heat, salt, speed = sides
    line = jnp.broadcast_to(line, (levels, LANES))
    for i, value in enumerate((heat, salt, speed)):
        side_ref[i * K : (i + 1) * K, :] = value
    side_ref[3 * K :, :] = line[:8]
    to_east = jnp.where(place < 2, heat, roll(salt, 2)), jnp.where(place == 2, roll(speed, 1), line)
    to_west = jnp.where(place < 2, roll(salt, -2), heat), line
    for i, (e, w) in enumerate(zip(to_east, to_west)):
        core_ref[i * K : (i + 1) * K, :] = jnp.where(is_odd, w, e)
        chip = jnp.where(is_odd, e, w)
        chip_ref[i * K : (i + 1) * K, :] = chip
        far_ref[4 * K + 8 + i * K : 4 * K + 8 + (i + 1) * K, :] = chip

    def tally(picks):
        return jnp.concatenate(
            [counts[j : j + 1] for j in picks] + [jnp.zeros((8 - len(picks), LANES), F32)], axis=0
        )

    far_ref[4 * K : 4 * K + 8, :] = mirrored(tally(fold))
    first = jnp.zeros((levels, LANES), F32)
    for i, (ref, j) in enumerate((ref, j) for ref in (t_ref, s_ref) for j in fold):
        first = jnp.where(lane == i, roll(strided(ref, j), i), first)
    column_ref[:K, :] = first
    column_ref[K : K + 8, :] = tally(fold)
    if more:
        lat_ref[5 * K :, :] = tally(north)
        more[0][4 * K : 5 * K, :] = jnp.zeros((K, LANES), F32)
        more[0][5 * K :, :] = tally(south)
    else:
        lat_ref[5 * K :, :] = jnp.where(is_top, tally(south), tally(north))
    copies[4].wait()
    lat_ref[4 * K : 5 * K, :] = strided(m_ref, rows - 1)
    for i, j in enumerate((0, rows - 2, rows - 1)):
        own_ref[i * K : (i + 1) * K, :] = strided(m_ref, j)


def relay_kernel(far_ref, _, out_ref):
    K = out_ref.shape[0] - 8
    lane = iota((K, LANES), 1)
    out = far_ref[:K, :]
    for i in (1, 2, 3):
        out = jnp.where(lane == i, roll(far_ref[i * K : (i + 1) * K, :], i), out)
    out_ref[:K, :] = out
    out_ref[K:, :] = far_ref[4 * K : 4 * K + 8, :]


NAMES = ("t", "s", "r", "tz", "sz", "rz")
STATE = 19


def south_kernel(levels, rows, last, early, t_ref, s_ref, c_ref, m_ref, n_ref, *more):
    *more, pt_ref, ps_ref, state_out = more[:-1] if early else more
    at_origin = (lax.axis_index("lat") == 0) & (lax.axis_index("lon") < 2)

    @pl.when(at_origin if early else jnp.logical_not(at_origin))
    def _():
        interior_kernel(levels, rows, 0, last, t_ref, s_ref, c_ref, m_ref, n_ref, pt_ref, ps_ref, state_out)


def interior_kernel(levels, rows, first, last, t_ref, s_ref, c_ref, m_ref, n_ref, *more):
    if first:
        _, _, _, state_in, pt_ref, ps_ref = more
    else:
        pt_ref, ps_ref, state_out = more
    shape = (levels, LANES)
    level = iota(shape, 0)
    last_lane = iota((1, LANES), 1) == LANES - 1
    factors = level_factors(levels)
    zero = jnp.zeros(shape, F32)

    def step(j, carry):
        prev, m1, d2, limited2, base2, wg2, m2, acc2, acc1 = carry
        t, s, c, m = (strided(ref, j) for ref in (t_ref, s_ref, c_ref, m_ref))
        n = n_ref[pl.ds(j, 1), :]
        here = column_row(t, s, n, factors, level)
        east = shifted(here, -1)
        wet = level < jnp.minimum(n, jnp.where(last_lane, 0, east["n"]))
        steps = [face_step(here, east, wet, q) for q in "ts"]
        base, wg, forward = face_base(here, east, c, wet, steps)
        inside = level < n
        acc = []
        for q, d, flux in zip("ts", steps, base):
            limited = minmod(roll(d, 1), d)
            flux = flux + wg * jnp.where(forward, limited, roll(limited, -1))
            acc.append(jnp.where(inside, here[q], 0.0) + roll(flux, 1) - flux)
        wet = level < jnp.minimum(prev["n"], n)
        d1 = [face_step(prev, here, wet, q) for q in "ts"]
        base1, wg1, _ = face_base(prev, here, m1, wet, d1)
        limited1 = [minmod(x, y) for x, y in zip(d2, d1)]
        forward2 = m2 > 0.0
        flux2 = [b + wg2 * jnp.where(forward2, x, y) for b, x, y in zip(base2, limited2, limited1)]
        done = [x - f for x, f in zip(acc2, flux2)]
        acc1 = [x + f for x, f in zip(acc1, flux2)]
        at = (j + rows - 2) % rows
        put(pt_ref, at, done[0])
        put(ps_ref, at, done[1])
        return here, m, d1, limited1, base1, wg1, m1, acc1, acc

    def pack(carry):
        prev, m1, d2, limited2, base2, wg2, m2, acc2, acc1 = carry
        return [prev[name] for name in NAMES] + [m1, *d2, *limited2, *base2, wg2, m2, *acc2, *acc1]

    def unpack(flat, n):
        prev = dict(zip(NAMES, flat), n=n)
        m1, d2, limited2, base2, wg2, m2, acc2, acc1 = (
            flat[6], flat[7:9], flat[9:11], flat[11:13], flat[13], flat[14], flat[15:17], flat[17:19]
        )
        return prev, m1, d2, limited2, base2, wg2, m2, acc2, acc1

    if first:
        carry = unpack([state_in[i] for i in range(STATE)], n_ref[first - 1 : first, :])
    else:
        carry = unpack([zero] * STATE, jnp.zeros((1, LANES), jnp.int32))

    def block(i, carry):
        for u in range(UNROLL):
            carry = step(first + i * UNROLL + u, carry)
        return carry

    carry = lax.fori_loop(0, (last - first) // UNROLL, block, carry)
    if last < rows:
        for i, value in enumerate(pack(carry)):
            state_out[i] = value
        return
    _, _, _, limited2, base2, wg2, m2, acc2, acc1 = carry
    flux2 = [b + wg2 * jnp.where(m2 > 0.0, x, 0.0) for b, x in zip(base2, limited2)]
    for ref, a2, a1, f in zip((pt_ref, ps_ref), acc2, acc1, flux2):
        put(ref, rows - 2, a2 - f)
        put(ref, rows - 1, a1 + f)


def edge_faces(cells, speeds):
    level = iota(cells[0]["t"].shape, 0).astype(F32)
    wets = [level < jnp.minimum(a["n"], b["n"]) for a, b in zip(cells, cells[1:])]
    d = [[face_step(a, b, w, q) for q in "ts"] for a, b, w in zip(cells, cells[1:], wets)]
    limited = [[minmod(x, y) for x, y in zip(d[i], d[i + 1])] for i in (0, 1)]
    base, wg, forward = face_base(cells[1], cells[2], speeds[1], wets[1], d[1])
    flux = [b + wg * jnp.where(forward, x, y) for b, x, y in zip(base, *limited)]
    first = last = None
    if speeds[0] is not None:
        _, wg0 = weights(speeds[0], wets[0])
        first = [wg0 * jnp.where(speeds[0] > 0.0, 0.0, x) for x in limited[0]]
    if speeds[2] is not None:
        _, wg2 = weights(speeds[2], wets[2])
        last = [wg2 * jnp.where(speeds[2] > 0.0, x, 0.0) for x in limited[1]]
    return first, flux, last


def longitude_kernel(
    levels, rows, lat_size, lon_size, pt_ref, ps_ref, side_ref, near_in, core_in, far_in, t_new, s_new
):
    shape = (levels, LANES)
    lane = iota(shape, 1)
    place = lane % 4
    factors = level_factors(levels)
    K = levels
    is_top = lax.axis_index("lat") == lat_size - 1
    lon_at = lax.axis_index("lon")
    is_odd = lon_at % 2 == 1
    wraps = (lon_at == 0) | (lon_at == lon_size - 1)

    def cell_row(t, s, n):
        return column_row(t, s, n, factors, iota(shape, 0))

    own_t, own_s, own_c = (side_ref[i * K : (i + 1) * K, :] for i in range(3))
    own_n = side_ref[3 * K : 3 * K + 1, :]
    core = core_in[...]
    chip = jnp.where(is_top & ~wraps, near_in[...], far_in[4 * K + 8 :, :])
    west, east = jnp.where(is_odd, core, chip), jnp.where(is_odd, chip, core)
    first_two = place < 2

    def side(t, s, n, speed):
        row = cell_row(t, s, n)
        cells = [row] + [shifted(row, -i) for i in (1, 2, 3)]
        return edge_faces(cells, [roll(speed, -i) for i in range(3)])

    _, west_flux, west_last = side(
        jnp.where(first_two, west[:K], own_t),
        jnp.where(first_two, roll(west[:K], -2), own_s),
        jnp.where(first_two[:1], west[K : K + 1], own_n),
        jnp.where(place == 1, roll(west[K:], -1), own_c),
    )
    east_first, east_flux, _ = side(
        jnp.where(first_two, own_t, east[:K]),
        jnp.where(first_two, own_s, roll(east[:K], 2)),
        jnp.where(first_two[:1], own_n, east[K : K + 1]),
        own_c,
    )
    lon = []
    for fw, lw, fe, le in zip(west_flux, west_last, east_flux, east_first):
        group = jnp.where(
            place == 0,
            -le,
            jnp.where(place == 1, roll(le - fe, 1), jnp.where(place == 2, roll(fw - lw, 2), roll(lw, 3))),
        )
        lon.append(group)

    edge_lanes = (lane >= LANES - 2) | (lane < 2)
    for q, (p_ref, new_ref) in enumerate(((pt_ref, t_new), (ps_ref, s_new))):
        for j in range(rows):
            moved = jnp.where(edge_lanes, roll(lon[q], LANES - 2 - 4 * j), 0.0)
            put(new_ref, j, strided(p_ref, j) + moved)


def latitude_kernel(
    levels, rows, lat_size, lon_size, t_new, s_new, t_ref, s_ref, n_ref, own_ref,
    far_in, below_in, above_in, column_in, relay_in, own_column, t_out, s_out, ends_ref, sems,
):
    shape = (levels, LANES)
    factors = level_factors(levels)
    K = levels
    row_at = lax.axis_index("lat")
    is_top, is_bottom = row_at == lat_size - 1, row_at == 0
    lon_at = lax.axis_index("lon")
    is_odd = lon_at % 2 == 1
    middle = pl.ds(8, rows - 16)
    copies = [
        pltpu.make_async_copy(new_ref.at[:, middle], out_ref.at[:, middle], sems.at[q])
        for q, (new_ref, out_ref) in enumerate(((t_new, t_out), (s_new, s_out)))
    ]
    for copy in copies:
        copy.start()

    def cell_row(t, s, n):
        return column_row(t, s, n, factors, iota(shape, 0))

    counts = n_ref[...].astype(F32)

    def own_row(j):
        return cell_row(strided(t_ref, j), strided(s_ref, j), counts[j : j + 1])

    def sent_row(array, which, at_counts):
        t, s = array[which * K : (which + 1) * K], array[(2 + which) * K : (3 + which) * K]
        return cell_row(t, s, array[at_counts + which : at_counts + which + 1])

    below = jnp.where(is_bottom, 0.0, below_in[...])
    cells = [sent_row(below, 0, 5 * K), sent_row(below, 1, 5 * K), own_row(0), own_row(1)]
    _, south_flux, south_last = edge_faces(cells, [None, below[4 * K : 5 * K], own_ref[:K]])

    pivot = (lon_at * 2) % lon_size == 0
    column = jnp.where(is_odd, relay_in[...], jnp.where(pivot, own_column[: K + 8, :], column_in[: K + 8, :]))
    parts = [roll(column[:K], -i) for i in range(4)] + [column[K : K + 8]]
    fold = far_in[: 4 * K + 8, :]
    fold = jnp.where(iota(fold.shape, 1) == 0, jnp.concatenate(parts, axis=0), fold)
    above = above_in[...]
    above = jnp.where(is_top, fold, jnp.concatenate([above[: 4 * K], above[5 * K :]], axis=0))
    cells = [own_row(rows - 2), own_row(rows - 1), sent_row(above, 0, 4 * K), sent_row(above, 1, 4 * K)]
    north_first, north_flux, _ = edge_faces(cells, [own_ref[K : 2 * K], own_ref[2 * K :], None])

    for q, (new_ref, out_ref) in enumerate(((t_new, t_out), (s_new, s_out))):
        ends = ends_ref.at[q]
        ends[:, :8, :] = new_ref[:, :8, :]
        ends[:, 8:16, :] = new_ref[:, rows - 8 : rows, :]
        extra = {
            0: south_flux[q] - south_last[q],
            1: south_last[q],
            14: -north_first[q],
            15: north_first[q] - north_flux[q],
        }
        for j, value in extra.items():
            put(ends, j, strided(ends, j) + value)
        for i, at in enumerate((0, rows - 8)):
            copy = pltpu.make_async_copy(
                ends.at[:, pl.ds(8 * i, 8)], out_ref.at[:, pl.ds(at, 8)], sems.at[2 + 2 * q + i]
            )
            copy.start()
            copies.append(copy)
    for copy in copies:
        copy.wait()


def body(nlat, nlon, t, s, c, m, n):
    levels, rows, _ = t.shape
    vmem, hbm = pl.BlockSpec(memory_space=pltpu.VMEM), pl.BlockSpec(memory_space=pltpu.HBM)
    f = functools.partial
    out = lambda *shape: jax.ShapeDtypeStruct(shape, F32)
    K = levels
    params = pltpu.CompilerParams(vmem_limit_bytes=VMEM)
    swap = nlat == 2
    field, lat_shape = out(rows, K, LANES), out(5 * K + 8, LANES)
    room = out(levels, rows + SPARE, LANES)
    shapes = [room] * 4 + [jax.ShapeDtypeStruct(n.shape, n.dtype)]
    shapes += [out(3 * K + 8, LANES), out(2 * K, LANES), out(2 * K, LANES), lat_shape, out(6 * K + 8, LANES)]
    shapes += [out(2 * K + 8, LANES), out(3 * K, LANES)]
    shapes += [] if swap else [lat_shape]
    t_v, s_v, c_v, m_v, n_v, side, core, chip, lat, far, column, own, *more = pl.pallas_call(
        f(pack_kernel, levels, rows, nlat),
        out_shape=tuple(shapes),
        in_specs=[hbm] * 5,
        out_specs=(vmem,) * len(shapes),
        scratch_shapes=[pltpu.SemaphoreType.DMA((5,))],
        compiler_params=params,
        name="pack",
    )(*[pltpu.with_memory_space_constraint(x, pltpu.HBM) for x in (t, s, c, m, n)])

    top = nlat - 1

    def exchange(array, top_to, others_to, helper=lambda i: i):
        to = {(j, i): (j, others_to(i)) for j in range(top) for i in range(nlon)}
        for i in range(nlon):
            partner, via = top_to(i), helper(i)
            if partner is not None:
                to[top, i] = (top, partner)
            elif to.get((0, via)) == (0, via ^ 1) and to.get((0, via ^ 1)) == (0, via):
                to[top, i], to[0, via], to[0, via ^ 1] = (0, via), (0, via ^ 1), (top, i)
            else:
                to[top, i] = (top, i)
        pairs = [(i * nlat + j, to[j, i][1] * nlat + to[j, i][0]) for i in range(nlon) for j in range(nlat)]
        return lax.ppermute(array, ("lon", "lat"), pairs)

    def chips(i):
        return (i + (1 if i % 2 else -1)) % nlon

    columns = {i: i ^ 1 if 2 * i % nlon == 0 else nlon - i for i in range(0, nlon, 2)}
    lone = [i for i in range(1, nlon, 2) if columns[i - 1] != i]
    columns |= {i: i - 1 for i in range(1, nlon, 2) if i not in lone}
    for part in ([i for i in lone if 2 * i < nlon], [i for i in lone if 2 * i > nlon]):
        columns |= dict(zip(part, part[1:] + part[:1]))

    middle = HEAD
    fields = (t_v, s_v, c_v, m_v, n_v)
    south_out = (room, room, out(STATE, K, LANES))
    cost = pl.CostEstimate(flops=20_000_000, bytes_accessed=1_000_000, transcendentals=0)
    pt, ps, state, far = pl.pallas_call(
        f(south_kernel, levels, rows, middle, True),
        out_shape=south_out + (out(*far.shape),),
        in_specs=[vmem] * 6,
        out_specs=(vmem,) * 4,
        input_output_aliases={5: 3},
        cost_estimate=cost,
        compiler_params=params,
        name="south_at_origin",
    )(*fields, far)

    ring, rung = range(nlon), range(nlat)
    far_in = exchange(far, lambda i: nlon - 1 - i, chips)
    below_in = above_in = lax.ppermute(lat, "lat", [(i, (i + 1) % nlat) for i in rung])
    if not swap:
        above_in = lax.ppermute(more[0], "lat", [(i, (i - 1) % nlat) for i in rung])
    near_in = exchange(
        chip,
        lambda i: chips(i) if 0 < i < nlon - 1 else None,
        lambda i: i ^ 1,
        lambda i: i + nlon // 4 if i == 0 else i - nlon // 4,
    )
    core_in = lax.ppermute(core, "lon", [(i, i ^ 1) for i in ring])
    column_in = exchange(column, columns.get, lambda i: i ^ 1)

    pt, ps, state = pl.pallas_call(
        f(south_kernel, levels, rows, middle, False),
        out_shape=south_out,
        in_specs=[vmem] * 8,
        out_specs=(vmem,) * 3,
        input_output_aliases={5: 0, 6: 1, 7: 2},
        cost_estimate=cost,
        compiler_params=params,
        name="south_elsewhere",
    )(*fields, pt, ps, state)
    relay = pl.pallas_call(
        relay_kernel,
        out_shape=out(K + 8, LANES),
        in_specs=[vmem] * 2,
        out_specs=vmem,
        compiler_params=params,
        name="relay",
    )(far_in, state)
    relay_in = lax.ppermute(relay, "lon", [(i, i ^ 1) for i in ring])

    pt, ps = pl.pallas_call(
        f(interior_kernel, levels, rows, middle, rows),
        out_shape=(room, room),
        in_specs=[vmem] * 9,
        out_specs=(vmem,) * 2,
        input_output_aliases={5: 0, 6: 1},
        cost_estimate=pl.CostEstimate(flops=20_000_000, bytes_accessed=1_000_000, transcendentals=0),
        compiler_params=params,
        name="interior_north",
    )(*fields, pt, ps, relay, state)

    t_new, s_new = pl.pallas_call(
        f(longitude_kernel, levels, rows, nlat, nlon),
        out_shape=(room, room),
        in_specs=[vmem] * 6,
        out_specs=(vmem,) * 2,
        input_output_aliases={0: 0, 1: 1},
        cost_estimate=pl.CostEstimate(flops=5_000_000, bytes_accessed=1_000_000, transcendentals=0),
        compiler_params=params,
        name="longitude_edges",
    )(pt, ps, side, near_in, core_in, far_in)

    return pl.pallas_call(
        f(latitude_kernel, levels, rows, nlat, nlon),
        out_shape=(out(*t.shape),) * 2,
        in_specs=[vmem] * 12,
        out_specs=(hbm,) * 2,
        scratch_shapes=[pltpu.VMEM((2, K, 24, LANES), F32), pltpu.SemaphoreType.DMA((6,))],
        compiler_params=params,
        name="latitude_edges",
    )(t_new, s_new, t_v, s_v, n_v, own, far_in, below_in, above_in, column_in, relay_in, column)


def solution(mesh):
    spec = P(None, "lat", "lon")
    return jax.shard_map(
        functools.partial(body, mesh.shape["lat"], mesh.shape["lon"]),
        mesh=mesh,
        in_specs=(spec,) * 4 + (P("lat", "lon"),),
        out_specs=(spec,) * 2,
        check_vma=False,
    )
```

```python
import functools

import jax
import jax.numpy as jnp
from jax import lax
from jax.experimental import pallas as pl
from jax.experimental.pallas import tpu as pltpu
from jax.sharding import PartitionSpec as P

heat_swelling_alpha = 0.1655
coef_beta = 0.76554
cabbeling_parameter = 0.05952
lambda_salt = 0.00054914
thermobaric_parameter = 0.0001497
press_salt = 1.109e-05
cross_coupling_contribution = 0.0024341
total_depth = 5000.0
kappa_iso = 0.1
strat_min = 0.1

LANES = 128
VMEM = 8 * 1024 * 1024
UNROLL = 8
HEAD = 16
SPARE = 8
F32 = jnp.float32


def iota(shape, axis):
    return lax.broadcasted_iota(jnp.int32, shape, axis)


def roll(array, shift, axis=1):
    size = array.shape[axis]
    return pltpu.roll(array, shift % size, axis)


def minmod(x, y):
    return jnp.maximum(jnp.minimum(x, jnp.maximum(y, 0.0)), jnp.minimum(y, 0.0))


def level_factors(levels):
    depth = total_depth * (iota((levels, LANES), 0).astype(F32) + 0.5) / levels
    heat = -heat_swelling_alpha * (1.0 + thermobaric_parameter * depth)
    salt = coef_beta * (1.0 - press_salt * depth)
    return heat, salt


def density(t, s, factors):
    heat, salt = factors
    return t * (
        heat
        - (0.5 * heat_swelling_alpha * cabbeling_parameter) * t
        - cross_coupling_contribution * s
    ) + s * (salt - (0.5 * coef_beta * lambda_salt) * s)


def vertical(q, level):
    levels = q.shape[0]
    step = roll(q, -1, 0) - q
    below = roll(step, 1, 0)
    return jnp.where(level == levels - 1, below, step) + jnp.where(level == 0, step, below)


def column_row(t, s, n, factors, level):
    r = density(t, s, factors)
    return {
        "t": t,
        "s": s,
        "r": r,
        "tz": vertical(t, level),
        "sz": vertical(s, level),
        "rz": vertical(r, level),
        "n": n,
    }


def shifted(row, by):
    return {name: roll(value, by) for name, value in row.items()}


def weights(c, wet):
    size = jnp.abs(c)
    return jnp.where(wet, c, 0.0), jnp.where(wet, 0.5 * (size - c * c), 0.0)


def face_step(a, b, wet, name):
    return jnp.where(wet, b[name] - a[name], 0.0)


def face_base(a, b, c, wet, steps):
    wc, wg = weights(c, wet)
    steep = (a["r"] - b["r"]) / jnp.maximum(a["rz"] + b["rz"], 4.0 * strat_min)
    tilt = jnp.where(wet, jnp.clip(steep, -0.25, 0.25), 0.0) * (-kappa_iso)
    forward = c > 0.0
    base = [
        wc * jnp.where(forward, a[q], b[q]) - kappa_iso * d + tilt * (a[q + "z"] + b[q + "z"])
        for q, d in zip("ts", steps)
    ]
    return base, wg, forward


def strided(ref, row):
    levels, rows, _ = ref.shape
    return ref.reshape(levels * rows, LANES)[pl.ds(row, levels, stride=rows), :]


def put(ref, row, value):
    levels, rows, _ = ref.shape
    ref.reshape(levels * rows, LANES)[pl.ds(row, levels, stride=rows), :] = value


def pack_kernel(
    levels, rows, lat_size, t_hbm, s_hbm, c_hbm, m_hbm, n_hbm,
    t_ref, s_ref, c_ref, m_ref, n_ref, side_ref, core_ref, chip_ref, lat_ref, far_ref, column_ref, own_ref, *more,
):
    *more, sems = more
    K = levels
    pairs = ((t_hbm, t_ref), (s_hbm, s_ref), (n_hbm, n_ref), (c_hbm, c_ref), (m_hbm, m_ref))
    pairs = [(src, dst if dst is n_ref else dst.at[:, :rows]) for src, dst in pairs]
    copies = [pltpu.make_async_copy(src, dst, sems.at[i]) for i, (src, dst) in enumerate(pairs)]
    for copy in copies:
        copy.start()
    lane = iota((levels, LANES), 1)
    group = lane // 4

    group = lane // 4

    def gather(ref):
        out = jnp.zeros((levels, LANES), F32)
        for j in range(rows):
            out = jnp.where(group == j, roll(strided(ref, j), 4 * j + 2), out)
        return out

    def mirrored(x):
        index = (LANES - iota(x.shape, 1)) % LANES
        return jnp.take_along_axis(x, index, axis=1)

    def tracer_rows(out_ref, tracer, ref, picks, change=lambda x: x):
        for i, j in enumerate(picks):
            at = (2 * tracer + i) * K
            out_ref[at : at + K, :] = change(strided(ref, j))

    south, north, fold = (0, 1), (rows - 2, rows - 1), (rows - 2, rows - 3)
    is_top = lax.axis_index("lat") == lat_size - 1
    is_odd = lax.axis_index("lon") % 2 == 1
    place = iota((levels, LANES), 1) % 4
    sides = []
    for tracer, ref in enumerate((t_ref, s_ref)):
        copies[tracer].wait()
        sides.append(gather(ref))
        tracer_rows(far_ref, tracer, ref, fold, mirrored)
        if more:
            tracer_rows(lat_ref, tracer, ref, north)
            tracer_rows(more[0], tracer, ref, south)
        else:
            for i in range(2):
                at = (2 * tracer + i) * K
                lat_ref[at : at + K, :] = jnp.where(is_top, strided(ref, south[i]), strided(ref, north[i]))

    copies[3].wait()
    sides.append(gather(c_ref))
    copies[2].wait()
    counts = n_ref[...].astype(F32)
    line = jnp.zeros((8, LANES), F32)
    for at in range(0, rows, 8):
        moved = pltpu.roll(counts[at : at + 8], 4 * at + 2, 1, stride=4, stride_axis=0)
        mine = iota((8, LANES), 1) // 4 == iota((8, LANES), 0) + at
        line = jnp.where(mine, moved, line)
    line = jnp.sum(line, axis=0, keepdims=True)
    heat, salt, speed = sides
    line = jnp.broadcast_to(line, (levels, LANES))
    for i, value in enumerate((heat, salt, speed)):
        side_ref[i * K : (i + 1) * K, :] = value
    side_ref[3 * K :, :] = line[:8]
    to_east = jnp.where(place < 2, heat, roll(salt, 2)), jnp.where(place == 2, roll(speed, 1), line)
    to_west = jnp.where(place < 2, roll(salt, -2), heat), line
    for i, (e, w) in enumerate(zip(to_east, to_west)):
        core_ref[i * K : (i + 1) * K, :] = jnp.where(is_odd, w, e)
        chip = jnp.where(is_odd, e, w)
        chip_ref[i * K : (i + 1) * K, :] = chip
        far_ref[4 * K + 8 + i * K : 4 * K + 8 + (i + 1) * K, :] = chip

    def tally(picks):
        return jnp.concatenate(
            [counts[j : j + 1] for j in picks] + [jnp.zeros((8 - len(picks), LANES), F32)], axis=0
        )

    far_ref[4 * K : 4 * K + 8, :] = mirrored(tally(fold))
    first = jnp.zeros((levels, LANES), F32)
    for i, (ref, j) in enumerate((ref, j) for ref in (t_ref, s_ref) for j in fold):
        first = jnp.where(lane == i, roll(strided(ref, j), i), first)
    column_ref[:K, :] = first
    column_ref[K : K + 8, :] = tally(fold)
    if more:
        lat_ref[5 * K :, :] = tally(north)
        more[0][4 * K : 5 * K, :] = jnp.zeros((K, LANES), F32)
        more[0][5 * K :, :] = tally(south)
    else:
        lat_ref[5 * K :, :] = jnp.where(is_top, tally(south), tally(north))
    copies[4].wait()
    lat_ref[4 * K : 5 * K, :] = strided(m_ref, rows - 1)
    for i, j in enumerate((0, rows - 2, rows - 1)):
        own_ref[i * K : (i + 1) * K, :] = strided(m_ref, j)


def relay_kernel(far_ref, _, out_ref):
    K = out_ref.shape[0] - 8
    lane = iota((K, LANES), 1)
    out = far_ref[:K, :]
    for i in (1, 2, 3):
        out = jnp.where(lane == i, roll(far_ref[i * K : (i + 1) * K, :], i), out)
    out_ref[:K, :] = out
    out_ref[K:, :] = far_ref[4 * K : 4 * K + 8, :]


NAMES = ("t", "s", "r", "tz", "sz", "rz")
STATE = 19


def south_kernel(levels, rows, last, early, t_ref, s_ref, c_ref, m_ref, n_ref, *more):
    *more, pt_ref, ps_ref, state_out = more[:-1] if early else more
    at_origin = (lax.axis_index("lat") == 0) & (lax.axis_index("lon") < 2)

    @pl.when(at_origin if early else jnp.logical_not(at_origin))
    def _():
        interior_kernel(levels, rows, 0, last, t_ref, s_ref, c_ref, m_ref, n_ref, pt_ref, ps_ref, state_out)


def interior_kernel(levels, rows, first, last, t_ref, s_ref, c_ref, m_ref, n_ref, *more):
    if first:
        _, _, _, state_in, pt_ref, ps_ref = more
    else:
        pt_ref, ps_ref, state_out = more
    shape = (levels, LANES)
    level = iota(shape, 0)
    last_lane = iota((1, LANES), 1) == LANES - 1
    factors = level_factors(levels)
    zero = jnp.zeros(shape, F32)

    def step(j, carry):
        prev, m1, d2, limited2, base2, wg2, m2, acc2, acc1 = carry
        t, s, c, m = (strided(ref, j) for ref in (t_ref, s_ref, c_ref, m_ref))
        n = n_ref[pl.ds(j, 1), :]
        here = column_row(t, s, n, factors, level)
        east = shifted(here, -1)
        wet = level < jnp.minimum(n, jnp.where(last_lane, 0, east["n"]))
        steps = [face_step(here, east, wet, q) for q in "ts"]
        base, wg, forward = face_base(here, east, c, wet, steps)
        inside = level < n
        acc = []
        for q, d, flux in zip("ts", steps, base):
            limited = minmod(roll(d, 1), d)
            flux = flux + wg * jnp.where(forward, limited, roll(limited, -1))
            acc.append(jnp.where(inside, here[q], 0.0) + roll(flux, 1) - flux)
        wet = level < jnp.minimum(prev["n"], n)
        d1 = [face_step(prev, here, wet, q) for q in "ts"]
        base1, wg1, _ = face_base(prev, here, m1, wet, d1)
        limited1 = [minmod(x, y) for x, y in zip(d2, d1)]
        forward2 = m2 > 0.0
        flux2 = [b + wg2 * jnp.where(forward2, x, y) for b, x, y in zip(base2, limited2, limited1)]
        done = [x - f for x, f in zip(acc2, flux2)]
        acc1 = [x + f for x, f in zip(acc1, flux2)]
        at = (j + rows - 2) % rows
        put(pt_ref, at, done[0])
        put(ps_ref, at, done[1])
        return here, m, d1, limited1, base1, wg1, m1, acc1, acc

    def pack(carry):
        prev, m1, d2, limited2, base2, wg2, m2, acc2, acc1 = carry
        return [prev[name] for name in NAMES] + [m1, *d2, *limited2, *base2, wg2, m2, *acc2, *acc1]

    def unpack(flat, n):
        prev = dict(zip(NAMES, flat), n=n)
        m1, d2, limited2, base2, wg2, m2, acc2, acc1 = (
            flat[6], flat[7:9], flat[9:11], flat[11:13], flat[13], flat[14], flat[15:17], flat[17:19]
        )
        return prev, m1, d2, limited2, base2, wg2, m2, acc2, acc1

    if first:
        carry = unpack([state_in[i] for i in range(STATE)], n_ref[first - 1 : first, :])
    else:
        carry = unpack([zero] * STATE, jnp.zeros((1, LANES), jnp.int32))

    def block(i, carry):
        for u in range(UNROLL):
            carry = step(first + i * UNROLL + u, carry)
        return carry

    carry = lax.fori_loop(0, (last - first) // UNROLL, block, carry)
    if last < rows:
        for i, value in enumerate(pack(carry)):
            state_out[i] = value
        return
    _, _, _, limited2, base2, wg2, m2, acc2, acc1 = carry
    flux2 = [b + wg2 * jnp.where(m2 > 0.0, x, 0.0) for b, x in zip(base2, limited2)]
    for ref, a2, a1, f in zip((pt_ref, ps_ref), acc2, acc1, flux2):
        put(ref, rows - 2, a2 - f)
        put(ref, rows - 1, a1 + f)


def edge_faces(cells, speeds):
    level = iota(cells[0]["t"].shape, 0).astype(F32)
    wets = [level < jnp.minimum(a["n"], b["n"]) for a, b in zip(cells, cells[1:])]
    d = [[face_step(a, b, w, q) for q in "ts"] for a, b, w in zip(cells, cells[1:], wets)]
    limited = [[minmod(x, y) for x, y in zip(d[i], d[i + 1])] for i in (0, 1)]
    base, wg, forward = face_base(cells[1], cells[2], speeds[1], wets[1], d[1])
    flux = [b + wg * jnp.where(forward, x, y) for b, x, y in zip(base, *limited)]
    first = last = None
    if speeds[0] is not None:
        _, wg0 = weights(speeds[0], wets[0])
        first = [wg0 * jnp.where(speeds[0] > 0.0, 0.0, x) for x in limited[0]]
    if speeds[2] is not None:
        _, wg2 = weights(speeds[2], wets[2])
        last = [wg2 * jnp.where(speeds[2] > 0.0, x, 0.0) for x in limited[1]]
    return first, flux, last


def longitude_kernel(
    levels, rows, lat_size, lon_size, pt_ref, ps_ref, side_ref, near_in, core_in, far_in, t_new, s_new
):
    shape = (levels, LANES)
    lane = iota(shape, 1)
    place = lane % 4
    factors = level_factors(levels)
    K = levels
    is_top = lax.axis_index("lat") == lat_size - 1
    lon_at = lax.axis_index("lon")
    is_odd = lon_at % 2 == 1
    wraps = (lon_at == 0) | (lon_at == lon_size - 1)

    def cell_row(t, s, n):
        return column_row(t, s, n, factors, iota(shape, 0))

    own_t, own_s, own_c = (side_ref[i * K : (i + 1) * K, :] for i in range(3))
    own_n = side_ref[3 * K : 3 * K + 1, :]
    core = core_in[...]
    chip = jnp.where(is_top & ~wraps, near_in[...], far_in[4 * K + 8 :, :])
    west, east = jnp.where(is_odd, core, chip), jnp.where(is_odd, chip, core)
    first_two = place < 2

    def side(t, s, n, speed):
        row = cell_row(t, s, n)
        cells = [row] + [shifted(row, -i) for i in (1, 2, 3)]
        return edge_faces(cells, [roll(speed, -i) for i in range(3)])

    _, west_flux, west_last = side(
        jnp.where(first_two, west[:K], own_t),
        jnp.where(first_two, roll(west[:K], -2), own_s),
        jnp.where(first_two[:1], west[K : K + 1], own_n),
        jnp.where(place == 1, roll(west[K:], -1), own_c),
    )
    east_first, east_flux, _ = side(
        jnp.where(first_two, own_t, east[:K]),
        jnp.where(first_two, own_s, roll(east[:K], 2)),
        jnp.where(first_two[:1], own_n, east[K : K + 1]),
        own_c,
    )
    lon = []
    for fw, lw, fe, le in zip(west_flux, west_last, east_flux, east_first):
        group = jnp.where(
            place == 0,
            -le,
            jnp.where(place == 1, roll(le - fe, 1), jnp.where(place == 2, roll(fw - lw, 2), roll(lw, 3))),
        )
        lon.append(group)

    edge_lanes = (lane >= LANES - 2) | (lane < 2)
    for q, (p_ref, new_ref) in enumerate(((pt_ref, t_new), (ps_ref, s_new))):
        for j in range(rows):
            moved = jnp.where(edge_lanes, roll(lon[q], LANES - 2 - 4 * j), 0.0)
            put(new_ref, j, strided(p_ref, j) + moved)


def latitude_kernel(
    levels, rows, lat_size, lon_size, t_new, s_new, t_ref, s_ref, n_ref, own_ref,
    far_in, below_in, above_in, column_in, relay_in, own_column, t_out, s_out, ends_ref, sems,
):
    shape = (levels, LANES)
    factors = level_factors(levels)
    K = levels
    row_at = lax.axis_index("lat")
    is_top, is_bottom = row_at == lat_size - 1, row_at == 0
    lon_at = lax.axis_index("lon")
    is_odd = lon_at % 2 == 1
    middle = pl.ds(8, rows - 16)
    copies = [
        pltpu.make_async_copy(new_ref.at[:, middle], out_ref.at[:, middle], sems.at[q])
        for q, (new_ref, out_ref) in enumerate(((t_new, t_out), (s_new, s_out)))
    ]
    for copy in copies:
        copy.start()

    def cell_row(t, s, n):
        return column_row(t, s, n, factors, iota(shape, 0))

    counts = n_ref[...].astype(F32)

    def own_row(j):
        return cell_row(strided(t_ref, j), strided(s_ref, j), counts[j : j + 1])

    def sent_row(array, which, at_counts):
        t, s = array[which * K : (which + 1) * K], array[(2 + which) * K : (3 + which) * K]
        return cell_row(t, s, array[at_counts + which : at_counts + which + 1])

    below = jnp.where(is_bottom, 0.0, below_in[...])
    cells = [sent_row(below, 0, 5 * K), sent_row(below, 1, 5 * K), own_row(0), own_row(1)]
    _, south_flux, south_last = edge_faces(cells, [None, below[4 * K : 5 * K], own_ref[:K]])

    pivot = (lon_at * 2) % lon_size == 0
    column = jnp.where(is_odd, relay_in[...], jnp.where(pivot, own_column[: K + 8, :], column_in[: K + 8, :]))
    parts = [roll(column[:K], -i) for i in range(4)] + [column[K : K + 8]]
    fold = far_in[: 4 * K + 8, :]
    fold = jnp.where(iota(fold.shape, 1) == 0, jnp.concatenate(parts, axis=0), fold)
    above = above_in[...]
    above = jnp.where(is_top, fold, jnp.concatenate([above[: 4 * K], above[5 * K :]], axis=0))
    cells = [own_row(rows - 2), own_row(rows - 1), sent_row(above, 0, 4 * K), sent_row(above, 1, 4 * K)]
    north_first, north_flux, _ = edge_faces(cells, [own_ref[K : 2 * K], own_ref[2 * K :], None])

    for q, (new_ref, out_ref) in enumerate(((t_new, t_out), (s_new, s_out))):
        ends = ends_ref.at[q]
        ends[:, :8, :] = new_ref[:, :8, :]
        ends[:, 8:16, :] = new_ref[:, rows - 8 : rows, :]
        extra = {
            0: south_flux[q] - south_last[q],
            1: south_last[q],
            14: -north_first[q],
            15: north_first[q] - north_flux[q],
        }
        for j, value in extra.items():
            put(ends, j, strided(ends, j) + value)
        for i, at in enumerate((0, rows - 8)):
            copy = pltpu.make_async_copy(
                ends.at[:, pl.ds(8 * i, 8)], out_ref.at[:, pl.ds(at, 8)], sems.at[2 + 2 * q + i]
            )
            copy.start()
            copies.append(copy)
    for copy in copies:
        copy.wait()


def body(nlat, nlon, t, s, c, m, n):
    levels, rows, _ = t.shape
    vmem, hbm = pl.BlockSpec(memory_space=pltpu.VMEM), pl.BlockSpec(memory_space=pltpu.HBM)
    f = functools.partial
    out = lambda *shape: jax.ShapeDtypeStruct(shape, F32)
    K = levels
    params = pltpu.CompilerParams(vmem_limit_bytes=VMEM)
    swap = nlat == 2
    field, lat_shape = out(rows, K, LANES), out(5 * K + 8, LANES)
    room = out(levels, rows + SPARE, LANES)
    shapes = [room] * 4 + [jax.ShapeDtypeStruct(n.shape, n.dtype)]
    shapes += [out(3 * K + 8, LANES), out(2 * K, LANES), out(2 * K, LANES), lat_shape, out(6 * K + 8, LANES)]
    shapes += [out(2 * K + 8, LANES), out(3 * K, LANES)]
    shapes += [] if swap else [lat_shape]
    t_v, s_v, c_v, m_v, n_v, side, core, chip, lat, far, column, own, *more = pl.pallas_call(
        f(pack_kernel, levels, rows, nlat),
        out_shape=tuple(shapes),
        in_specs=[hbm] * 5,
        out_specs=(vmem,) * len(shapes),
        scratch_shapes=[pltpu.SemaphoreType.DMA((5,))],
        compiler_params=params,
        name="pack",
    )(*[pltpu.with_memory_space_constraint(x, pltpu.HBM) for x in (t, s, c, m, n)])

    top = nlat - 1

    def exchange(array, top_to, others_to, helper=lambda i: i):
        to = {(j, i): (j, others_to(i)) for j in range(top) for i in range(nlon)}
        for i in range(nlon):
            partner, via = top_to(i), helper(i)
            if partner is not None:
                to[top, i] = (top, partner)
            elif to.get((0, via)) == (0, via ^ 1) and to.get((0, via ^ 1)) == (0, via):
                to[top, i], to[0, via], to[0, via ^ 1] = (0, via), (0, via ^ 1), (top, i)
            else:
                to[top, i] = (top, i)
        pairs = [(i * nlat + j, to[j, i][1] * nlat + to[j, i][0]) for i in range(nlon) for j in range(nlat)]
        return lax.ppermute(array, ("lon", "lat"), pairs)

    def chips(i):
        return (i + (1 if i % 2 else -1)) % nlon

    columns = {i: i ^ 1 if 2 * i % nlon == 0 else nlon - i for i in range(0, nlon, 2)}
    lone = [i for i in range(1, nlon, 2) if columns[i - 1] != i]
    columns |= {i: i - 1 for i in range(1, nlon, 2) if i not in lone}
    for part in ([i for i in lone if 2 * i < nlon], [i for i in lone if 2 * i > nlon]):
        columns |= dict(zip(part, part[1:] + part[:1]))

    middle = HEAD
    fields = (t_v, s_v, c_v, m_v, n_v)
    south_out = (room, room, out(STATE, K, LANES))
    cost = pl.CostEstimate(flops=20_000_000, bytes_accessed=1_000_000, transcendentals=0)
    pt, ps, state, far = pl.pallas_call(
        f(south_kernel, levels, rows, middle, True),
        out_shape=south_out + (out(*far.shape),),
        in_specs=[vmem] * 6,
        out_specs=(vmem,) * 4,
        input_output_aliases={5: 3},
        cost_estimate=cost,
        compiler_params=params,
        name="south_at_origin",
    )(*fields, far)

    ring, rung = range(nlon), range(nlat)
    far_in = exchange(far, lambda i: nlon - 1 - i, chips)
    below_in = above_in = lax.ppermute(lat, "lat", [(i, (i + 1) % nlat) for i in rung])
    if not swap:
        above_in = lax.ppermute(more[0], "lat", [(i, (i - 1) % nlat) for i in rung])
    near_in = exchange(
        chip,
        lambda i: chips(i) if 0 < i < nlon - 1 else None,
        lambda i: i ^ 1,
        lambda i: i + nlon // 4 if i == 0 else i - nlon // 4,
    )
    core_in = lax.ppermute(core, "lon", [(i, i ^ 1) for i in ring])
    column_in = exchange(column, columns.get, lambda i: i ^ 1)

    pt, ps, state = pl.pallas_call(
        f(south_kernel, levels, rows, middle, False),
        out_shape=south_out,
        in_specs=[vmem] * 8,
        out_specs=(vmem,) * 3,
        input_output_aliases={5: 0, 6: 1, 7: 2},
        cost_estimate=cost,
        compiler_params=params,
        name="south_elsewhere",
    )(*fields, pt, ps, state)
    relay = pl.pallas_call(
        relay_kernel,
        out_shape=out(K + 8, LANES),
        in_specs=[vmem] * 2,
        out_specs=vmem,
        compiler_params=params,
        name="relay",
    )(far_in, state)
    relay_in = lax.ppermute(relay, "lon", [(i, i ^ 1) for i in ring])

    pt, ps = pl.pallas_call(
        f(interior_kernel, levels, rows, middle, rows),
        out_shape=(room, room),
        in_specs=[vmem] * 9,
        out_specs=(vmem,) * 2,
        input_output_aliases={5: 0, 6: 1},
        cost_estimate=pl.CostEstimate(flops=20_000_000, bytes_accessed=1_000_000, transcendentals=0),
        compiler_params=params,
        name="interior_north",
    )(*fields, pt, ps, relay, state)

    t_new, s_new = pl.pallas_call(
        f(longitude_kernel, levels, rows, nlat, nlon),
        out_shape=(room, room),
        in_specs=[vmem] * 6,
        out_specs=(vmem,) * 2,
        input_output_aliases={0: 0, 1: 1},
        cost_estimate=pl.CostEstimate(flops=5_000_000, bytes_accessed=1_000_000, transcendentals=0),
        compiler_params=params,
        name="longitude_edges",
    )(pt, ps, side, near_in, core_in, far_in)

    return pl.pallas_call(
        f(latitude_kernel, levels, rows, nlat, nlon),
        out_shape=(out(*t.shape),) * 2,
        in_specs=[vmem] * 12,
        out_specs=(hbm,) * 2,
        scratch_shapes=[pltpu.VMEM((2, K, 24, LANES), F32), pltpu.SemaphoreType.DMA((6,))],
        compiler_params=params,
        name="latitude_edges",
    )(t_new, s_new, t_v, s_v, n_v, own, far_in, below_in, above_in, column_in, relay_in, column)


def solution(mesh):
    spec = P(None, "lat", "lon")
    return jax.shard_map(
        functools.partial(body, mesh.shape["lat"], mesh.shape["lon"]),
        mesh=mesh,
        in_specs=(spec,) * 4 + (P("lat", "lon"),),
        out_specs=(spec,) * 2,
        check_vma=False,
    )
```

```python
import functools

import jax
import jax.numpy as jnp
from jax import lax
from jax.experimental import pallas as pl
from jax.experimental.pallas import tpu as pltpu
from jax.sharding import PartitionSpec as P

heat_swelling_alpha = 0.1655
coef_beta = 0.76554
cabbeling_parameter = 0.05952
lambda_salt = 0.00054914
thermobaric_parameter = 0.0001497
press_salt = 1.109e-05
cross_coupling_contribution = 0.0024341
total_depth = 5000.0
kappa_iso = 0.1
strat_min = 0.1

LANES = 128
VMEM = 8 * 1024 * 1024
UNROLL = 8
HEAD = 24
SPARE = 8
F32 = jnp.float32


def iota(shape, axis):
    return lax.broadcasted_iota(jnp.int32, shape, axis)


def roll(array, shift, axis=1):
    size = array.shape[axis]
    return pltpu.roll(array, shift % size, axis)


def minmod(x, y):
    return jnp.maximum(jnp.minimum(x, jnp.maximum(y, 0.0)), jnp.minimum(y, 0.0))


def level_factors(levels):
    depth = total_depth * (iota((levels, LANES), 0).astype(F32) + 0.5) / levels
    heat = -heat_swelling_alpha * (1.0 + thermobaric_parameter * depth)
    salt = coef_beta * (1.0 - press_salt * depth)
    return heat, salt


def density(t, s, factors):
    heat, salt = factors
    return t * (
        heat
        - (0.5 * heat_swelling_alpha * cabbeling_parameter) * t
        - cross_coupling_contribution * s
    ) + s * (salt - (0.5 * coef_beta * lambda_salt) * s)


def vertical(q, level):
    levels = q.shape[0]
    step = roll(q, -1, 0) - q
    below = roll(step, 1, 0)
    return jnp.where(level == levels - 1, below, step) + jnp.where(level == 0, step, below)


def column_row(t, s, n, factors, level):
    r = density(t, s, factors)
    return {
        "t": t,
        "s": s,
        "r": r,
        "tz": vertical(t, level),
        "sz": vertical(s, level),
        "rz": vertical(r, level),
        "n": n,
    }


def shifted(row, by):
    return {name: roll(value, by) for name, value in row.items()}


def weights(c, wet):
    size = jnp.abs(c)
    return jnp.where(wet, c, 0.0), jnp.where(wet, 0.5 * (size - c * c), 0.0)


def face_step(a, b, wet, name):
    return jnp.where(wet, b[name] - a[name], 0.0)


def face_base(a, b, c, wet, steps):
    wc, wg = weights(c, wet)
    steep = (a["r"] - b["r"]) / jnp.maximum(a["rz"] + b["rz"], 4.0 * strat_min)
    tilt = jnp.where(wet, jnp.clip(steep, -0.25, 0.25), 0.0) * (-kappa_iso)
    forward = c > 0.0
    base = [
        wc * jnp.where(forward, a[q], b[q]) - kappa_iso * d + tilt * (a[q + "z"] + b[q + "z"])
        for q, d in zip("ts", steps)
    ]
    return base, wg, forward


def strided(ref, row):
    levels, rows, _ = ref.shape
    return ref.reshape(levels * rows, LANES)[pl.ds(row, levels, stride=rows), :]


def put(ref, row, value):
    levels, rows, _ = ref.shape
    ref.reshape(levels * rows, LANES)[pl.ds(row, levels, stride=rows), :] = value


def pack_kernel(
    levels, rows, lat_size, t_hbm, s_hbm, c_hbm, m_hbm, n_hbm,
    t_ref, s_ref, c_ref, m_ref, n_ref, side_ref, core_ref, chip_ref, lat_ref, far_ref, column_ref, own_ref, *more,
):
    *more, sems = more
    K = levels
    pairs = ((t_hbm, t_ref), (s_hbm, s_ref), (n_hbm, n_ref), (c_hbm, c_ref), (m_hbm, m_ref))
    pairs = [(src, dst if dst is n_ref else dst.at[:, :rows]) for src, dst in pairs]
    copies = [pltpu.make_async_copy(src, dst, sems.at[i]) for i, (src, dst) in enumerate(pairs)]
    for copy in copies:
        copy.start()
    lane = iota((levels, LANES), 1)
    group = lane // 4

    group = lane // 4

    def gather(ref):
        out = jnp.zeros((levels, LANES), F32)
        for j in range(rows):
            out = jnp.where(group == j, roll(strided(ref, j), 4 * j + 2), out)
        return out

    def mirrored(x):
        index = (LANES - iota(x.shape, 1)) % LANES
        return jnp.take_along_axis(x, index, axis=1)

    def tracer_rows(out_ref, tracer, ref, picks, change=lambda x: x):
        for i, j in enumerate(picks):
            at = (2 * tracer + i) * K
            out_ref[at : at + K, :] = change(strided(ref, j))

    south, north, fold = (0, 1), (rows - 2, rows - 1), (rows - 2, rows - 3)
    is_top = lax.axis_index("lat") == lat_size - 1
    is_odd = lax.axis_index("lon") % 2 == 1
    place = iota((levels, LANES), 1) % 4
    sides = []
    for tracer, ref in enumerate((t_ref, s_ref)):
        copies[tracer].wait()
        sides.append(gather(ref))
        tracer_rows(far_ref, tracer, ref, fold, mirrored)
        if more:
            tracer_rows(lat_ref, tracer, ref, north)
            tracer_rows(more[0], tracer, ref, south)
        else:
            for i in range(2):
                at = (2 * tracer + i) * K
                lat_ref[at : at + K, :] = jnp.where(is_top, strided(ref, south[i]), strided(ref, north[i]))

    copies[3].wait()
    sides.append(gather(c_ref))
    copies[2].wait()
    counts = n_ref[...].astype(F32)
    line = jnp.zeros((8, LANES), F32)
    for at in range(0, rows, 8):
        moved = pltpu.roll(counts[at : at + 8], 4 * at + 2, 1, stride=4, stride_axis=0)
        mine = iota((8, LANES), 1) // 4 == iota((8, LANES), 0) + at
        line = jnp.where(mine, moved, line)
    line = jnp.sum(line, axis=0, keepdims=True)
    heat, salt, speed = sides
    line = jnp.broadcast_to(line, (levels, LANES))
    for i, value in enumerate((heat, salt, speed)):
        side_ref[i * K : (i + 1) * K, :] = value
    side_ref[3 * K :, :] = line[:8]
    to_east = jnp.where(place < 2, heat, roll(salt, 2)), jnp.where(place == 2, roll(speed, 1), line)
    to_west = jnp.where(place < 2, roll(salt, -2), heat), line
    for i, (e, w) in enumerate(zip(to_east, to_west)):
        core_ref[i * K : (i + 1) * K, :] = jnp.where(is_odd, w, e)
        chip = jnp.where(is_odd, e, w)
        chip_ref[i * K : (i + 1) * K, :] = chip
        far_ref[4 * K + 8 + i * K : 4 * K + 8 + (i + 1) * K, :] = chip

    def tally(picks):
        return jnp.concatenate(
            [counts[j : j + 1] for j in picks] + [jnp.zeros((8 - len(picks), LANES), F32)], axis=0
        )

    far_ref[4 * K : 4 * K + 8, :] = mirrored(tally(fold))
    first = jnp.zeros((levels, LANES), F32)
    for i, (ref, j) in enumerate((ref, j) for ref in (t_ref, s_ref) for j in fold):
        first = jnp.where(lane == i, roll(strided(ref, j), i), first)
    column_ref[:K, :] = first
    column_ref[K : K + 8, :] = tally(fold)
    if more:
        lat_ref[5 * K :, :] = tally(north)
        more[0][4 * K : 5 * K, :] = jnp.zeros((K, LANES), F32)
        more[0][5 * K :, :] = tally(south)
    else:
        lat_ref[5 * K :, :] = jnp.where(is_top, tally(south), tally(north))
    copies[4].wait()
    lat_ref[4 * K : 5 * K, :] = strided(m_ref, rows - 1)
    for i, j in enumerate((0, rows - 2, rows - 1)):
        own_ref[i * K : (i + 1) * K, :] = strided(m_ref, j)


def relay_kernel(far_ref, _, out_ref):
    K = out_ref.shape[0] - 8
    lane = iota((K, LANES), 1)
    out = far_ref[:K, :]
    for i in (1, 2, 3):
        out = jnp.where(lane == i, roll(far_ref[i * K : (i + 1) * K, :], i), out)
    out_ref[:K, :] = out
    out_ref[K:, :] = far_ref[4 * K : 4 * K + 8, :]


NAMES = ("t", "s", "r", "tz", "sz", "rz")
STATE = 19


def south_kernel(levels, rows, last, early, lon_size, t_ref, s_ref, c_ref, m_ref, n_ref, *more):
    *more, pt_ref, ps_ref, state_out = more[:-1] if early else more
    lon_at = lax.axis_index("lon")
    at_origin = (lax.axis_index("lat") == 0) & ((lon_at < 2) | (lon_at == lon_size // 4 + 1))

    @pl.when(at_origin if early else jnp.logical_not(at_origin))
    def _():
        interior_kernel(levels, rows, 0, last, t_ref, s_ref, c_ref, m_ref, n_ref, pt_ref, ps_ref, state_out)


def interior_kernel(levels, rows, first, last, t_ref, s_ref, c_ref, m_ref, n_ref, *more):
    if first:
        _, _, _, state_in, pt_ref, ps_ref = more
    else:
        pt_ref, ps_ref, state_out = more
    shape = (levels, LANES)
    level = iota(shape, 0)
    last_lane = iota((1, LANES), 1) == LANES - 1
    factors = level_factors(levels)
    zero = jnp.zeros(shape, F32)

    def step(j, carry):
        prev, m1, d2, limited2, base2, wg2, m2, acc2, acc1 = carry
        t, s, c, m = (strided(ref, j) for ref in (t_ref, s_ref, c_ref, m_ref))
        n = n_ref[pl.ds(j, 1), :]
        here = column_row(t, s, n, factors, level)
        east = shifted(here, -1)
        wet = level < jnp.minimum(n, jnp.where(last_lane, 0, east["n"]))
        steps = [face_step(here, east, wet, q) for q in "ts"]
        base, wg, forward = face_base(here, east, c, wet, steps)
        inside = level < n
        acc = []
        for q, d, flux in zip("ts", steps, base):
            limited = minmod(roll(d, 1), d)
            flux = flux + wg * jnp.where(forward, limited, roll(limited, -1))
            acc.append(jnp.where(inside, here[q], 0.0) + roll(flux, 1) - flux)
        wet = level < jnp.minimum(prev["n"], n)
        d1 = [face_step(prev, here, wet, q) for q in "ts"]
        base1, wg1, _ = face_base(prev, here, m1, wet, d1)
        limited1 = [minmod(x, y) for x, y in zip(d2, d1)]
        forward2 = m2 > 0.0
        flux2 = [b + wg2 * jnp.where(forward2, x, y) for b, x, y in zip(base2, limited2, limited1)]
        done = [x - f for x, f in zip(acc2, flux2)]
        acc1 = [x + f for x, f in zip(acc1, flux2)]
        at = (j + rows - 2) % rows
        put(pt_ref, at, done[0])
        put(ps_ref, at, done[1])
        return here, m, d1, limited1, base1, wg1, m1, acc1, acc

    def pack(carry):
        prev, m1, d2, limited2, base2, wg2, m2, acc2, acc1 = carry
        return [prev[name] for name in NAMES] + [m1, *d2, *limited2, *base2, wg2, m2, *acc2, *acc1]

    def unpack(flat, n):
        prev = dict(zip(NAMES, flat), n=n)
        m1, d2, limited2, base2, wg2, m2, acc2, acc1 = (
            flat[6], flat[7:9], flat[9:11], flat[11:13], flat[13], flat[14], flat[15:17], flat[17:19]
        )
        return prev, m1, d2, limited2, base2, wg2, m2, acc2, acc1

    if first:
        carry = unpack([state_in[i] for i in range(STATE)], n_ref[first - 1 : first, :])
    else:
        carry = unpack([zero] * STATE, jnp.zeros((1, LANES), jnp.int32))

    def block(i, carry):
        for u in range(UNROLL):
            carry = step(first + i * UNROLL + u, carry)
        return carry

    carry = lax.fori_loop(0, (last - first) // UNROLL, block, carry)
    if last < rows:
        for i, value in enumerate(pack(carry)):
            state_out[i] = value
        return
    _, _, _, limited2, base2, wg2, m2, acc2, acc1 = carry
    flux2 = [b + wg2 * jnp.where(m2 > 0.0, x, 0.0) for b, x in zip(base2, limited2)]
    for ref, a2, a1, f in zip((pt_ref, ps_ref), acc2, acc1, flux2):
        put(ref, rows - 2, a2 - f)
        put(ref, rows - 1, a1 + f)


def edge_faces(cells, speeds):
    level = iota(cells[0]["t"].shape, 0).astype(F32)
    wets = [level < jnp.minimum(a["n"], b["n"]) for a, b in zip(cells, cells[1:])]
    d = [[face_step(a, b, w, q) for q in "ts"] for a, b, w in zip(cells, cells[1:], wets)]
    limited = [[minmod(x, y) for x, y in zip(d[i], d[i + 1])] for i in (0, 1)]
    base, wg, forward = face_base(cells[1], cells[2], speeds[1], wets[1], d[1])
    flux = [b + wg * jnp.where(forward, x, y) for b, x, y in zip(base, *limited)]
    first = last = None
    if speeds[0] is not None:
        _, wg0 = weights(speeds[0], wets[0])
        first = [wg0 * jnp.where(speeds[0] > 0.0, 0.0, x) for x in limited[0]]
    if speeds[2] is not None:
        _, wg2 = weights(speeds[2], wets[2])
        last = [wg2 * jnp.where(speeds[2] > 0.0, x, 0.0) for x in limited[1]]
    return first, flux, last


def longitude_kernel(
    levels, rows, lat_size, lon_size, pt_ref, ps_ref, side_ref, near_in, core_in, far_in, t_new, s_new
):
    shape = (levels, LANES)
    lane = iota(shape, 1)
    place = lane % 4
    factors = level_factors(levels)
    K = levels
    is_top = lax.axis_index("lat") == lat_size - 1
    lon_at = lax.axis_index("lon")
    is_odd = lon_at % 2 == 1
    wraps = (lon_at == 0) | (lon_at == lon_size - 1)

    def cell_row(t, s, n):
        return column_row(t, s, n, factors, iota(shape, 0))

    own_t, own_s, own_c = (side_ref[i * K : (i + 1) * K, :] for i in range(3))
    own_n = side_ref[3 * K : 3 * K + 1, :]
    core = core_in[...]
    chip = jnp.where(is_top & ~wraps, near_in[...], far_in[4 * K + 8 :, :])
    west, east = jnp.where(is_odd, core, chip), jnp.where(is_odd, chip, core)
    first_two = place < 2

    def side(t, s, n, speed):
        row = cell_row(t, s, n)
        cells = [row] + [shifted(row, -i) for i in (1, 2, 3)]
        return edge_faces(cells, [roll(speed, -i) for i in range(3)])

    _, west_flux, west_last = side(
        jnp.where(first_two, west[:K], own_t),
        jnp.where(first_two, roll(west[:K], -2), own_s),
        jnp.where(first_two[:1], west[K : K + 1], own_n),
        jnp.where(place == 1, roll(west[K:], -1), own_c),
    )
    east_first, east_flux, _ = side(
        jnp.where(first_two, own_t, east[:K]),
        jnp.where(first_two, own_s, roll(east[:K], 2)),
        jnp.where(first_two[:1], own_n, east[K : K + 1]),
        own_c,
    )
    lon = []
    for fw, lw, fe, le in zip(west_flux, west_last, east_flux, east_first):
        group = jnp.where(
            place == 0,
            -le,
            jnp.where(place == 1, roll(le - fe, 1), jnp.where(place == 2, roll(fw - lw, 2), roll(lw, 3))),
        )
        lon.append(group)

    edge_lanes = (lane >= LANES - 2) | (lane < 2)
    for q, (p_ref, new_ref) in enumerate(((pt_ref, t_new), (ps_ref, s_new))):
        for j in range(rows):
            moved = jnp.where(edge_lanes, roll(lon[q], LANES - 2 - 4 * j), 0.0)
            put(new_ref, j, strided(p_ref, j) + moved)


def latitude_kernel(
    levels, rows, lat_size, lon_size, t_new, s_new, t_ref, s_ref, n_ref, own_ref,
    far_in, below_in, above_in, column_in, relay_in, own_column, t_out, s_out, ends_ref, sems,
):
    shape = (levels, LANES)
    factors = level_factors(levels)
    K = levels
    row_at = lax.axis_index("lat")
    is_top, is_bottom = row_at == lat_size - 1, row_at == 0
    lon_at = lax.axis_index("lon")
    is_odd = lon_at % 2 == 1
    middle = pl.ds(8, rows - 16)
    copies = [
        pltpu.make_async_copy(new_ref.at[:, middle], out_ref.at[:, middle], sems.at[q])
        for q, (new_ref, out_ref) in enumerate(((t_new, t_out), (s_new, s_out)))
    ]
    for copy in copies:
        copy.start()

    def cell_row(t, s, n):
        return column_row(t, s, n, factors, iota(shape, 0))

    counts = n_ref[...].astype(F32)

    def own_row(j):
        return cell_row(strided(t_ref, j), strided(s_ref, j), counts[j : j + 1])

    def sent_row(array, which, at_counts):
        t, s = array[which * K : (which + 1) * K], array[(2 + which) * K : (3 + which) * K]
        return cell_row(t, s, array[at_counts + which : at_counts + which + 1])

    below = jnp.where(is_bottom, 0.0, below_in[...])
    cells = [sent_row(below, 0, 5 * K), sent_row(below, 1, 5 * K), own_row(0), own_row(1)]
    _, south_flux, south_last = edge_faces(cells, [None, below[4 * K : 5 * K], own_ref[:K]])

    pivot = (lon_at * 2) % lon_size == 0
    column = jnp.where(is_odd, relay_in[...], jnp.where(pivot, own_column[: K + 8, :], column_in[: K + 8, :]))
    parts = [roll(column[:K], -i) for i in range(4)] + [column[K : K + 8]]
    fold = far_in[: 4 * K + 8, :]
    fold = jnp.where(iota(fold.shape, 1) == 0, jnp.concatenate(parts, axis=0), fold)
    above = above_in[...]
    above = jnp.where(is_top, fold, jnp.concatenate([above[: 4 * K], above[5 * K :]], axis=0))
    cells = [own_row(rows - 2), own_row(rows - 1), sent_row(above, 0, 4 * K), sent_row(above, 1, 4 * K)]
    north_first, north_flux, _ = edge_faces(cells, [own_ref[K : 2 * K], own_ref[2 * K :], None])

    for q, (new_ref, out_ref) in enumerate(((t_new, t_out), (s_new, s_out))):
        ends = ends_ref.at[q]
        ends[:, :8, :] = new_ref[:, :8, :]
        ends[:, 8:16, :] = new_ref[:, rows - 8 : rows, :]
        extra = {
            0: south_flux[q] - south_last[q],
            1: south_last[q],
            14: -north_first[q],
            15: north_first[q] - north_flux[q],
        }
        for j, value in extra.items():
            put(ends, j, strided(ends, j) + value)
        for i, at in enumerate((0, rows - 8)):
            copy = pltpu.make_async_copy(
                ends.at[:, pl.ds(8 * i, 8)], out_ref.at[:, pl.ds(at, 8)], sems.at[2 + 2 * q + i]
            )
            copy.start()
            copies.append(copy)
    for copy in copies:
        copy.wait()


def body(nlat, nlon, t, s, c, m, n):
    levels, rows, _ = t.shape
    vmem, hbm = pl.BlockSpec(memory_space=pltpu.VMEM), pl.BlockSpec(memory_space=pltpu.HBM)
    f = functools.partial
    out = lambda *shape: jax.ShapeDtypeStruct(shape, F32)
    K = levels
    params = pltpu.CompilerParams(vmem_limit_bytes=VMEM)
    swap = nlat == 2
    field, lat_shape = out(rows, K, LANES), out(5 * K + 8, LANES)
    room = out(levels, rows + SPARE, LANES)
    shapes = [room] * 4 + [jax.ShapeDtypeStruct(n.shape, n.dtype)]
    shapes += [out(3 * K + 8, LANES), out(2 * K, LANES), out(2 * K, LANES), lat_shape, out(6 * K + 8, LANES)]
    shapes += [out(2 * K + 8, LANES), out(3 * K, LANES)]
    shapes += [] if swap else [lat_shape]
    t_v, s_v, c_v, m_v, n_v, side, core, chip, lat, far, column, own, *more = pl.pallas_call(
        f(pack_kernel, levels, rows, nlat),
        out_shape=tuple(shapes),
        in_specs=[hbm] * 5,
        out_specs=(vmem,) * len(shapes),
        scratch_shapes=[pltpu.SemaphoreType.DMA((5,))],
        compiler_params=params,
        name="pack",
    )(*[pltpu.with_memory_space_constraint(x, pltpu.HBM) for x in (t, s, c, m, n)])

    top = nlat - 1

    def exchange(array, top_to, others_to, helper=lambda i: i):
        to = {(j, i): (j, others_to(i)) for j in range(top) for i in range(nlon)}
        for i in range(nlon):
            partner, via = top_to(i), helper(i)
            if partner is not None:
                to[top, i] = (top, partner)
            elif to.get((0, via)) == (0, via ^ 1) and to.get((0, via ^ 1)) == (0, via):
                to[top, i], to[0, via], to[0, via ^ 1] = (0, via), (0, via ^ 1), (top, i)
            else:
                to[top, i] = (top, i)
        pairs = [(i * nlat + j, to[j, i][1] * nlat + to[j, i][0]) for i in range(nlon) for j in range(nlat)]
        return lax.ppermute(array, ("lon", "lat"), pairs)

    def chips(i):
        return (i + (1 if i % 2 else -1)) % nlon

    columns = {i: i ^ 1 if 2 * i % nlon == 0 else nlon - i for i in range(0, nlon, 2)}
    lone = [i for i in range(1, nlon, 2) if columns[i - 1] != i]
    columns |= {i: i - 1 for i in range(1, nlon, 2) if i not in lone}
    for part in ([i for i in lone if 2 * i < nlon], [i for i in lone if 2 * i > nlon]):
        columns |= dict(zip(part, part[1:] + part[:1]))

    middle = HEAD
    fields = (t_v, s_v, c_v, m_v, n_v)
    south_out = (room, room, out(STATE, K, LANES))
    cost = pl.CostEstimate(flops=20_000_000, bytes_accessed=1_000_000, transcendentals=0)
    pt, ps, state, far = pl.pallas_call(
        f(south_kernel, levels, rows, middle, True, nlon),
        out_shape=south_out + (out(*far.shape),),
        in_specs=[vmem] * 6,
        out_specs=(vmem,) * 4,
        input_output_aliases={5: 3},
        cost_estimate=cost,
        compiler_params=params,
        name="south_at_origin",
    )(*fields, far)

    ring, rung = range(nlon), range(nlat)
    far_in = exchange(far, lambda i: nlon - 1 - i, chips)
    below_in = above_in = lax.ppermute(lat, "lat", [(i, (i + 1) % nlat) for i in rung])
    if not swap:
        above_in = lax.ppermute(more[0], "lat", [(i, (i - 1) % nlat) for i in rung])
    near_in = exchange(
        chip,
        lambda i: chips(i) if 0 < i < nlon - 1 else None,
        lambda i: i ^ 1,
        lambda i: i + nlon // 4 if i == 0 else i - nlon // 4,
    )
    core_in = lax.ppermute(core, "lon", [(i, i ^ 1) for i in ring])
    column_in = exchange(column, columns.get, lambda i: i ^ 1)

    pt, ps, state = pl.pallas_call(
        f(south_kernel, levels, rows, middle, False, nlon),
        out_shape=south_out,
        in_specs=[vmem] * 8,
        out_specs=(vmem,) * 3,
        input_output_aliases={5: 0, 6: 1, 7: 2},
        cost_estimate=cost,
        compiler_params=params,
        name="south_elsewhere",
    )(*fields, pt, ps, state)
    relay = pl.pallas_call(
        relay_kernel,
        out_shape=out(K + 8, LANES),
        in_specs=[vmem] * 2,
        out_specs=vmem,
        compiler_params=params,
        name="relay",
    )(far_in, state)
    relay_in = lax.ppermute(relay, "lon", [(i, i ^ 1) for i in ring])

    pt, ps = pl.pallas_call(
        f(interior_kernel, levels, rows, middle, rows),
        out_shape=(room, room),
        in_specs=[vmem] * 9,
        out_specs=(vmem,) * 2,
        input_output_aliases={5: 0, 6: 1},
        cost_estimate=pl.CostEstimate(flops=20_000_000, bytes_accessed=1_000_000, transcendentals=0),
        compiler_params=params,
        name="interior_north",
    )(*fields, pt, ps, relay, state)

    t_new, s_new = pl.pallas_call(
        f(longitude_kernel, levels, rows, nlat, nlon),
        out_shape=(room, room),
        in_specs=[vmem] * 6,
        out_specs=(vmem,) * 2,
        input_output_aliases={0: 0, 1: 1},
        cost_estimate=pl.CostEstimate(flops=5_000_000, bytes_accessed=1_000_000, transcendentals=0),
        compiler_params=params,
        name="longitude_edges",
    )(pt, ps, side, near_in, core_in, far_in)

    return pl.pallas_call(
        f(latitude_kernel, levels, rows, nlat, nlon),
        out_shape=(out(*t.shape),) * 2,
        in_specs=[vmem] * 12,
        out_specs=(hbm,) * 2,
        scratch_shapes=[pltpu.VMEM((2, K, 24, LANES), F32), pltpu.SemaphoreType.DMA((6,))],
        compiler_params=params,
        name="latitude_edges",
    )(t_new, s_new, t_v, s_v, n_v, own, far_in, below_in, above_in, column_in, relay_in, column)


def solution(mesh):
    spec = P(None, "lat", "lon")
    return jax.shard_map(
        functools.partial(body, mesh.shape["lat"], mesh.shape["lon"]),
        mesh=mesh,
        in_specs=(spec,) * 4 + (P("lat", "lon"),),
        out_specs=(spec,) * 2,
        check_vma=False,
    )
```
